32 devices in a mesh: section: 2 (over x), tensor: 2 (over y), dp: 8 (over z, core).
Axes of the slice: x: 2, y: 2, z: 4, core: 2. Of those that a mesh axis runs over, the one named last changes fastest.
Arguments:
- inputs: bfloat16 [2, 8, 128, 768], P(None, 'dp'), may hold values from -6 to 6
- cotangent: bfloat16 [2, 8, 128, 768], P(None, 'dp'), may hold values from -6 to 6
- ln1_gain: bfloat16 [2, 768], P('section'), may hold values from 0.25 to 1.75
- ln1_bias: bfloat16 [2, 768], P('section'), may hold values from -4 to 4
- ln2_gain: bfloat16 [2, 768], P('section'), may hold values from 0.25 to 1.75
- ln2_bias: bfloat16 [2, 768], P('section'), may hold values from -4 to 4
- w_qkv: bfloat16 [2, 768, 3, 768], P('section', None, None, 'tensor'), may hold values from -0.21875 to 0.21875
- b_qkv: bfloat16 [2, 3, 768], P('section', None, 'tensor'), may hold values from -4 to 4
- w_out: bfloat16 [2, 768, 768], P('section', 'tensor'), may hold values from -1.25 to 1.25
- b_out: bfloat16 [2, 768], P('section'), may hold values from -4 to 4
- w_up: bfloat16 [2, 768, 3072], P('section', None, 'tensor'), may hold values from -0.21875 to 0.21875
- b_up: bfloat16 [2, 3072], P('section', 'tensor'), may hold values from -4 to 4
- w_down: bfloat16 [2, 3072, 768], P('section', 'tensor'), may hold values from -0.15625 to 0.15625
- b_down: bfloat16 [2, 768], P('section'), may hold values from -4 to 4
Outputs:
- section_out: bfloat16 [2, 2, 8, 128, 768], P('section', None, 'dp')
- input_grad: float32 [2, 2, 8, 128, 768], P('section', None, 'dp')
- grad_ln1_gain: float32 [2, 768], P('section', ('tensor', 'dp'))
- grad_ln1_bias: float32 [2, 768], P('section', ('tensor', 'dp'))
- grad_ln2_gain: float32 [2, 768], P('section', ('tensor', 'dp'))
- grad_ln2_bias: float32 [2, 768], P('section', ('tensor', 'dp'))
- grad_w_qkv: float32 [2, 768, 3, 768], P('section', 'dp', None, 'tensor')
- grad_b_qkv: float32 [2, 3, 768], P('section', None, ('tensor', 'dp'))
- grad_w_out: float32 [2, 768, 768], P('section', ('tensor', 'dp'))
- grad_b_out: float32 [2, 768], P('section', ('tensor', 'dp'))
- grad_w_up: float32 [2, 768, 3072], P('section', 'dp', 'tensor')
- grad_b_up: float32 [2, 3072], P('section', ('tensor', 'dp'))
- grad_w_down: float32 [2, 3072, 768], P('section', ('tensor', 'dp'))
- grad_b_down: float32 [2, 768], P('section', ('tensor', 'dp'))
The draws below stay inside these ranges and needn't reach their ends.
All inputs are finite; a program needn't handle non-finite values.
Results may differ from the reference program's by a relative error of at most 0.019.
Values may be sent and summed in bfloat16 or wider, within the bound.
No kernel may reach another device: no remote copies, remote signals or barrier semaphores. Data moves between devices by JAX's collectives and lax.ppermute only.
A program may use at most 128 MiB of HBM per device.

```python
import math
import jax
import jax.numpy as jnp
from jax import lax

D = 768
HEADS = 12
HEAD = 64
ROT = 16
FF = 3072
SEQ = 128
MICRO = 2
SECTIONS = 2
BATCH = 8


def raised(array, key, source, target, parts, factor):
    def block_of(axis_at):
        return (jnp.arange(array.shape[axis_at]) // (array.shape[axis_at] // parts)).reshape((-1,) + (1,) * (array.ndim - 1 - axis_at))

    one_side = jax.random.permutation(key, parts)[block_of(target)]
    second = (block_of(target) + parts // 2) % parts
    return jnp.where((block_of(source) == one_side) | (block_of(source) == second), factor * array, array)


def shard_levels(key, shape, cuts, least, high):
    factor_of = 1.0
    for dim, blocks in cuts:
        steps = jax.random.uniform(jax.random.fold_in(jax.random.fold_in(key, 6), dim), (blocks,), jnp.float32, least / len(cuts), high / len(cuts))
        factor_of = factor_of * jnp.repeat(jnp.exp(steps), shape[dim] // blocks).reshape((-1,) + (1,) * (len(shape) - 1 - dim))
    return factor_of


def normal_values(own_key, shape, deviation, most, pieces=(), kind=jnp.bfloat16):
    array = deviation * jax.random.normal(own_key, shape, jnp.float32)
    if pieces:
        array = array * shard_levels(own_key, shape, pieces, -0.22, 0.18)
    return jnp.clip(array, -most, most).astype(kind)


def noise_with(rng, extent, width, bound, cuts, heavy, kind=jnp.bfloat16):
    values = width * jax.random.normal(rng, extent, jnp.float32)
    if cuts:
        values = values * shard_levels(rng, extent, cuts, -0.22, 0.18)
    return jnp.clip(raised(values, jax.random.fold_in(rng, 3), *heavy), -bound, bound).astype(kind)


def setup_inputs(seed: int = 0) -> dict:
    arg_keys = jax.random.split(jax.random.key(seed), 15)
    inputs = normal_values(arg_keys[0], (MICRO, BATCH, SEQ, D), 1.0, 6.0, ((1, 8),))
    cotangent = noise_with(arg_keys[1], (MICRO, BATCH, SEQ, D), 1.0, 6.0, ((1, 8),), (1, 3, 8, 2.0))
    ln1_gain = jnp.clip(1.0 + 0.15 * jax.random.normal(arg_keys[2], (SECTIONS, D), jnp.float32), 0.25, 1.75).astype(jnp.bfloat16)
    ln1_bias = normal_values(arg_keys[3], (SECTIONS, D), 0.3, 4.0, ((0, 2),))
    ln2_gain = jnp.clip(1.0 + 0.15 * jax.random.normal(arg_keys[4], (SECTIONS, D), jnp.float32), 0.25, 1.75).astype(jnp.bfloat16)
    ln2_bias = normal_values(arg_keys[5], (SECTIONS, D), 0.3, 4.0, ((0, 2),))
    w_qkv = normal_values(arg_keys[6], (SECTIONS, D, 3, D), D ** -0.5, 0.21875, ((0, 2), (3, 2)))
    b_qkv = normal_values(arg_keys[7], (SECTIONS, 3, D), 0.5, 4.0, ((0, 2), (2, 2)))
    w_out = normal_values(arg_keys[8], (SECTIONS, D, D), (D // 32) ** -0.5, 1.25, ((0, 2), (1, 2)))
    b_out = normal_values(arg_keys[9], (SECTIONS, D), 0.5, 4.0, ((0, 2),))
    w_up = normal_values(arg_keys[10], (SECTIONS, D, FF), D ** -0.5, 0.21875, ((0, 2), (2, 2)))
    b_up = normal_values(arg_keys[11], (SECTIONS, FF), 0.5, 4.0, ((0, 2), (1, 2)))
    w_down = normal_values(arg_keys[12], (SECTIONS, FF, D), (FF // 2) ** -0.5, 0.15625, ((0, 2), (1, 2)))
    b_down = normal_values(arg_keys[13], (SECTIONS, D), 0.5, 4.0, ((0, 2),))
    return dict(inputs=inputs, cotangent=cotangent, ln1_gain=ln1_gain, ln1_bias=ln1_bias, ln2_gain=ln2_gain, ln2_bias=ln2_bias, w_qkv=w_qkv, b_qkv=b_qkv, w_out=w_out, b_out=b_out, w_up=w_up, b_up=b_up, w_down=w_down, b_down=b_down)


@jax.custom_vjp
def low(v):
    return lax.optimization_barrier(v.astype(jnp.bfloat16)).astype(jnp.float32)

@jax.custom_vjp
def low_back(v):
    return v

def low_keep(v):
    return (low(v), None)

def low_pass(kept, grad):
    return (grad,)

def back_keep(v):
    return (v, None)

def back_low(kept, grad):
    return (low(grad),)
low.defvjp(low_keep, low_pass)
low_back.defvjp(back_keep, back_low)
EPSILON = 1e-05
HIGH = lax.Precision.HIGHEST

def rope_tables():
    half = ROT // 2
    inverse = jnp.exp(-math.log(10000.0) * jnp.arange(half, dtype=jnp.float32) * 2.0 / ROT)
    angle = jnp.arange(SEQ, dtype=jnp.float32)[:, None] * inverse[None, :]
    angle = jnp.concatenate([angle, angle], axis=1)
    return (jnp.cos(angle), jnp.sin(angle))

def rotate(tensor, cosine, sine):
    half = ROT // 2
    front = tensor[..., :ROT]
    turned = jnp.concatenate([-front[..., half:], front[..., :half]], axis=-1)
    moved = front * cosine[:, None, :] + turned * sine[:, None, :]
    return jnp.concatenate([moved, tensor[..., ROT:]], axis=-1)

def layer_norm(value, gain, shift):
    center = value - lax.optimization_barrier(jnp.mean(value, axis=-1, keepdims=True))
    spread = lax.optimization_barrier(jnp.mean(center * center, axis=-1, keepdims=True))
    return center * lax.rsqrt(spread + EPSILON) * gain + shift

def layer(block, params):
    gain_one, bias_one, gain_two, bias_two, wqkv, bqkv, wout, bout, wup, bup, wdown, bdown = params
    groups = block.shape[0]
    cosine, sine = rope_tables()
    first = low(layer_norm(block, gain_one, bias_one))
    second = low(layer_norm(block, gain_two, bias_two))
    packed = low_back(jnp.einsum('gsd,dch->gsch', first, wqkv, precision=HIGH) + bqkv)
    split = packed.reshape(groups, SEQ, 3, HEADS, HEAD)
    query = low(rotate(split[:, :, 0], cosine, sine))
    keys = low(rotate(split[:, :, 1], cosine, sine))
    values = low(split[:, :, 2])
    scores = low_back(jnp.einsum('gqhe,gkhe->ghqk', query, keys, precision=HIGH) * HEAD ** (-0.5))
    causal = jnp.arange(SEQ)[:, None] >= jnp.arange(SEQ)[None, :]
    weights = jax.nn.softmax(jnp.where(causal, scores, -1e+30), axis=-1)
    mixed = low(low_back(jnp.einsum('ghqk,gkhe->gqhe', low(weights), values, precision=HIGH)))
    mixed = mixed.reshape(groups, SEQ, D)
    attended = jnp.einsum('gsc,cd->gsd', mixed, wout, precision=HIGH) + bout
    hidden = low_back(jnp.einsum('gsd,df->gsf', second, wup, precision=HIGH) + bup)
    active = low(jax.nn.gelu(hidden, approximate=False))
    fed = jnp.einsum('gsf,fd->gsd', active, wdown, precision=HIGH) + bdown
    return block + attended + fed

def reference(inputs, cotangent, ln1_gain, ln1_bias, ln2_gain, ln2_bias, w_qkv, b_qkv, w_out, b_out, w_up, b_up, w_down, b_down):
    weights_all = tuple((a.astype(jnp.float32) for a in (ln1_gain, ln1_bias, ln2_gain, ln2_bias, w_qkv, b_qkv, w_out, b_out, w_up, b_up, w_down, b_down)))
    count = MICRO * BATCH
    group = math.gcd(count, 2 ** (max(1, 4096 // SEQ).bit_length() - 1))
    blocks = inputs.reshape(count // group, group, SEQ, D)
    backs = cotangent.reshape(count // group, group, SEQ, D)
    zeros = tuple((jnp.zeros_like(a) for a in weights_all))

    def step(carry, pair):
        block, back = pair
        current = block.astype(jnp.float32)
        outputs = []
        pullbacks = []
        for section in range(SECTIONS):
            layer_params = tuple((a[section] for a in weights_all))
            result, pull = jax.vjp(layer, current, layer_params)
            pullbacks.append(pull)
            outputs.append(result.astype(jnp.bfloat16))
            current = low(result)
        flow = back.astype(jnp.float32)
        input_grads = [None] * SECTIONS
        param_grads = [None] * SECTIONS
        for section in reversed(range(SECTIONS)):
            d_input, d_params = pullbacks[section](flow)
            input_grads[section] = d_input
            param_grads[section] = d_params
            flow = low(d_input)
        total = tuple((c + jnp.stack([param_grads[s][i] for s in range(SECTIONS)]) for i, c in enumerate(carry)))
        return (total, (jnp.stack(outputs), jnp.stack(input_grads)))
    sums, (acts, grads) = lax.scan(step, zeros, (blocks, backs))
    section_out = jnp.moveaxis(acts, 1, 0).reshape(SECTIONS, MICRO, BATCH, SEQ, D)
    input_grad = jnp.moveaxis(grads, 1, 0).reshape(SECTIONS, MICRO, BATCH, SEQ, D)
    return (section_out, input_grad, sums[0], sums[1], sums[2], sums[3], sums[4], sums[5], sums[6], sums[7], sums[8], sums[9], sums[10], sums[11])
```

```python
import functools
import math

import jax
import jax.numpy as jnp
import numpy as np
from jax import lax
from jax.experimental import pallas as pl
from jax.experimental.pallas import tpu as pltpu
from jax.sharding import PartitionSpec as P

HEAD = 64
ROT = 16
LANES = 128
EPSILON = 1e-05
BF = jnp.bfloat16
F32 = jnp.float32
VMEM_LIMIT = 48 * 2**20


def rope_tables(length):
    half = ROT // 2
    inverse = np.exp(-math.log(10000.0) * np.arange(half, dtype=np.float32) * np.float32(2.0) / ROT)
    angle = np.arange(length, dtype=np.float32)[:, None] * inverse[None, :].astype(np.float32)
    cosine, sine = np.cos(angle), np.sin(angle)
    table = np.zeros((3, length, LANES), np.float32)
    table[0] = 1.0
    for head in range(LANES // HEAD):
        at = head * HEAD
        table[0, :, at : at + half] = cosine
        table[0, :, at + half : at + ROT] = cosine
        table[1, :, at : at + half] = -sine
        table[2, :, at + half : at + ROT] = sine
    return table


def dot(a, b):
    return jnp.dot(a, b, preferred_element_type=F32)


def dot_nt(a, b):
    return lax.dot_general(a, b, (((1,), (1,)), ((), ())), preferred_element_type=F32)


def dot_tn(a, b):
    return lax.dot_general(a, b, (((0,), (0,)), ((), ())), preferred_element_type=F32)


def roped(value, table, sign):
    half = ROT // 2
    ahead = pltpu.roll(value, LANES - half, 1) * table[1]
    behind = pltpu.roll(value, half, 1) * table[2]
    return value * table[0] + sign * (ahead + behind)


def head_pair(value):
    low = lax.broadcasted_iota(jnp.int32, value.shape, 1) < HEAD
    zero = jnp.zeros_like(value)
    return jnp.concatenate([jnp.where(low, value, zero), jnp.where(low, zero, value)], axis=0)


def pair_merge(value):
    rows = value.shape[0] // 2
    low = lax.broadcasted_iota(jnp.int32, (rows, LANES), 1) < HEAD
    return jnp.where(low, value[:rows], value[rows:])


def normal(block):
    width = block.shape[1]
    center = block - jnp.sum(block, axis=1, keepdims=True) * (1.0 / width)
    spread = jnp.sum(center * center, axis=1, keepdims=True) * (1.0 / width)
    scale = lax.rsqrt(spread + EPSILON)
    return center * scale, scale


def forward_part(x, vec, table, w, wait, put):
    rows, width = x.shape
    unit, unused = normal(x.astype(F32))
    first = (unit * vec["g1"] + vec["b1"]).astype(BF)
    second = (unit * vec["g2"] + vec["b2"]).astype(BF)
    put("a1", first)
    put("a2", second)
    wait("wqkv")
    bqkv = vec["bqkv"]
    raw = [dot(first, w["wqkv"][j]) + bqkv[j : j + 1] for j in range(3)]
    local = raw[0].shape[1]
    row = lax.broadcasted_iota(jnp.int32, (rows, rows), 0)
    keep = row >= lax.broadcasted_iota(jnp.int32, (rows, rows), 1)
    for p in range(local // LANES):
        sl = slice(p * LANES, (p + 1) * LANES)
        q = roped(raw[0][:, sl], table, 1.0).astype(BF)
        k = roped(raw[1][:, sl], table, 1.0).astype(BF)
        v = raw[2][:, sl].astype(BF)
        put("q", q, sl)
        put("k", k, sl)
        put("v", v, sl)
        scores = dot_nt(q, head_pair(k)) * HEAD**-0.5
        prob = []
        for h in range(2):
            part = jnp.where(keep, scores[:, h * rows : (h + 1) * rows], -1e30)
            expo = jnp.exp(part - jnp.max(part, axis=1, keepdims=True))
            prob.append(expo * (1.0 / jnp.sum(expo, axis=1, keepdims=True)))
        prob = jnp.concatenate(prob, axis=1)
        put("prob", prob, slice(p * 2 * rows, (p + 1) * 2 * rows))
        put("mixed", dot(prob.astype(BF), head_pair(v)).astype(BF), sl)
    wait("wup")
    hidden = w["wup"].shape[1]
    step = 256
    for c in range(0, hidden, step):
        sl = slice(c, c + step)
        u = dot(second, w["wup"][:, sl]) + vec["bup"][:, sl]
        phi = 0.5 + 0.5 * lax.erf(u * (2.0**-0.5))
        put("g", (u * phi).astype(BF), sl)
        put("gp", lambda: phi + u * (jnp.exp(-0.5 * u * u) * (2.0 * math.pi) ** -0.5), sl)


def output_part(mixed, active, vec, w, wait, owner):
    wait("wout")
    total = dot(mixed[...], w["wout"][...])
    wait("wdown")
    total = total + dot(active[...], w["wdown"][...])
    extra = vec["bout"] + vec["bdown"]
    return (total + jnp.where(owner == 0, extra, jnp.zeros_like(extra))).astype(BF)


def backward_part(x, dy, saved, vec, table, w, wait, put):
    rows, width = x.shape
    hidden = w["wdown"].shape[0]
    step = 256
    wait("wdown")
    for c in range(0, hidden, step):
        sl = slice(c, c + step)
        du = (dot_nt(dy, w["wdown"][sl, :]) * saved["gp"][:, sl].astype(F32)).astype(BF)
        put("du", du, sl)
    wait("wout")
    d_mixed = dot_nt(dy, w["wout"][...]).astype(BF)
    local = d_mixed.shape[1]
    for p in range(local // LANES):
        sl = slice(p * LANES, (p + 1) * LANES)
        q, k, v = saved["q"][:, sl], saved["k"][:, sl], saved["v"][:, sl]
        prob = saved["prob"][:, p * 2 * rows : (p + 1) * 2 * rows]
        d_tile = d_mixed[:, sl]
        d_prob = dot_nt(d_tile, head_pair(v))
        d_value = pair_merge(dot_tn(prob.astype(BF), d_tile))
        d_scores = []
        for h in range(2):
            part = prob[:, h * rows : (h + 1) * rows]
            d_part = d_prob[:, h * rows : (h + 1) * rows]
            both = part * d_part
            d_scores.append(both - part * jnp.sum(both, axis=1, keepdims=True))
        d_scores = jnp.concatenate(d_scores, axis=1).astype(BF)
        scale = HEAD**-0.5
        d_query = dot(d_scores, head_pair(k)) * scale
        d_keys = pair_merge(dot_tn(d_scores, q)) * scale
        put("dqkv", roped(d_query, table, -1.0).astype(BF), slice(p * LANES, (p + 1) * LANES))
        at = local + p * LANES
        put("dqkv", roped(d_keys, table, -1.0).astype(BF), slice(at, at + LANES))
        at = 2 * local + p * LANES
        put("dqkv", d_value.astype(BF), slice(at, at + LANES))
    return local


def norm_back(x, du, dqkv, local, vec, w, wait):
    wait("wup")
    d_second = dot_nt(du[...], w["wup"][...])
    wait("wqkv")
    d_first = dot_nt(dqkv[:, :local], w["wqkv"][0])
    for j in range(1, 3):
        d_first = d_first + dot_nt(dqkv[:, j * local : (j + 1) * local], w["wqkv"][j])
    unit, scale = normal(x.astype(F32))
    e = d_first * vec["g1"] + d_second * vec["g2"]
    width = x.shape[1]
    mean = jnp.sum(e, axis=1, keepdims=True) * (1.0 / width)
    along = jnp.sum(e * unit, axis=1, keepdims=True) * (1.0 / width)
    dx = (e - mean - unit * along) * scale
    return dx.astype(BF), d_first, d_second, unit


WEIGHTS = ("wqkv", "wout", "wup", "wdown")
VECTORS = ("g1", "b1", "g2", "b2", "bqkv", "bout", "bup", "bdown")


def start_weights(hbm, scratch, sems):
    waited = set()
    copies = {}
    order = {name: i for i, name in enumerate(WEIGHTS)}
    for name in hbm:
        copies[name] = pltpu.make_async_copy(hbm[name], scratch[name], sems.at[order[name]])

    def start(names):
        for name in names:
            copies[name].start()

    def wait(name):
        if name not in waited:
            waited.add(name)
            copies[name].wait()

    return start, wait


def f_kernel(*refs):
    x_ref, owner_ref, table_ref = refs[:3]
    vec = {n: r[...].astype(F32) for n, r in zip(VECTORS, refs[3:11])}
    hbm = dict(zip(WEIGHTS, refs[11:15]))
    out_ref = refs[15]
    w = dict(zip(WEIGHTS, refs[16:20]))
    mixed, active, sems = refs[20:]
    start, wait = start_weights(hbm, w, sems)
    start(("wqkv", "wup", "wout", "wdown"))

    def put(name, value, sl=slice(None)):
        if name == "mixed":
            mixed[:, sl] = value
        if name == "g":
            active[:, sl] = value

    forward_part(x_ref[...], vec, table_ref, w, wait, put)
    out_ref[...] = output_part(mixed, active, vec, w, wait, owner_ref[0])


SAVED = ("a1", "a2", "q", "k", "v", "prob", "mixed", "g", "gp")


def fb_kernel(*refs):
    x_ref, dy_ref, owner_ref, table_ref = refs[:4]
    vec = {n: r[...].astype(F32) for n, r in zip(VECTORS, refs[4:12])}
    hbm = dict(zip(WEIGHTS, refs[12:16]))
    out_ref, dx_ref = refs[16:18]
    saved = dict(zip(SAVED, refs[18:27]))
    w = dict(zip(WEIGHTS, refs[27:31]))
    du, dqkv, sems = refs[31:]
    start, wait = start_weights(hbm, w, sems)
    start(("wqkv", "wup", "wdown", "wout"))
    saved_too = dict(saved, du=du, dqkv=dqkv)

    def put(name, value, sl=slice(None)):
        ref = saved_too[name]
        value = value() if callable(value) else value
        ref[:, sl] = value.astype(ref.dtype)

    x = x_ref[...]
    forward_part(x, vec, table_ref, w, wait, put)
    local = backward_part(x, dy_ref[...], saved, vec, table_ref, w, wait, put)
    dx_ref[...] = norm_back(x, du, dqkv, local, vec, w, wait)[0]
    out_ref[...] = output_part(saved["mixed"], saved["g"], vec, w, wait, owner_ref[0])


def b_kernel(*refs):
    x_ref, dy_ref, table_ref = refs[:3]
    vec = {n: r[...].astype(F32) for n, r in zip(("g1", "g2"), refs[3:5])}
    hbm = dict(zip(WEIGHTS, refs[5:9]))
    saved = dict(zip(("q", "k", "v", "prob", "gp"), refs[9:14]))
    dx_ref, du, dqkv, sum_d, sum_up, sum_qkv = refs[14:20]
    w = dict(zip(WEIGHTS, refs[20:24]))
    sems = refs[24]
    start, wait = start_weights(hbm, w, sems)
    start(("wdown", "wout", "wup", "wqkv"))
    kept = {"du": du, "dqkv": dqkv}

    def put(name, value, sl=slice(None)):
        kept[name][:, sl] = value

    x = x_ref[...]
    dy = dy_ref[...]
    local = backward_part(x, dy, saved, vec, table_ref, w, wait, put)
    dx, d_first, d_second, unit = norm_back(x, du, dqkv, local, vec, w, wait)
    dx_ref[...] = dx

    def total(value):
        return jnp.sum(value, axis=0, keepdims=True)

    sum_d[0:1] = total(d_first * unit)
    sum_d[1:2] = total(d_first)
    sum_d[2:3] = total(d_second * unit)
    sum_d[3:4] = total(d_second)
    sum_d[4:5] = total(dy.astype(F32)) * 0.5
    sum_up[...] = total(du[...].astype(F32))
    sum_qkv[...] = total(dqkv[...].astype(F32))


VM = pl.BlockSpec(memory_space=pltpu.VMEM)
SM = pl.BlockSpec(memory_space=pltpu.SMEM)
ANY = pl.BlockSpec(memory_space=pl.ANY)


def weight_scratch(ws):
    return [pltpu.VMEM(a.shape, a.dtype) for a in ws]


def cost(ws, rows, passes):
    size = sum(math.prod(a.shape) for a in ws)
    return pl.CostEstimate(flops=2 * size * rows * passes, bytes_accessed=2 * size, transcendentals=0)


def call_f(x, owner, table, vecs, ws):
    rows, width = x.shape
    local, hidden = ws[1].shape[0], ws[3].shape[0]
    return pl.pallas_call(
        f_kernel,
        out_shape=jax.ShapeDtypeStruct((rows, width), BF),
        in_specs=[VM, SM, VM] + [VM] * 8 + [ANY] * 4,
        out_specs=VM,
        scratch_shapes=weight_scratch(ws)
        + [pltpu.VMEM((rows, local), BF), pltpu.VMEM((rows, hidden), BF), pltpu.SemaphoreType.DMA((4,))],
        compiler_params=pltpu.CompilerParams(vmem_limit_bytes=VMEM_LIMIT),
        cost_estimate=cost(ws, rows, 1),
    )(x, owner, table, *vecs, *ws)


def call_fb(x, dy, owner, table, vecs, ws):
    rows, width = x.shape
    local, hidden = ws[1].shape[0], ws[3].shape[0]
    shape = jax.ShapeDtypeStruct
    outs = [
        shape((rows, width), BF),
        shape((rows, width), BF),
        shape((rows, width), BF),
        shape((rows, width), BF),
        shape((rows, local), BF),
        shape((rows, local), BF),
        shape((rows, local), BF),
        shape((rows, 2 * rows * local // LANES), F32),
        shape((rows, local), BF),
        shape((rows, hidden), BF),
        shape((rows, hidden), F32),
    ]
    return pl.pallas_call(
        fb_kernel,
        out_shape=outs,
        in_specs=[VM, VM, SM, VM] + [VM] * 8 + [ANY] * 4,
        out_specs=[VM] * len(outs),
        scratch_shapes=weight_scratch(ws)
        + [pltpu.VMEM((rows, hidden), BF), pltpu.VMEM((rows, 3 * local), BF), pltpu.SemaphoreType.DMA((4,))],
        compiler_params=pltpu.CompilerParams(vmem_limit_bytes=VMEM_LIMIT),
        cost_estimate=cost(ws, rows, 2),
    )(x, dy, owner, table, *vecs, *ws)


def call_b(x, dy, table, gains, ws, saved):
    rows, width = x.shape
    local, hidden = ws[1].shape[0], ws[3].shape[0]
    shape = jax.ShapeDtypeStruct
    outs = [
        shape((rows, width), BF),
        shape((rows, hidden), BF),
        shape((rows, 3 * local), BF),
        shape((5, width), F32),
        shape((1, hidden), F32),
        shape((1, 3 * local), F32),
    ]
    return pl.pallas_call(
        b_kernel,
        out_shape=outs,
        in_specs=[VM] * 3 + [VM] * 2 + [ANY] * 4 + [VM] * 5,
        out_specs=[VM] * len(outs),
        scratch_shapes=weight_scratch(ws) + [pltpu.SemaphoreType.DMA((4,))],
        compiler_params=pltpu.CompilerParams(vmem_limit_bytes=VMEM_LIMIT),
        cost_estimate=cost(ws, rows, 1),
    )(x, dy, table, *gains, *ws, *saved)


def swap(value):
    return lax.ppermute(value, "tensor", [(0, 1), (1, 0)])


def per_device(inputs, cotangent, g1, b1, g2, b2, w_qkv, b_qkv, w_out, b_out, w_up, b_up, w_down, b_down):
    section = lax.axis_index("section")
    owner_at = lax.axis_index("tensor")
    dp_at = lax.axis_index("dp")
    parts = lax.axis_size("dp")
    tensors = lax.axis_size("tensor")
    micro, seqs, length, width = inputs.shape
    rows = seqs * length
    local, hidden = w_out.shape[1], w_up.shape[2]
    owner = owner_at.astype(jnp.int32).reshape(1)
    table = jnp.asarray(rope_tables(length))
    vecs = (g1, b1, g2, b2, b_qkv[0], b_out, b_up, b_down)
    ws = (w_qkv[0].transpose(1, 0, 2), w_out[0], w_up[0], w_down[0])
    xs = inputs.reshape(micro, rows, width)
    cots = cotangent.reshape(micro, rows, width)

    sources = []
    for m in range(micro):
        part = call_f(xs[m], owner, table, vecs, ws)
        other = swap(part)
        whole = (xs[m].astype(F32) + (part.astype(F32) + other.astype(F32))).astype(BF)
        arrived = lax.ppermute(whole, "section", [(0, 1)])
        sources.append(jnp.where(section == 0, xs[m], arrived))
    kept, ups, produced = [], [], []
    for m in range(micro):
        part, dx, *saved = call_fb(sources[m], cots[m], owner, table, vecs, ws)
        other = swap(dx)
        whole = (cots[m].astype(F32) + (dx.astype(F32) + other.astype(F32))).astype(BF)
        arrived = lax.ppermute(whole, "section", [(1, 0)])
        ups.append(jnp.where(section == 1, cots[m], arrived))
        kept.append(dict(zip(SAVED, saved)))
        produced.append(part)
    grads, dus, dqkvs, sums = [], [], [], []
    for m in range(micro):
        saved = [kept[m][n] for n in ("q", "k", "v", "prob", "gp")]
        dx, du, dqkv, sum_d, sum_up, sum_qkv = call_b(sources[m], ups[m], table, (g1, g2), ws, saved)
        grads.append(dx)
        dus.append(du)
        dqkvs.append(dqkv)
        sums.append((sum_d, sum_up, sum_qkv))
    input_grad = []
    section_out = []
    for m in range(micro):
        dx, part = grads[m], produced[m]
        input_grad.append(ups[m].astype(F32) + (dx.astype(F32) + swap(dx).astype(F32)))
        whole = sources[m].astype(F32) + (part.astype(F32) + swap(part).astype(F32))
        section_out.append(whole.astype(BF))
    input_grad = jnp.stack(input_grad).reshape(1, micro, seqs, length, width)
    section_out = jnp.stack(section_out).reshape(1, micro, seqs, length, width)

    def rowed(pieces):
        return jnp.concatenate(pieces, axis=0)

    all_up = rowed(ups)
    all_du, all_dqkv = rowed(dus), rowed(dqkvs)
    a1, a2, mixed, active = (rowed([kept[m][n] for m in range(micro)]) for n in ("a1", "a2", "mixed", "g"))

    def outer(a, b):
        return jnp.einsum("ta,tb->ab", a, b, preferred_element_type=F32).astype(BF)

    def scatter(value):
        return lax.psum_scatter(value, "dp", scatter_dimension=0, tiled=True).astype(F32)

    d_wdown = scatter(outer(active, all_up))
    d_wout = scatter(outer(mixed, all_up))
    d_wup = scatter(outer(a2, all_du))
    d_wqkv = scatter(outer(a1, all_dqkv)).reshape(-1, 3, local)
    sum_d = sum(s[0] for s in sums)
    sum_up = sum(s[1] for s in sums)
    sum_qkv = sum(s[2] for s in sums).reshape(3, local)
    mine = jnp.concatenate([sum_up.reshape(-1), sum_qkv.reshape(-1)])
    flat = jnp.zeros((tensors, mine.shape[0]), F32)
    flat = lax.dynamic_update_slice(flat, mine[None], (owner_at, 0)).reshape(-1)
    total = lax.psum(jnp.concatenate([sum_d.reshape(-1), flat]), ("tensor", "dp"))
    total_d = total[: 5 * width].reshape(5, width)
    mine = lax.dynamic_slice_in_dim(total[5 * width :].reshape(tensors, -1), owner_at, 1, 0).reshape(-1)
    share = width // (tensors * parts)
    d_vec = lax.dynamic_slice_in_dim(total_d, (owner_at * parts + dp_at) * share, share, 1)
    up_share, qkv_share = hidden // parts, local // parts
    d_bup = lax.dynamic_slice_in_dim(mine[:hidden], dp_at * up_share, up_share, 0)
    d_bqkv = lax.dynamic_slice_in_dim(mine[hidden:].reshape(3, local), dp_at * qkv_share, qkv_share, 1)
    return (
        section_out,
        input_grad,
        d_vec[0:1],
        d_vec[1:2],
        d_vec[2:3],
        d_vec[3:4],
        d_wqkv[None],
        d_bqkv[None],
        d_wout[None],
        d_vec[4:5],
        d_wup[None],
        d_bup[None],
        d_wdown[None],
        d_vec[4:5],
    )


def solution(mesh):
    return jax.shard_map(
        per_device,
        mesh=mesh,
        in_specs=(
            P(None, "dp", None, None),
            P(None, "dp", None, None),
            P("section", None),
            P("section", None),
            P("section", None),
            P("section", None),
            P("section", None, None, "tensor"),
            P("section", None, "tensor"),
            P("section", "tensor", None),
            P("section", None),
            P("section", None, "tensor"),
            P("section", "tensor"),
            P("section", "tensor", None),
            P("section", None),
        ),
        out_specs=(
            P("section", None, "dp", None, None),
            P("section", None, "dp", None, None),
            P("section", ("tensor", "dp")),
            P("section", ("tensor", "dp")),
            P("section", ("tensor", "dp")),
            P("section", ("tensor", "dp")),
            P("section", "dp", None, "tensor"),
            P("section", None, ("tensor", "dp")),
            P("section", ("tensor", "dp"), None),
            P("section", ("tensor", "dp")),
            P("section", "dp", "tensor"),
            P("section", ("tensor", "dp")),
            P("section", ("tensor", "dp"), None),
            P("section", ("tensor", "dp")),
        ),
        check_vma=False,
    )
```

```python
import functools
import math

import jax
import jax.numpy as jnp
import numpy as np
from jax import lax
from jax.experimental import pallas as pl
from jax.experimental.pallas import tpu as pltpu
from jax.sharding import PartitionSpec as P

HEAD = 64
ROT = 16
LANES = 128
PIECE = 512
EPSILON = 1e-05
BF = jnp.bfloat16
F32 = jnp.float32


def rope_tables(length):
    half = ROT // 2
    inverse = np.exp(-math.log(10000.0) * np.arange(half, dtype=np.float32) * np.float32(2.0) / ROT)
    angle = np.arange(length, dtype=np.float32)[:, None] * inverse[None, :].astype(np.float32)
    cosine, sine = np.cos(angle), np.sin(angle)
    table = np.zeros((3, length, LANES), np.float32)
    table[0] = 1.0
    for head in range(LANES // HEAD):
        at = head * HEAD
        table[0, :, at : at + half] = cosine
        table[0, :, at + half : at + ROT] = cosine
        table[1, :, at : at + half] = -sine
        table[2, :, at + half : at + ROT] = sine
    return table


def dot(a, b):
    return jnp.dot(a, b, preferred_element_type=F32)


def dot_nt(a, b):
    return lax.dot_general(a, b, (((1,), (1,)), ((), ())), preferred_element_type=F32)


def dot_tn(a, b):
    return lax.dot_general(a, b, (((0,), (0,)), ((), ())), preferred_element_type=F32)


def roped(value, table, sign):
    half = ROT // 2
    ahead = pltpu.roll(value, LANES - half, 1) * table[1]
    behind = pltpu.roll(value, half, 1) * table[2]
    return value * table[0] + sign * (ahead + behind)


def head_pair(value):
    low = lax.broadcasted_iota(jnp.int32, value.shape, 1) < HEAD
    zero = jnp.zeros_like(value)
    return jnp.concatenate([jnp.where(low, value, zero), jnp.where(low, zero, value)], axis=0)


def pair_merge(value):
    rows = value.shape[0] // 2
    low = lax.broadcasted_iota(jnp.int32, (rows, LANES), 1) < HEAD
    return jnp.where(low, value[:rows], value[rows:])


def normal(block):
    width = block.shape[1]
    center = block - jnp.sum(block, axis=1, keepdims=True) * (1.0 / width)
    spread = jnp.sum(center * center, axis=1, keepdims=True) * (1.0 / width)
    scale = lax.rsqrt(spread + EPSILON)
    return center * scale, scale


def forward_part(x, vec, table, w, wait, put):
    rows, width = x.shape
    unit, unused = normal(x.astype(F32))
    first = (unit * vec["g1"] + vec["b1"]).astype(BF)
    second = (unit * vec["g2"] + vec["b2"]).astype(BF)
    put("a1", first)
    put("a2", second)
    bqkv = vec["bqkv"]
    raw = []
    for j in range(3):
        wait("wqkv", j)
        raw.append(dot(first, w["wqkv"][j]) + bqkv[j : j + 1])
    local = raw[0].shape[1]
    row = lax.broadcasted_iota(jnp.int32, (rows, rows), 0)
    keep = row >= lax.broadcasted_iota(jnp.int32, (rows, rows), 1)
    for p in range(local // LANES):
        sl = slice(p * LANES, (p + 1) * LANES)
        q = roped(raw[0][:, sl], table, 1.0).astype(BF)
        k = roped(raw[1][:, sl], table, 1.0).astype(BF)
        v = raw[2][:, sl].astype(BF)
        put("q", q, sl)
        put("k", k, sl)
        put("v", v, sl)
        scores = dot_nt(q, head_pair(k)) * HEAD**-0.5
        prob = []
        for h in range(2):
            part = jnp.where(keep, scores[:, h * rows : (h + 1) * rows], -1e30)
            expo = jnp.exp(part - jnp.max(part, axis=1, keepdims=True))
            prob.append(expo * (1.0 / jnp.sum(expo, axis=1, keepdims=True)))
        prob = jnp.concatenate(prob, axis=1)
        put("prob", prob, slice(p * 2 * rows, (p + 1) * 2 * rows))
        put("mixed", dot(prob.astype(BF), head_pair(v)).astype(BF), sl)
    hidden = w["wup"].shape[1]
    step = 256
    for c in range(0, hidden, step):
        sl = slice(c, c + step)
        wait("wup", c // PIECE)
        u = dot(second, w["wup"][:, sl]) + vec["bup"][:, sl]
        phi = 0.5 + 0.5 * lax.erf(u * (2.0**-0.5))
        put("g", (u * phi).astype(BF), sl)
        put("gp", lambda: phi + u * (jnp.exp(-0.5 * u * u) * (2.0 * math.pi) ** -0.5), sl)


def output_part(mixed, active, vec, w, wait):
    wait("wout")
    total = dot(mixed[...], w["wout"][...])
    wait("wdown")
    total = total + dot(active[...], w["wdown"][...])
    return (total + vec["extra"]).astype(BF)


def backward_part(dy, saved, table, w, wait, put):
    rows = dy.shape[0]
    hidden = w["wdown"].shape[0]
    step = 256
    for c in range(0, hidden, step):
        sl = slice(c, c + step)
        wait("wdown", c // PIECE)
        du = (dot_nt(dy, w["wdown"][sl, :]) * saved["gp"][:, sl].astype(F32)).astype(BF)
        put("du", du, sl)
    wait("wout")
    d_mixed = dot_nt(dy, w["wout"][...]).astype(BF)
    local = d_mixed.shape[1]
    for p in range(local // LANES):
        sl = slice(p * LANES, (p + 1) * LANES)
        q, k, v = saved["q"][:, sl], saved["k"][:, sl], saved["v"][:, sl]
        prob = saved["prob"][:, p * 2 * rows : (p + 1) * 2 * rows]
        d_tile = d_mixed[:, sl]
        d_prob = dot_nt(d_tile, head_pair(v))
        d_value = pair_merge(dot_tn(prob.astype(BF), d_tile))
        d_scores = []
        for h in range(2):
            part = prob[:, h * rows : (h + 1) * rows]
            d_part = d_prob[:, h * rows : (h + 1) * rows]
            both = part * d_part
            d_scores.append(both - part * jnp.sum(both, axis=1, keepdims=True))
        d_scores = jnp.concatenate(d_scores, axis=1).astype(BF)
        scale = HEAD**-0.5
        d_query = dot(d_scores, head_pair(k)) * scale
        d_keys = pair_merge(dot_tn(d_scores, q)) * scale
        put("dqkv", roped(d_query, table, -1.0).astype(BF), slice(p * LANES, (p + 1) * LANES))
        at = local + p * LANES
        put("dqkv", roped(d_keys, table, -1.0).astype(BF), slice(at, at + LANES))
        at = 2 * local + p * LANES
        put("dqkv", d_value.astype(BF), slice(at, at + LANES))


def norm_back(x, du, dqkv, local, vec, w, wait):
    wait("wup")
    d_second = dot_nt(du[...], w["wup"][...])
    for j in range(3):
        wait("wqkv", j)
    d_first = dot_nt(dqkv[:, :local], w["wqkv"][0])
    for j in range(1, 3):
        d_first = d_first + dot_nt(dqkv[:, j * local : (j + 1) * local], w["wqkv"][j])
    unit, scale = normal(x.astype(F32))
    e = d_first * vec["g1"] + d_second * vec["g2"]
    width = x.shape[1]
    mean = jnp.sum(e, axis=1, keepdims=True) * (1.0 / width)
    along = jnp.sum(e * unit, axis=1, keepdims=True) * (1.0 / width)
    dx = (e - mean - unit * along) * scale
    return dx.astype(BF), d_first, d_second, unit


WEIGHTS = ("wqkv", "wout", "wup", "wdown")
VECTORS = ("g1", "b1", "g2", "b2", "bqkv", "bout", "bup", "bdown")
SAVED = ("a1", "a2", "q", "k", "v", "prob", "mixed", "g", "gp")


class Loads:
    def __init__(self, sems):
        self.sems, self.copies, self.count = sems, {}, 0

    def start(self, name, source, target):
        copy = pltpu.make_async_copy(source, target, self.sems.at[self.count])
        self.count += 1
        self.copies.setdefault(name, {})[len(self.copies.get(name, {}))] = copy
        copy.start()

    def weight(self, name, hbm, w):
        source, target = hbm[name], w[name]
        if name == "wqkv":
            for j in range(3):
                self.start(name, source.at[j], target.at[j])
        elif name == "wout":
            self.start(name, source, target)
        else:
            for c in range(0, source.shape[0 if name == "wdown" else 1], PIECE):
                at = (pl.ds(c, PIECE), slice(None)) if name == "wdown" else (slice(None), pl.ds(c, PIECE))
                self.start(name, source.at[at], target.at[at])

    def wait(self, name, index=None):
        left = self.copies[name]
        for piece in [index] if index is not None else list(left):
            copy = left.pop(piece, None)
            if copy is not None:
                copy.wait()


def unpacked(pack, width, local, hidden):
    return {
        "g1": pack[0:1, :width],
        "b1": pack[1:2, :width],
        "g2": pack[2:3, :width],
        "b2": pack[3:4, :width],
        "extra": pack[4:5, :width],
        "bup": pack[5:6, :hidden],
        "bqkv": pack[6:9, :local],
    }


def f_kernel(at, first, *refs):
    flag_ref, x_hbm, table_ref = refs[:3]
    refs = refs[3:]
    hbm = dict(zip(WEIGHTS, refs[:4]))
    refs = refs[4:]
    if first:
        vec_hbm = dict(zip(VECTORS, refs[:8]))
        refs = refs[8:]
        out_ref, pack_ref = refs[:2]
        refs = refs[2:]
    else:
        pack_ref, out_ref = refs[:2]
        refs = refs[2:]
    w = dict(zip(WEIGHTS, refs[:4]))
    mixed, active, x_ref, sems = refs[4:8]
    loads = Loads(sems)
    loads.start("x", x_hbm.at[at], x_ref)
    if first:
        vec_ref = dict(zip(VECTORS, refs[8:]))
        for name in VECTORS:
            loads.start(name, vec_hbm[name], vec_ref[name])
    for name in ("wqkv", "wup", "wout", "wdown"):
        loads.weight(name, hbm, w)
    width, (local, hidden) = x_ref.shape[1], (mixed.shape[1], active.shape[1])
    if first:
        for name in VECTORS:
            loads.wait(name)
        for i, name in enumerate(("g1", "b1", "g2", "b2")):
            pack_ref[i : i + 1, :width] = vec_ref[name][...].astype(F32)
        extra = vec_ref["bout"][...].astype(F32) + vec_ref["bdown"][...].astype(F32)
        pack_ref[4:5, :width] = jnp.where(flag_ref[1] == 0, extra, jnp.zeros_like(extra))
        pack_ref[5:6, :hidden] = vec_ref["bup"][...].astype(F32)
        pack_ref[6:9, :local] = vec_ref["bqkv"][...].astype(F32)
    vec = unpacked(pack_ref, width, local, hidden)

    def put(name, value, sl=slice(None)):
        if name == "mixed":
            mixed[:, sl] = value
        if name == "g":
            active[:, sl] = value

    loads.wait("x")
    forward_part(x_ref[...], vec, table_ref, w, loads.wait, put)
    out_ref[...] = output_part(mixed, active, vec, w, loads.wait)


def fb_kernel(at, *refs):
    flag_ref, x_hbm, dy_hbm, arrived_ref, table_ref, pack_ref = refs[:6]
    hbm = dict(zip(WEIGHTS, refs[6:10]))
    names = ("dx", "source") + SAVED
    outs = dict(zip(names, refs[10 : 10 + len(names)]))
    refs = refs[10 + len(names) :]
    held = dict(zip(names, refs[: len(names)]))
    refs = refs[len(names) :]
    w = dict(zip(WEIGHTS, refs[:4]))
    du, dqkv, x_ref, dy_ref, sems, out_sems = refs[4:]
    loads, stores = Loads(sems), Loads(out_sems)
    loads.start("x", x_hbm.at[at], x_ref)
    loads.weight("wqkv", hbm, w)
    loads.weight("wup", hbm, w)
    loads.start("dy", dy_hbm.at[at], dy_ref)
    loads.weight("wdown", hbm, w)
    loads.weight("wout", hbm, w)
    held_too = dict(held, du=du, dqkv=dqkv)

    def put(name, value, sl=slice(None)):
        ref = held_too[name]
        value = value() if callable(value) else value
        ref[:, sl] = value.astype(ref.dtype)

    width, (local, hidden) = x_ref.shape[1], (dqkv.shape[1] // 3, du.shape[1])
    vec = unpacked(pack_ref, width, local, hidden)
    loads.wait("x")
    x = jnp.where(flag_ref[0] == 0, x_ref[...], arrived_ref[...])
    held["source"][...] = x
    forward_part(x, vec, table_ref, w, loads.wait, put)
    for name in ("source",) + SAVED:
        stores.start(name, held[name], outs[name])
    loads.wait("dy")
    backward_part(dy_ref[...], held, table_ref, w, loads.wait, put)
    held["dx"][...] = norm_back(x, du, dqkv, local, vec, w, loads.wait)[0]
    stores.start("dx", held["dx"], outs["dx"])
    for name in names:
        stores.wait(name)


def b_kernel(at, first, last, *refs):
    flag_ref, x_ref, dy_hbm, arrived_ref, table_ref, pack_ref = refs[:6]
    hbm = dict(zip(WEIGHTS, refs[6:10]))
    saved = dict(zip(("q", "k", "v", "prob", "gp"), refs[10:15]))
    refs = refs[15:]
    if last:
        refs = refs[2:]
    if not first:
        own_before, other_before = refs[:2]
        refs = refs[2:]
    dx_ref, du, dqkv, own, other, dy_out = refs[:6]
    w = dict(zip(WEIGHTS, refs[6:10]))
    dy_ref, sems = refs[10:]
    loads = Loads(sems)
    loads.start("dy", dy_hbm.at[at], dy_ref)
    for name in ("wdown", "wout", "wup", "wqkv"):
        loads.weight(name, hbm, w)
    kept = {"du": du, "dqkv": dqkv}

    def put(name, value, sl=slice(None)):
        kept[name][:, sl] = value

    x = x_ref[...]
    loads.wait("dy")
    dy = jnp.where(flag_ref[0] == 0, arrived_ref[...], dy_ref[...])
    dy_out[...] = dy
    width, (local, hidden) = x.shape[1], (dqkv.shape[1] // 3, du.shape[1])
    vec = unpacked(pack_ref, width, local, hidden)
    backward_part(dy, saved, table_ref, w, loads.wait, put)
    dx, d_first, d_second, unit = norm_back(x, du, dqkv, local, vec, w, loads.wait)
    dx_ref[...] = dx
    if first:
        own[...] = jnp.zeros_like(own)
        other[...] = jnp.zeros_like(other)
    else:
        own[...] = own_before[...]
        other[...] = other_before[...]
    low = flag_ref[1] == 0
    terms = (d_first * unit, d_first, d_second * unit, d_second, dy.astype(F32))
    for i, term in enumerate(terms):
        total = jnp.sum(term, axis=0, keepdims=True)
        front, back = total[:, :local], total[:, local:]
        own[i : i + 1] += jnp.where(low, front, back)
        if i < 4:
            other[i : i + 1] += jnp.where(low, back, front)
    line = 5
    for ref in (dqkv, du):
        for c in range(0, ref.shape[1], local):
            own[line : line + 1] += jnp.sum(ref[:, c : c + local].astype(F32), axis=0, keepdims=True)
            line += 1


def deal(theirs, mine, place, at, core, value, share):
    for z in range(value.shape[0] // (2 * share)):
        front = value[2 * z * share : (2 * z + 1) * share]
        back = value[(2 * z + 1) * share : (2 * z + 2) * share]
        theirs[place + z, at : at + share] = jnp.where(core == 0, back, front)
        mine[place + z, at : at + share] = jnp.where(core == 0, front, back)


def outer(pieces, sl, right):
    return dot_tn(jnp.concatenate([piece[:, sl] for piece in pieces], axis=0), right).astype(BF)


def down_kernel(chips, micro, *refs):
    flag_ref, dy_hbm, arrived_ref = refs[:3]
    before = refs[3 : 2 + micro]
    refs = refs[2 + micro :]
    active, mixed = refs[:micro], refs[micro : 2 * micro]
    theirs, mine, dy_ref, sem = refs[2 * micro :]
    copy = pltpu.make_async_copy(dy_hbm.at[micro - 1], dy_ref, sem)
    copy.start()
    copy.wait()
    core = flag_ref[2]
    last = jnp.where(flag_ref[0] == 0, arrived_ref[...], dy_ref[...])
    dy = jnp.concatenate([ref[...] for ref in before] + [last], axis=0)
    hidden, local = active[0].shape[1], mixed[0].shape[1]
    share, step = hidden // (2 * chips), hidden // chips
    for z in range(chips):
        deal(theirs, mine, z, 0, core, outer(active, slice(z * step, (z + 1) * step), dy), share)
    deal(theirs, mine, 0, share, core, outer(mixed, slice(0, local), dy), local // (2 * chips))


def up_kernel(chips, micro, *refs):
    flag_ref = refs[0]
    a2, du, (theirs, mine) = refs[1 : 1 + micro], refs[1 + micro : 1 + 2 * micro], refs[1 + 2 * micro :]
    right = jnp.concatenate([ref[...] for ref in du], axis=0)
    width = a2[0].shape[1]
    share = width // (2 * chips)
    step = width // 2
    for j in range(2):
        value = outer(a2, slice(j * step, (j + 1) * step), right)
        deal(theirs, mine, j * chips // 2, 0, flag_ref[2], value, share)


def qkv_kernel(chips, micro, *refs):
    flag_ref = refs[0]
    a1, dqkv = refs[1 : 1 + micro], refs[1 + micro : 1 + 2 * micro]
    own, got, theirs, mine = refs[1 + 2 * micro :]
    width, local = a1[0].shape[1], own.shape[1]
    share = width // (2 * chips)
    step = width // 2
    for t in range(3):
        right = jnp.concatenate([ref[:, t * local : (t + 1) * local] for ref in dqkv], axis=0)
        for j in range(2):
            value = outer(a1, slice(j * step, (j + 1) * step), right)
            deal(theirs, mine, j * chips // 2, t * share, flag_ref[2], value, share)
    half = got.shape[0]
    lines = jnp.concatenate([own[:half] + got[...], own[half:]], axis=0).astype(BF)
    for z in range(chips):
        theirs[z, 3 * share :] = lines
        mine[z, 3 * share :] = lines


def o_kernel(micro, *refs):
    mixed_refs, active_refs = refs[:micro], refs[micro : 2 * micro]
    pack_ref, wout_hbm, wdown_hbm, out_ref, wout, wdown, mixed, active, sems = refs[2 * micro :]
    loads = Loads(sems)
    hbm, w = {"wout": wout_hbm, "wdown": wdown_hbm}, {"wout": wout, "wdown": wdown}
    loads.weight("wout", hbm, w)
    loads.weight("wdown", hbm, w)
    rows = mixed_refs[0].shape[0]
    for m in range(micro):
        mixed[m * rows : (m + 1) * rows] = mixed_refs[m][...]
        active[m * rows : (m + 1) * rows] = active_refs[m][...]
    vec = unpacked(pack_ref, wout.shape[1], wout.shape[0], wdown.shape[0])
    out_ref[...] = output_part(mixed, active, vec, w, loads.wait)


def add_kernel(at, x_hbm, one_ref, two_ref, out_ref, x_ref, sems):
    loads = Loads(sems)
    loads.start("x", x_hbm.at[at], x_ref)
    loads.wait("x")
    whole = x_ref[...].astype(F32) + (one_ref[...].astype(F32) + two_ref[...].astype(F32))
    out_ref[...] = whole.astype(BF)


VM = pl.BlockSpec(memory_space=pltpu.VMEM)
SM = pl.BlockSpec(memory_space=pltpu.SMEM)
HB = pl.BlockSpec(memory_space=pltpu.HBM)


def scratch_like(arrays):
    return [pltpu.VMEM(a.shape, a.dtype) for a in arrays]


def cost(ws, rows, passes):
    size = sum(math.prod(a.shape) for a in ws)
    return pl.CostEstimate(flops=2 * size * rows * passes, bytes_accessed=2 * size, transcendentals=0)


def params(mib):
    return pltpu.CompilerParams(vmem_limit_bytes=mib * 2**20)


def call_add(at, xs, one, two):
    rows, width = one.shape
    return pl.pallas_call(
        functools.partial(add_kernel, at),
        out_shape=jax.ShapeDtypeStruct((rows, width), BF),
        in_specs=[HB, VM, VM],
        out_specs=VM,
        scratch_shapes=[pltpu.VMEM((rows, width), BF), pltpu.SemaphoreType.DMA((1,))],
        compiler_params=params(8),
        cost_estimate=pl.CostEstimate(flops=rows * width * 2, bytes_accessed=rows * width * 8, transcendentals=0),
    )(xs, one, two)


def call_f(at, first, flags, xs, table, ws, vecs):
    rows, width = xs.shape[1:]
    local, hidden = ws[1].shape[0], ws[3].shape[0]
    out = jax.ShapeDtypeStruct((rows, width), BF)
    pack = jax.ShapeDtypeStruct((16, hidden), F32)
    scratch = scratch_like(ws) + [
        pltpu.VMEM((rows, local), BF),
        pltpu.VMEM((rows, hidden), BF),
        pltpu.VMEM((rows, width), BF),
        pltpu.SemaphoreType.DMA((24,)),
    ]
    return pl.pallas_call(
        functools.partial(f_kernel, at, first),
        out_shape=[out, pack] if first else out,
        in_specs=[SM, HB, VM] + [HB] * 4 + ([HB] * 8 if first else [VM]),
        out_specs=[VM, VM] if first else VM,
        scratch_shapes=scratch + (scratch_like(vecs) if first else []),
        compiler_params=params(60),
        cost_estimate=cost(ws, rows, 1),
    )(flags, xs, table, *ws, *vecs)


def call_fb(at, flags, xs, cots, arrived, table, pack, ws):
    rows, width = arrived.shape
    local, hidden = ws[1].shape[0], ws[3].shape[0]
    shape = jax.ShapeDtypeStruct
    outs = [shape((rows, width), BF)] * 4
    outs += [shape((rows, local), BF)] * 3
    outs += [
        shape((rows, 2 * rows * local // LANES), F32),
        shape((rows, local), BF),
        shape((rows, hidden), BF),
        shape((rows, hidden), F32),
    ]
    return pl.pallas_call(
        functools.partial(fb_kernel, at),
        out_shape=outs,
        in_specs=[SM, HB, HB, VM, VM, VM] + [HB] * 4,
        out_specs=[HB] * len(outs),
        scratch_shapes=scratch_like(outs)
        + scratch_like(ws)
        + [
            pltpu.VMEM((rows, hidden), BF),
            pltpu.VMEM((rows, 3 * local), BF),
            pltpu.VMEM((rows, width), BF),
            pltpu.VMEM((rows, width), BF),
            pltpu.SemaphoreType.DMA((16,)),
            pltpu.SemaphoreType.DMA((len(outs),)),
        ],
        compiler_params=params(60),
        cost_estimate=cost(ws, rows, 2),
    )(flags, xs, cots, arrived, table, pack, *ws)


def call_b(at, flags, x, cots, arrived, table, pack, ws, saved, after, before):
    rows, width = x.shape
    local, hidden = ws[1].shape[0], ws[3].shape[0]
    shape = jax.ShapeDtypeStruct
    outs = [
        shape((rows, width), BF),
        shape((rows, hidden), BF),
        shape((rows, 3 * local), BF),
        shape((16, local), F32),
        shape((8, local), F32),
        shape((rows, width), BF),
    ]
    return pl.pallas_call(
        functools.partial(b_kernel, at, not before, bool(after)),
        out_shape=outs,
        in_specs=[SM, VM, HB, VM, VM, VM] + [HB] * 4 + [VM] * 5 + [HB] * len(after) + [VM] * len(before),
        out_specs=[VM] * len(outs),
        scratch_shapes=scratch_like(ws) + [pltpu.VMEM((rows, width), BF), pltpu.SemaphoreType.DMA((16,))],
        compiler_params=params(60),
        cost_estimate=cost(ws, rows, 1),
    )(flags, x, cots, arrived, table, pack, *ws, *saved, *after, *before)


def call_blocks(kernel, flags, operands, specs, block, flops, scratch=()):
    outs = [jax.ShapeDtypeStruct(block, BF)] * 2
    return pl.pallas_call(
        kernel,
        out_shape=outs,
        in_specs=[SM] + specs,
        out_specs=[VM] * 2,
        scratch_shapes=list(scratch),
        compiler_params=params(60),
        cost_estimate=pl.CostEstimate(flops=flops, bytes_accessed=4 * math.prod(block), transcendentals=0),
    )(flags, *operands)


def call_o(mixed, active, pack, ws):
    micro, (rows, local) = len(mixed), mixed[0].shape
    hidden, width = ws[3].shape
    total = micro * rows
    return pl.pallas_call(
        functools.partial(o_kernel, micro),
        out_shape=jax.ShapeDtypeStruct((total, width), BF),
        in_specs=[VM] * (2 * micro + 1) + [HB] * 2,
        out_specs=VM,
        scratch_shapes=[
            pltpu.VMEM((local, width), BF),
            pltpu.VMEM((hidden, width), BF),
            pltpu.VMEM((total, local), BF),
            pltpu.VMEM((total, hidden), BF),
            pltpu.SemaphoreType.DMA((8,)),
        ],
        compiler_params=params(60),
        cost_estimate=cost((ws[1], ws[3]), total, 1),
    )(*mixed, *active, pack, ws[1], ws[3])


def swap(value):
    return lax.ppermute(value, "tensor", [(0, 1), (1, 0)])


def joined(one, two):
    return (one.astype(F32) + two.astype(F32)).astype(BF)


class Line:
    def __init__(self, theirs, mine, at):
        self.chips = mine.shape[0]
        self.place = at // 2
        parts = 2 * self.chips
        got = lax.ppermute(theirs, "dp", [(i, i ^ 1) for i in range(parts)])
        self.mine, self.got = mine, got
        self.right = self.left = None
        self.first = None
        self.sent = 0

    def block(self, index):
        index = jnp.clip(index, 0, self.chips - 1)
        one = lax.dynamic_index_in_dim(self.mine, index, 0, keepdims=False)
        two = lax.dynamic_index_in_dim(self.got, index, 0, keepdims=False)
        return one.astype(F32) + two.astype(F32)

    def step(self):
        self.sent += 1
        step, chips = self.sent, self.chips
        up = self.block(self.place + chips - step)
        down = self.block(self.place - chips + step)
        if self.right is not None:
            up = up + self.right.astype(F32)
            down = down + self.left.astype(F32)
        up, down = up.astype(BF), down.astype(BF)
        pairs = [(2 * z + c, 2 * z + 2 + c) for z in range(step) for c in range(2)]
        self.right = lax.ppermute(up, "dp", pairs)
        pairs = [(2 * z + c, 2 * z - 2 + c) for z in range(chips - step, chips) for c in range(2)]
        self.left = lax.ppermute(down, "dp", pairs)
        return [up, down]

    def result(self):
        while self.sent < self.chips - 1:
            self.step()
        return self.block(self.place) + (self.right.astype(F32) + self.left.astype(F32))


def wide(pieces, others):
    left, right = jnp.concatenate(pieces, axis=0), jnp.concatenate(others, axis=0)
    return jnp.einsum("ta,tb->ab", left, right, preferred_element_type=F32).astype(BF)


def scattered(blocks):
    parts, rows, columns = blocks.shape
    return lax.psum_scatter(blocks.reshape(parts * rows, columns), "dp", scatter_dimension=0, tiled=True).astype(F32)


def per_device(inputs, cotangent, g1, b1, g2, b2, w_qkv, b_qkv, w_out, b_out, w_up, b_up, w_down, b_down):
    section = lax.axis_index("section")
    owner = lax.axis_index("tensor")
    dp_at = lax.axis_index("dp")
    parts = lax.axis_size("dp")
    micro, seqs, length, width = inputs.shape
    rows = seqs * length
    local, hidden = w_out.shape[1], w_up.shape[2]
    flags = jnp.stack([section, owner, dp_at % 2]).astype(jnp.int32)
    table = jnp.asarray(rope_tables(length))
    vecs = (g1, b1, g2, b2, b_qkv[0], b_out, b_up, b_down)
    ws = (w_qkv[0].transpose(1, 0, 2), w_out[0], w_up[0], w_down[0])
    xs = inputs.reshape(micro, rows, width)
    cots = cotangent.reshape(micro, rows, width)
    lined = parts <= 8
    chips = parts // 2

    arrivals = []
    for m in range(micro):
        if m == 0:
            part, pack = call_f(m, True, flags, xs, table, ws, vecs)
        else:
            part = call_f(m, False, flags, xs, table, ws, (pack,))
        whole = call_add(m, xs, part, swap(part))
        arrivals.append(lax.ppermute(whole, "section", [(0, 1)]))
    kept, sources, backs = [], [], []
    for m in range(micro):
        dx, source, *saved = call_fb(m, flags, xs, cots, arrivals[m], table, pack, ws)
        whole = call_add(m, cots, dx, swap(dx))
        backs.append(lax.ppermute(whole, "section", [(1, 0)]))
        kept.append(dict(zip(SAVED, saved)))
        sources.append(source)
    a1, a2, mixed, active = ([kept[m][n] for m in range(micro)] for n in ("a1", "a2", "mixed", "g"))

    grads, dus, dqkvs, ups = [], [], [], []
    before, after = (), ()
    for m in range(micro):
        if m == micro - 1 and lined:
            block = (chips, hidden // parts + local // parts, width)
            theirs, mine = call_blocks(
                functools.partial(down_kernel, chips, micro),
                flags,
                (cots, backs[m], *ups, *active, *mixed),
                [HB] + [VM] * (3 * micro),
                block,
                2 * micro * rows * width * (hidden + local),
                [pltpu.VMEM((rows, width), BF), pltpu.SemaphoreType.DMA],
            )
            line_down = Line(theirs, mine, dp_at)
            after = tuple(line_down.step())
        saved = [kept[m][n] for n in ("q", "k", "v", "prob", "gp")]
        dx, du, dqkv, own, other, dy = call_b(
            m, flags, sources[m], cots, backs[m], table, pack, ws, saved, after, before
        )
        before = (own, other)
        grads.append(dx)
        dus.append(du)
        dqkvs.append(dqkv)
        ups.append(dy)
    got = swap(other)
    share = width // parts
    if lined:
        flops = 2 * micro * rows * width
        theirs, mine = call_blocks(
            functools.partial(up_kernel, chips, micro),
            flags,
            (*a2, *dus),
            [VM] * (2 * micro),
            (chips, share, hidden),
            flops * hidden,
        )
        line_up = Line(theirs, mine, dp_at)
        theirs, mine = call_blocks(
            functools.partial(qkv_kernel, chips, micro),
            flags,
            (*a1, *dqkvs, own, got),
            [VM] * (2 * micro + 2),
            (chips, 3 * share + own.shape[0], local),
            flops * 3 * local,
        )
        line_qkv = Line(theirs, mine, dp_at)
        d_both, d_wup, last = line_down.result(), line_up.result(), line_qkv.result()
    else:
        d_wdown = wide(active, ups).reshape(parts, -1, width)
        d_wout = wide(mixed, ups).reshape(parts, -1, width)
        d_both = scattered(jnp.concatenate([d_wdown, d_wout], axis=1))
        d_wup = scattered(wide(a2, dus).reshape(parts, -1, hidden))
        d_wqkv = wide(a1, dqkvs).reshape(parts, share, 3, local).transpose(0, 2, 1, 3)
        lines = jnp.concatenate([own[: got.shape[0]] + got, own[got.shape[0] :]]).astype(BF)
        lines = jnp.broadcast_to(lines[None], (parts,) + lines.shape)
        last = scattered(jnp.concatenate([d_wqkv.reshape(parts, 3 * share, local), lines], axis=1))
    down_rows = hidden // parts
    d_wdown, d_wout = d_both[:down_rows], d_both[down_rows:]
    d_wqkv = last[: 3 * share].reshape(3, share, local).transpose(1, 0, 2)
    lines = last[3 * share :]
    d_vec = lax.dynamic_slice(lines, (0, dp_at * (local // parts)), (8, local // parts))
    up_lines = lines[8 : 8 + hidden // local].reshape(1, hidden)
    d_bup = lax.dynamic_slice_in_dim(up_lines, dp_at * down_rows, down_rows, 1)

    part = call_o(mixed, active, pack, ws)
    other_part = swap(part)
    section_out = jnp.concatenate(sources, axis=0).astype(F32) + (part.astype(F32) + other_part.astype(F32))
    input_grad = jnp.stack([ups[m].astype(F32) + (grads[m].astype(F32) + swap(grads[m]).astype(F32)) for m in range(micro)])
    return (
        section_out.astype(BF).reshape(1, micro, seqs, length, width),
        input_grad.reshape(1, micro, seqs, length, width),
        d_vec[0:1],
        d_vec[1:2],
        d_vec[2:3],
        d_vec[3:4],
        d_wqkv[None],
        d_vec[5:8][None],
        d_wout[None],
        d_vec[4:5],
        d_wup[None],
        d_bup,
        d_wdown[None],
        d_vec[4:5],
    )


def solution(mesh):
    return jax.shard_map(
        per_device,
        mesh=mesh,
        in_specs=(
            P(None, "dp", None, None),
            P(None, "dp", None, None),
            P("section", None),
            P("section", None),
            P("section", None),
            P("section", None),
            P("section", None, None, "tensor"),
            P("section", None, "tensor"),
            P("section", "tensor", None),
            P("section", None),
            P("section", None, "tensor"),
            P("section", "tensor"),
            P("section", "tensor", None),
            P("section", None),
        ),
        out_specs=(
            P("section", None, "dp", None, None),
            P("section", None, "dp", None, None),
            P("section", ("tensor", "dp")),
            P("section", ("tensor", "dp")),
            P("section", ("tensor", "dp")),
            P("section", ("tensor", "dp")),
            P("section", "dp", None, "tensor"),
            P("section", None, ("tensor", "dp")),
            P("section", ("tensor", "dp"), None),
            P("section", ("tensor", "dp")),
            P("section", "dp", "tensor"),
            P("section", ("tensor", "dp")),
            P("section", ("tensor", "dp"), None),
            P("section", ("tensor", "dp")),
        ),
        check_vma=False,
    )
```

```python
import functools
import math

import jax
import jax.numpy as jnp
import numpy as np
from jax import lax
from jax.experimental import pallas as pl
from jax.experimental.pallas import tpu as pltpu
from jax.sharding import PartitionSpec as P

HEAD = 64
ROT = 16
LANES = 128
PIECE = 512
AHEAD = 40
EPSILON = 1e-05
BF = jnp.bfloat16
F32 = jnp.float32


def rope_tables(length):
    half = ROT // 2
    inverse = np.exp(-math.log(10000.0) * np.arange(half, dtype=np.float32) * np.float32(2.0) / ROT)
    angle = np.arange(length, dtype=np.float32)[:, None] * inverse[None, :].astype(np.float32)
    cosine, sine = np.cos(angle), np.sin(angle)
    table = np.zeros((3, length, LANES), np.float32)
    table[0] = 1.0
    for head in range(LANES // HEAD):
        at = head * HEAD
        table[0, :, at : at + half] = cosine
        table[0, :, at + half : at + ROT] = cosine
        table[1, :, at : at + half] = -sine
        table[2, :, at + half : at + ROT] = sine
    return table


def dot(a, b):
    return jnp.dot(a, b, preferred_element_type=F32)


def dot_nt(a, b):
    return lax.dot_general(a, b, (((1,), (1,)), ((), ())), preferred_element_type=F32)


def dot_tn(a, b):
    return lax.dot_general(a, b, (((0,), (0,)), ((), ())), preferred_element_type=F32)


def roped(value, table, sign):
    half = ROT // 2
    ahead = pltpu.roll(value, LANES - half, 1) * table[1]
    behind = pltpu.roll(value, half, 1) * table[2]
    return value * table[0] + sign * (ahead + behind)


def head_pair(value):
    low = lax.broadcasted_iota(jnp.int32, value.shape, 1) < HEAD
    zero = jnp.zeros_like(value)
    return jnp.concatenate([jnp.where(low, value, zero), jnp.where(low, zero, value)], axis=0)


def pair_merge(value):
    rows = value.shape[0] // 2
    low = lax.broadcasted_iota(jnp.int32, (rows, LANES), 1) < HEAD
    return jnp.where(low, value[:rows], value[rows:])


def normal(block):
    width = block.shape[1]
    center = block - jnp.sum(block, axis=1, keepdims=True) * (1.0 / width)
    spread = jnp.sum(center * center, axis=1, keepdims=True) * (1.0 / width)
    scale = lax.rsqrt(spread + EPSILON)
    return center * scale, scale


def forward_part(x, vec, table, w, wait, put):
    rows, width = x.shape
    unit, unused = normal(x.astype(F32))
    first = (unit * vec["g1"] + vec["b1"]).astype(BF)
    second = (unit * vec["g2"] + vec["b2"]).astype(BF)
    put("a1", first)
    put("a2", second)
    bqkv = vec["bqkv"]
    raw = []
    for j in range(3):
        wait("wqkv", j)
        raw.append(dot(first, w["wqkv"][j]) + bqkv[j : j + 1])
    local = raw[0].shape[1]
    wait("table")
    length = table.shape[1]
    row = lax.broadcasted_iota(jnp.int32, (length, length), 0)
    keep = row >= lax.broadcasted_iota(jnp.int32, (length, length), 1)
    for start in range(0, rows, length):
        rs = slice(start, start + length)
        for p in range(local // LANES):
            sl = slice(p * LANES, (p + 1) * LANES)
            q = roped(raw[0][rs, sl], table, 1.0).astype(BF)
            k = roped(raw[1][rs, sl], table, 1.0).astype(BF)
            v = raw[2][rs, sl].astype(BF)
            put("q", q, sl)
            put("k", k, sl)
            put("v", v, sl)
            scores = dot_nt(q, head_pair(k)) * HEAD**-0.5
            prob = []
            for h in range(2):
                part = jnp.where(keep, scores[:, h * length : (h + 1) * length], -1e30)
                expo = jnp.exp(part - jnp.max(part, axis=1, keepdims=True))
                prob.append(expo * (1.0 / jnp.sum(expo, axis=1, keepdims=True)))
            prob = jnp.concatenate(prob, axis=1).astype(BF)
            put("prob", prob, slice(p * 2 * length, (p + 1) * 2 * length))
            put("mixed", dot(prob, head_pair(v)).astype(BF), sl, rs)
    hidden = w["wup"].shape[1]
    step = 256
    for c in range(0, hidden, step):
        sl = slice(c, c + step)
        wait("wup", c // PIECE)
        u = dot(second, w["wup"][:, sl]) + vec["bup"][:, sl]
        phi = 0.5 + 0.5 * lax.erf(u * (2.0**-0.5))
        put("g", (u * phi).astype(BF), sl)
        put("gp", lambda: phi + u * (jnp.exp(-0.5 * u * u) * (2.0 * math.pi) ** -0.5), sl)


def output_part(mixed, active, vec, w, wait):
    wait("wout")
    total = dot(mixed[...], w["wout"][...])
    wait("wdown")
    total = total + dot(active[...], w["wdown"][...])
    return (total + vec["extra"]).astype(BF)


def backward_part(dy, saved, table, w, wait, put):
    rows = dy.shape[0]
    hidden = w["wdown"].shape[0]
    step = 256
    wait("gp")
    for c in range(0, hidden, step):
        sl = slice(c, c + step)
        wait("wdown", c // PIECE)
        du = (dot_nt(dy, w["wdown"][sl, :]) * saved["gp"][:, sl].astype(F32)).astype(BF)
        put("du", du, sl)
    wait("wout")
    for name in ("table", "q", "k", "v", "prob"):
        wait(name)
    d_mixed = dot_nt(dy, w["wout"][...]).astype(BF)
    local = d_mixed.shape[1]
    length = table.shape[1]
    scale = HEAD**-0.5
    for start in range(0, rows, length):
        rs = slice(start, start + length)
        for p in range(local // LANES):
            sl = slice(p * LANES, (p + 1) * LANES)
            q, k, v = saved["q"][rs, sl], saved["k"][rs, sl], saved["v"][rs, sl]
            low = saved["prob"][rs, p * 2 * length : (p + 1) * 2 * length]
            prob = low.astype(F32)
            d_tile = d_mixed[rs, sl]
            d_prob = dot_nt(d_tile, head_pair(v))
            d_value = pair_merge(dot_tn(low, d_tile))
            d_scores = []
            for h in range(2):
                part = prob[:, h * length : (h + 1) * length]
                d_part = d_prob[:, h * length : (h + 1) * length]
                both = part * d_part
                d_scores.append(both - part * jnp.sum(both, axis=1, keepdims=True))
            d_scores = jnp.concatenate(d_scores, axis=1).astype(BF)
            d_query = dot(d_scores, head_pair(k)) * scale
            d_keys = pair_merge(dot_tn(d_scores, q)) * scale
            at = p * LANES
            put("dqkv", roped(d_query, table, -1.0).astype(BF), slice(at, at + LANES), rs)
            at += local
            put("dqkv", roped(d_keys, table, -1.0).astype(BF), slice(at, at + LANES), rs)
            at += local
            put("dqkv", d_value.astype(BF), slice(at, at + LANES), rs)


def norm_back(x, du, dqkv, local, vec, w, wait):
    wait("wup")
    d_second = dot_nt(du[...], w["wup"][...])
    for j in range(3):
        wait("wqkv", j)
    d_first = dot_nt(dqkv[:, :local], w["wqkv"][0])
    for j in range(1, 3):
        d_first = d_first + dot_nt(dqkv[:, j * local : (j + 1) * local], w["wqkv"][j])
    unit, scale = normal(x.astype(F32))
    e = d_first * vec["g1"] + d_second * vec["g2"]
    width = x.shape[1]
    mean = jnp.sum(e, axis=1, keepdims=True) * (1.0 / width)
    along = jnp.sum(e * unit, axis=1, keepdims=True) * (1.0 / width)
    dx = (e - mean - unit * along) * scale
    return dx.astype(BF), d_first, d_second, unit


WEIGHTS = ("wqkv", "wout", "wup", "wdown")
VECTORS = ("g1", "b1", "g2", "b2", "bqkv", "bout", "bup", "bdown")
NEEDED = ("q", "k", "v", "prob", "gp")
SAVED = ("a1", "a2", "q", "k", "v", "prob", "mixed", "g", "gp")


class Loads:
    def __init__(self, sems, ahead=64):
        self.sems, self.copies, self.queue, self.ahead = sems, {}, [], ahead
        self.started = self.waited = 0

    def start(self, name, source, target):
        copy = pltpu.make_async_copy(source, target, self.sems.at[len(self.queue)])
        self.copies.setdefault(name, {})[len(self.copies.get(name, {}))] = (len(self.queue), copy)
        self.queue.append(copy)
        self.pump(self.waited + self.ahead)

    def pump(self, until):
        while self.started < min(until, len(self.queue)):
            self.queue[self.started].start()
            self.started += 1

    def weight(self, name, hbm, w):
        source, target = hbm[name], w[name]
        if name == "wqkv":
            for j in range(3):
                self.start(name, source.at[j], target.at[j])
        elif name == "wout":
            self.start(name, source, target)
        else:
            for c in range(0, source.shape[0 if name == "wdown" else 1], PIECE):
                at = (pl.ds(c, PIECE), slice(None)) if name == "wdown" else (slice(None), pl.ds(c, PIECE))
                self.start(name, source.at[at], target.at[at])

    def wait(self, name, index=None):
        left = self.copies.get(name, {})
        for piece in [index] if index is not None else list(left):
            if piece in left:
                at, copy = left.pop(piece)
                self.pump(at + 1)
                copy.wait()
                self.waited += 1
                self.pump(self.waited + self.ahead)


def unpacked(pack, width, local, hidden):
    return {
        "g1": pack[0:1, :width],
        "b1": pack[1:2, :width],
        "g2": pack[2:3, :width],
        "b2": pack[3:4, :width],
        "extra": pack[4:5, :width],
        "bup": pack[5:6, :hidden],
        "bqkv": pack[6:9, :local],
    }


def f_kernel(micro, *refs):
    flag_ref, x_hbm, table_hbm = refs[:3]
    hbm = dict(zip(WEIGHTS, refs[3:7]))
    vec_hbm = dict(zip(VECTORS, refs[7:15]))
    out_refs, pack_ref = refs[15 : 15 + micro], refs[15 + micro]
    refs = refs[16 + micro :]
    w = dict(zip(WEIGHTS, refs[:4]))
    mixed, active, x_ref, table_ref, sems = refs[4:9]
    loads = Loads(sems)
    vec_ref = dict(zip(VECTORS, refs[9:]))
    rows, width = out_refs[0].shape
    for m in range(micro):
        loads.start("x", x_hbm.at[m], x_ref.at[pl.ds(m * rows, rows)])
    for name in VECTORS:
        loads.start(name, vec_hbm[name], vec_ref[name])
    loads.weight("wqkv", hbm, w)
    loads.start("table", table_hbm, table_ref)
    for name in ("wup", "wout", "wdown"):
        loads.weight(name, hbm, w)
    local, hidden = mixed.shape[1], active.shape[1]
    for name in VECTORS:
        loads.wait(name)
    for i, name in enumerate(("g1", "b1", "g2", "b2")):
        pack_ref[i : i + 1, :width] = vec_ref[name][...].astype(F32)
    extra = vec_ref["bout"][...].astype(F32) + vec_ref["bdown"][...].astype(F32)
    pack_ref[4:5, :width] = jnp.where(flag_ref[1] == 0, extra, jnp.zeros_like(extra))
    pack_ref[5:6, :hidden] = vec_ref["bup"][...].astype(F32)
    pack_ref[6:9, :local] = vec_ref["bqkv"][...].astype(F32)
    vec = unpacked(pack_ref, width, local, hidden)

    def put(name, value, sl=slice(None), rs=slice(None)):
        if name == "mixed":
            mixed[rs, sl] = value
        if name == "g":
            active[rs, sl] = value

    loads.wait("x")
    forward_part(x_ref[...], vec, table_ref, w, loads.wait, put)
    out = output_part(mixed, active, vec, w, loads.wait)
    for m in range(micro):
        out_refs[m][...] = out[m * rows : (m + 1) * rows]


def fb_kernel(at, *refs):
    flag_ref, x_hbm, dy_hbm, arrived_hbm, table_hbm, pack_hbm = refs[:6]
    hbm = dict(zip(WEIGHTS, refs[6:10]))
    names = ("dx", "source") + SAVED
    outs = dict(zip(names, refs[10 : 10 + len(names)]))
    refs = refs[10 + len(names) :]
    held = dict(zip(names, refs[: len(names)]))
    refs = refs[len(names) :]
    w = dict(zip(WEIGHTS, refs[:4]))
    du, dqkv, x_ref, dy_ref, arrived_ref, table_ref, pack_ref, sems, out_sems = refs[4:]
    loads, stores = Loads(sems, AHEAD + 2), Loads(out_sems)
    loads.start("x", x_hbm.at[at], x_ref)
    loads.start("arrived", arrived_hbm, arrived_ref)
    loads.start("pack", pack_hbm, pack_ref)
    loads.weight("wqkv", hbm, w)
    loads.start("table", table_hbm, table_ref)
    loads.weight("wup", hbm, w)
    loads.start("dy", dy_hbm.at[at], dy_ref)
    loads.weight("wdown", hbm, w)
    loads.weight("wout", hbm, w)
    held_too = dict(held, du=du, dqkv=dqkv)

    def put(name, value, sl=slice(None), rs=slice(None)):
        ref = held_too[name]
        value = value() if callable(value) else value
        ref[rs, sl] = value.astype(ref.dtype)

    width, (local, hidden) = x_ref.shape[1], (dqkv.shape[1] // 3, du.shape[1])
    loads.wait("x")
    loads.wait("arrived")
    x = jnp.where(flag_ref[0] == 0, x_ref[...], arrived_ref[...])
    loads.wait("pack")
    vec = unpacked(pack_ref, width, local, hidden)
    held["source"][...] = x
    forward_part(x, vec, table_ref, w, loads.wait, put)
    for name in ("source",) + SAVED:
        stores.start(name, held[name], outs[name])
    loads.wait("dy")
    backward_part(dy_ref[...], held, table_ref, w, loads.wait, put)
    held["dx"][...] = norm_back(x, du, dqkv, local, vec, w, loads.wait)[0]
    stores.start("dx", held["dx"], outs["dx"])
    for name in names:
        stores.wait(name)


def b_kernel(micro, *refs):
    flag_ref, dy_hbm, table_hbm, pack_hbm = refs[:4]
    hbm = dict(zip(WEIGHTS, refs[4:8]))
    names = ("arrived", "x") + NEEDED
    pieces = {n: refs[8 + i * micro : 8 + (i + 1) * micro] for i, n in enumerate(names)}
    refs = refs[-(6 + 4 + 3 + len(names) + 1) :]
    dx_ref, du, dqkv, own, other, dy_out = refs[:6]
    w = dict(zip(WEIGHTS, refs[6:10]))
    dy_ref, table_ref, pack_ref = refs[10:13]
    saved = dict(zip(names, refs[13:-1]))
    loads = Loads(refs[-1])
    rows = pieces["x"][0].shape[0]

    def both(name):
        for m in range(micro):
            loads.start(name, pieces[name][m], saved[name].at[pl.ds(m * rows, rows)])

    for m in range(micro):
        loads.start("dy", dy_hbm.at[m], dy_ref.at[pl.ds(m * rows, rows)])
    both("arrived")
    both("gp")
    loads.weight("wdown", hbm, w)
    loads.weight("wout", hbm, w)
    loads.start("table", table_hbm, table_ref)
    for name in NEEDED[:4]:
        both(name)
    loads.weight("wup", hbm, w)
    loads.weight("wqkv", hbm, w)
    both("x")
    loads.start("pack", pack_hbm, pack_ref)
    kept = {"du": du, "dqkv": dqkv}

    def put(name, value, sl=slice(None), rs=slice(None)):
        kept[name][rs, sl] = value

    loads.wait("dy")
    loads.wait("arrived")
    dy = jnp.where(flag_ref[0] == 0, saved["arrived"][...], dy_ref[...])
    dy_out[...] = dy
    width, (local, hidden) = dy.shape[1], (dqkv.shape[1] // 3, du.shape[1])
    backward_part(dy, saved, table_ref, w, loads.wait, put)
    loads.wait("x")
    loads.wait("pack")
    vec = unpacked(pack_ref, width, local, hidden)
    dx, d_first, d_second, unit = norm_back(saved["x"][...], du, dqkv, local, vec, w, loads.wait)
    dx_ref[...] = dx
    own[...] = jnp.zeros_like(own)
    other[...] = jnp.zeros_like(other)
    low = flag_ref[1] == 0
    terms = (d_first * unit, d_first, d_second * unit, d_second, dy.astype(F32))
    for i, term in enumerate(terms):
        total = jnp.sum(term, axis=0, keepdims=True)
        front, back = total[:, :local], total[:, local:]
        own[i : i + 1] = jnp.where(low, front, back)
        if i < 4:
            other[i : i + 1] = jnp.where(low, back, front)
    line = 5
    for ref in (dqkv, du):
        for c in range(0, ref.shape[1], local):
            own[line : line + 1] = jnp.sum(ref[:, c : c + local].astype(F32), axis=0, keepdims=True)
            line += 1


def deal(theirs, mine, place, at, core, value, share):
    for z in range(value.shape[0] // (2 * share)):
        front = value[2 * z * share : (2 * z + 1) * share]
        back = value[(2 * z + 1) * share : (2 * z + 2) * share]
        theirs[place + z, at : at + share] = jnp.where(core == 0, back, front)
        mine[place + z, at : at + share] = jnp.where(core == 0, front, back)


def outer(pieces, sl, right):
    return dot_tn(jnp.concatenate([piece[:, sl] for piece in pieces], axis=0), right).astype(BF)


def down_kernel(chips, micro, *refs):
    flag_ref, dy_hbm = refs[:2]
    arrived, active, mixed = (refs[2 + i * micro : 2 + (i + 1) * micro] for i in range(3))
    theirs, mine, dy_ref, sem = refs[2 + 3 * micro :]
    copy = pltpu.make_async_copy(dy_hbm, dy_ref, sem)
    copy.start()
    copy.wait()
    core = flag_ref[2]
    dy = [jnp.where(flag_ref[0] == 0, arrived[m][...], dy_ref[m]) for m in range(micro)]
    dy = jnp.concatenate(dy, axis=0)
    hidden, local = active[0].shape[1], mixed[0].shape[1]
    share, step = hidden // (2 * chips), hidden // chips
    for z in range(chips):
        deal(theirs, mine, z, 0, core, outer(active, slice(z * step, (z + 1) * step), dy), share)
    deal(theirs, mine, 0, share, core, outer(mixed, slice(0, local), dy), local // (2 * chips))


def rest_kernel(chips, micro, *refs):
    flag_ref, du, dqkv, own, got = refs[:5]
    a1, a2, (theirs, mine) = refs[5 : 5 + micro], refs[5 + micro : 5 + 2 * micro], refs[-2:]
    width, local = a1[0].shape[1], own.shape[1]
    share = width // (2 * chips)
    step = width // 2
    at = 0
    for left, right in ((a2, du), (a1, dqkv)):
        for c in range(0, right.shape[1], local):
            columns = right[:, c : c + local]
            for j in range(2):
                value = outer(left, slice(j * step, (j + 1) * step), columns)
                deal(theirs, mine, j * chips // 2, at, flag_ref[2], value, share)
            at += share
    half = got.shape[0]
    lines = jnp.concatenate([own[:half] + got[...], own[half:]], axis=0).astype(BF)
    for z in range(chips):
        theirs[z, at:] = lines
        mine[z, at:] = lines


def arrived_sum(flag_ref, refs, scratch, sems):
    place = flag_ref[3]
    loads = Loads(sems)
    for i in range(2):
        loads.start(i, refs[i].at[place], scratch.at[i])
    edge = jnp.logical_or(place == 0, place == 3)
    for i in range(2):
        loads.wait(i)

    def total(at, rows):
        sl = slice(at, at + rows)
        value = refs[2][sl, :].astype(F32)
        value = jnp.where(edge, value, jnp.zeros_like(value))
        value = value + (scratch[0, sl, :].astype(F32) + scratch[1, sl, :].astype(F32))
        for ref in refs[3:7]:
            value = value + ref[sl, :].astype(F32)
        return value

    return total


def final_down_kernel(flag_ref, *refs):
    down_ref, out_ref, scratch, sems = refs[-4:]
    total = arrived_sum(flag_ref, refs[:7], scratch, sems)
    rows = down_ref.shape[0]
    down_ref[...] = total(0, rows)
    out_ref[...] = total(rows, out_ref.shape[0])


def final_rest_kernel(flag_ref, *refs):
    up_ref, qkv_ref, vec_ref, bqkv_ref, bup_ref, lines, scratch, sems = refs[-8:]
    total = arrived_sum(flag_ref, refs[:7], scratch, sems)
    share, local = qkv_ref.shape[1:]
    at = 0
    for c in range(0, up_ref.shape[1], local):
        up_ref[:, c : c + local] = total(at, share)
        at += share
    for t in range(3):
        qkv_ref[t] = total(at, share)
        at += share
    lines[...] = total(at, lines.shape[0])
    dp_at = 2 * flag_ref[3] + flag_ref[2]
    width = bqkv_ref.shape[1]
    front = pltpu.roll(lines[0:8], local - dp_at * width, 1)
    vec_ref[...] = front[0:5, :width]
    bqkv_ref[...] = front[5:8, :width]
    width = bup_ref.shape[1]
    per_line = local // width
    line = pltpu.roll(lines[8:16], local - (dp_at % per_line) * width, 1)
    row = dp_at // per_line
    picked = jnp.zeros((1, width), F32)
    for i in range(per_line and 8 // per_line):
        picked = jnp.where(row == i, line[i : i + 1, :width], picked)
    bup_ref[...] = picked


def tail_kernel(micro, *refs):
    part, other, up, grad, other_grad = refs[:5]
    sources = refs[5 : 5 + micro]
    out_ref, grad_ref = refs[-2:]
    rows = sources[0].shape[0]
    for m in range(micro):
        sl = slice(m * rows, (m + 1) * rows)
        both = part[sl].astype(F32) + other[sl].astype(F32)
        out_ref[sl] = (sources[m][...].astype(F32) + both).astype(BF)
    grad_ref[...] = up[...].astype(F32) + (grad[...].astype(F32) + other_grad[...].astype(F32))


def o_kernel(micro, *refs):
    mixed_refs, active_refs = refs[:micro], refs[micro : 2 * micro]
    pack_ref, wout_hbm, wdown_hbm = refs[2 * micro : 2 * micro + 3]
    out_ref, wout, wdown, mixed, active, sems = refs[-6:]
    loads = Loads(sems)
    hbm, w = {"wout": wout_hbm, "wdown": wdown_hbm}, {"wout": wout, "wdown": wdown}
    loads.weight("wout", hbm, w)
    loads.weight("wdown", hbm, w)
    rows = mixed_refs[0].shape[0]
    for m in range(micro):
        mixed[m * rows : (m + 1) * rows] = mixed_refs[m][...]
        active[m * rows : (m + 1) * rows] = active_refs[m][...]
    vec = unpacked(pack_ref, wout.shape[1], wout.shape[0], wdown.shape[0])
    out_ref[...] = output_part(mixed, active, vec, w, loads.wait)


def add_kernel(at, x_hbm, one_ref, two_ref, out_ref, x_ref, sems):
    loads = Loads(sems)
    loads.start("x", x_hbm.at[at], x_ref)
    loads.wait("x")
    whole = x_ref[...].astype(F32) + (one_ref[...].astype(F32) + two_ref[...].astype(F32))
    out_ref[...] = whole.astype(BF)


VM = pl.BlockSpec(memory_space=pltpu.VMEM)
SM = pl.BlockSpec(memory_space=pltpu.SMEM)
HB = pl.BlockSpec(memory_space=pltpu.HBM)


def scratch_like(arrays):
    return [pltpu.VMEM(a.shape, a.dtype) for a in arrays]


def cost(ws, rows, passes):
    size = sum(math.prod(a.shape) for a in ws)
    return pl.CostEstimate(flops=2 * size * rows * passes, bytes_accessed=2 * size, transcendentals=0)


def params(mib):
    return pltpu.CompilerParams(vmem_limit_bytes=mib * 2**20)


def call_add(at, xs, one, two):
    rows, width = one.shape
    return pl.pallas_call(
        functools.partial(add_kernel, at),
        out_shape=jax.ShapeDtypeStruct((rows, width), BF),
        in_specs=[HB, VM, VM],
        out_specs=VM,
        scratch_shapes=[pltpu.VMEM((rows, width), BF), pltpu.SemaphoreType.DMA((1,))],
        compiler_params=params(8),
        cost_estimate=pl.CostEstimate(flops=rows * width * 2, bytes_accessed=rows * width * 8, transcendentals=0),
    )(xs, one, two)


def call_f(flags, xs, table, ws, vecs):
    micro, rows, width = xs.shape
    local, hidden = ws[1].shape[0], ws[3].shape[0]
    total = micro * rows
    scratch = scratch_like(ws) + [
        pltpu.VMEM((total, local), BF),
        pltpu.VMEM((total, hidden), BF),
        pltpu.VMEM((total, width), BF),
        pltpu.VMEM(table.shape, F32),
        pltpu.SemaphoreType.DMA((24,)),
    ]
    out = [jax.ShapeDtypeStruct((rows, width), BF)] * micro + [jax.ShapeDtypeStruct((16, hidden), F32)]
    return pl.pallas_call(
        functools.partial(f_kernel, micro),
        out_shape=out,
        in_specs=[SM] + [HB] * 14,
        out_specs=[VM] * len(out),
        scratch_shapes=scratch + scratch_like(vecs),
        compiler_params=params(54),
        cost_estimate=cost(ws, total, 1),
    )(flags, xs, table, *ws, *vecs)


def call_fb(at, flags, xs, cots, arrived, table, pack, ws):
    rows, width = arrived.shape
    local, hidden = ws[1].shape[0], ws[3].shape[0]
    shape = jax.ShapeDtypeStruct
    outs = [shape((rows, width), BF)] * 4
    outs += [shape((rows, local), BF)] * 3
    outs += [
        shape((rows, 2 * rows * local // LANES), BF),
        shape((rows, local), BF),
        shape((rows, hidden), BF),
        shape((rows, hidden), BF),
    ]
    return pl.pallas_call(
        functools.partial(fb_kernel, at),
        out_shape=outs,
        in_specs=[SM] + [HB] * 9,
        out_specs=[HB] * len(outs),
        scratch_shapes=scratch_like(outs)
        + scratch_like(ws)
        + [
            pltpu.VMEM((rows, hidden), BF),
            pltpu.VMEM((rows, 3 * local), BF),
            pltpu.VMEM((rows, width), BF),
            pltpu.VMEM((rows, width), BF),
            pltpu.VMEM((rows, width), BF),
            pltpu.VMEM(table.shape, F32),
            pltpu.VMEM(pack.shape, F32),
            pltpu.SemaphoreType.DMA((24,)),
            pltpu.SemaphoreType.DMA((len(outs),)),
        ],
        compiler_params=params(54),
        cost_estimate=cost(ws, rows, 2),
    )(flags, xs, cots, arrived, table, pack, *ws)


def call_b(flags, cots, table, pack, ws, pieces, after):
    micro, rows, width = cots.shape
    local, hidden = ws[1].shape[0], ws[3].shape[0]
    shape = jax.ShapeDtypeStruct
    total = micro * rows
    outs = [
        shape((total, width), BF),
        shape((total, hidden), BF),
        shape((total, 3 * local), BF),
        shape((16, local), F32),
        shape((8, local), F32),
        shape((total, width), BF),
    ]
    flat = [array for group in pieces for array in group]
    return pl.pallas_call(
        functools.partial(b_kernel, micro),
        out_shape=outs,
        in_specs=[SM] + [HB] * (7 + len(flat) + len(after)),
        out_specs=[VM] * len(outs),
        scratch_shapes=scratch_like(ws)
        + [pltpu.VMEM((total, width), BF)]
        + scratch_like([table, pack])
        + [pltpu.VMEM((total, group[0].shape[1]), group[0].dtype) for group in pieces]
        + [pltpu.SemaphoreType.DMA((32,))],
        compiler_params=params(54),
        cost_estimate=cost(ws, total, 1),
    )(flags, cots, table, pack, *ws, *flat, *after)


def call_blocks(kernel, flags, operands, specs, block, flops, scratch=()):
    outs = [jax.ShapeDtypeStruct(block, BF)] * 2
    return pl.pallas_call(
        kernel,
        out_shape=outs,
        in_specs=[SM] + specs,
        out_specs=[VM] * 2,
        scratch_shapes=list(scratch),
        compiler_params=params(54),
        cost_estimate=pl.CostEstimate(flops=flops, bytes_accessed=4 * math.prod(block), transcendentals=0),
    )(flags, *operands)


def call_final(kernel, flags, parts, outs, after, scratch=()):
    return pl.pallas_call(
        kernel,
        out_shape=[jax.ShapeDtypeStruct(shape, F32) for shape in outs],
        in_specs=[SM, HB, HB] + [VM] * 5 + [HB] * len(after),
        out_specs=[VM] * len(outs),
        scratch_shapes=list(scratch)
        + [pltpu.VMEM((2,) + parts[2].shape, BF), pltpu.SemaphoreType.DMA((2,))],
        compiler_params=params(16),
    )(flags, *parts, *after)


def call_tail(part, other, up, grad, other_grad, sources, after):
    micro = len(sources)
    return pl.pallas_call(
        functools.partial(tail_kernel, micro),
        out_shape=[jax.ShapeDtypeStruct(part.shape, BF), jax.ShapeDtypeStruct(part.shape, F32)],
        in_specs=[VM] * (5 + micro) + [HB] * len(after),
        out_specs=[VM] * 2,
        compiler_params=params(16),
    )(part, other, up, grad, other_grad, *sources, *after)


def call_o(mixed, active, pack, ws, after=()):
    micro, (rows, local) = len(mixed), mixed[0].shape
    hidden, width = ws[3].shape
    total = micro * rows
    return pl.pallas_call(
        functools.partial(o_kernel, micro),
        out_shape=jax.ShapeDtypeStruct((total, width), BF),
        in_specs=[VM] * (2 * micro + 1) + [HB] * (2 + len(after)),
        out_specs=VM,
        scratch_shapes=[
            pltpu.VMEM((local, width), BF),
            pltpu.VMEM((hidden, width), BF),
            pltpu.VMEM((total, local), BF),
            pltpu.VMEM((total, hidden), BF),
            pltpu.SemaphoreType.DMA((8,)),
        ],
        compiler_params=params(54),
        cost_estimate=cost((ws[1], ws[3]), total, 1),
    )(*mixed, *active, pack, ws[1], ws[3], *after)


def swap(value):
    return lax.ppermute(value, "tensor", [(0, 1), (1, 0)])


class Line:
    def __init__(self, theirs, mine, at):
        self.place = at // 2
        self.mine = mine
        self.got = lax.ppermute(theirs, "dp", [(i, i ^ 1) for i in range(8)])

    def block(self, index):
        one = lax.dynamic_index_in_dim(self.mine, index, 0, keepdims=False)
        two = lax.dynamic_index_in_dim(self.got, index, 0, keepdims=False)
        return one.astype(F32) + two.astype(F32)

    def send(self, value, pairs):
        return lax.ppermute(value, "dp", [(2 * a + c, 2 * b + c) for a, b in pairs for c in range(2)])

    def start(self):
        place = self.place
        values = [
            self.block(index).astype(BF)
            for index in (
                jnp.where(place % 2 == 0, 3, 0),
                jnp.where(place == 1, 2, 1),
                jnp.where(place == 0, 2, 1),
                jnp.where(place == 0, 1, 2),
            )
        ]
        self.one = self.send(values[0], [(0, 1), (1, 0), (2, 3), (3, 2)])
        self.three = self.send(values[1], [(1, 2), (2, 1)])
        self.four = self.send(values[2], [(0, 2), (3, 1)])
        self.two = self.send(values[3], [(0, 1), (3, 2)])
        return tuple(values)

    def relay(self):
        value = (self.block(jnp.where(self.place == 1, 3, 0)) + self.one.astype(F32)).astype(BF)
        self.five = self.send(value, [(1, 3), (2, 0)])
        return value

    def parts(self):
        return self.mine, self.got, self.one, self.two, self.three, self.four, self.five


def wide(pieces, others):
    left, right = jnp.concatenate(pieces, axis=0), jnp.concatenate(others, axis=0)
    return jnp.einsum("ta,tb->ab", left, right, preferred_element_type=F32).astype(BF)


def scattered(blocks):
    parts, rows, columns = blocks.shape
    return lax.psum_scatter(blocks.reshape(parts * rows, columns), "dp", scatter_dimension=0, tiled=True).astype(F32)


def per_device(inputs, cotangent, g1, b1, g2, b2, w_qkv, b_qkv, w_out, b_out, w_up, b_up, w_down, b_down):
    section = lax.axis_index("section")
    owner = lax.axis_index("tensor")
    dp_at = lax.axis_index("dp")
    parts = lax.axis_size("dp")
    micro, seqs, length, width = inputs.shape
    rows = seqs * length
    local, hidden = w_out.shape[1], w_up.shape[2]
    flags = jnp.stack([section, owner, dp_at % 2, dp_at // 2]).astype(jnp.int32)
    table = jnp.asarray(rope_tables(length))
    vecs = (g1, b1, g2, b2, b_qkv[0], b_out, b_up, b_down)
    ws = (w_qkv[0].transpose(1, 0, 2), w_out[0], w_up[0], w_down[0])
    xs = inputs.reshape(micro, rows, width)
    cots = cotangent.reshape(micro, rows, width)
    lined = parts == 8
    chips = parts // 2

    *outs, pack = call_f(flags, xs, table, ws, vecs)
    arrivals = []
    for m in range(micro):
        whole = call_add(m, xs, outs[m], swap(outs[m]))
        arrivals.append(lax.ppermute(whole, "section", [(0, 1)]))
    kept, sources, backs = [], [], []
    for m in range(micro):
        dx, source, *saved = call_fb(m, flags, xs, cots, arrivals[m], table, pack, ws)
        whole = call_add(m, cots, dx, swap(dx))
        backs.append(lax.ppermute(whole, "section", [(1, 0)]))
        kept.append(dict(zip(SAVED, saved)))
        sources.append(source)
    a1, a2, mixed, active = ([kept[m][n] for m in range(micro)] for n in ("a1", "a2", "mixed", "g"))

    after = ()
    if lined:
        theirs, mine = call_blocks(
            functools.partial(down_kernel, chips, micro),
            flags,
            (cots, *backs, *active, *mixed),
            [HB] + [VM] * (3 * micro),
            (chips, hidden // parts + local // parts, width),
            2 * micro * rows * width * (hidden + local),
            [pltpu.VMEM(cots.shape, BF), pltpu.SemaphoreType.DMA],
        )
        line_down = Line(theirs, mine, dp_at)
        after = line_down.start()
    pieces = [backs, sources] + [[kept[m][n] for m in range(micro)] for n in NEEDED]
    grad, du, dqkv, own, other, up = call_b(flags, cots, table, pack, ws, pieces, after)
    got = swap(other)
    share = width // parts
    if lined:
        after = (line_down.relay(), line_down.two, line_down.three, line_down.four)
        slabs = hidden // local
        lines = own.shape[0]
        theirs, mine = call_blocks(
            functools.partial(rest_kernel, chips, micro),
            flags,
            (du, dqkv, own, got, *a1, *a2, *after),
            [VM] * (4 + 2 * micro) + [HB] * len(after),
            (chips, (slabs + 3) * share + lines, local),
            2 * micro * rows * width * (hidden + 3 * local),
        )
        line_rest = Line(theirs, mine, dp_at)
        part = call_o(mixed, active, pack, ws, (mine,))
        line_rest.start()
        line_rest.relay()
        after = (line_rest.one,)
        down_rows = hidden // parts
        outs = [(down_rows, width), (local // parts, width)]
        d_wdown, d_wout = call_final(final_down_kernel, flags, line_down.parts(), outs, after)
        section_out, input_grad = call_tail(part, swap(part), up, grad, swap(grad), sources, after)
        outs = [(share, hidden), (3, share, local), (5, local // parts), (3, local // parts), (1, down_rows)]
        d_wup, d_wqkv, d_vec, d_bqkv, d_bup = call_final(
            final_rest_kernel, flags, line_rest.parts(), outs, (), [pltpu.VMEM((lines, local), F32)]
        )
        d_wqkv = d_wqkv.transpose(1, 0, 2)
    else:
        d_wdown = wide(active, [up]).reshape(parts, -1, width)
        d_wout = wide(mixed, [up]).reshape(parts, -1, width)
        d_both = scattered(jnp.concatenate([d_wdown, d_wout], axis=1))
        d_wup = scattered(wide(a2, [du]).reshape(parts, -1, hidden))
        d_wqkv = wide(a1, [dqkv]).reshape(parts, share, 3, local).transpose(0, 2, 1, 3)
        lines = jnp.concatenate([own[: got.shape[0]] + got, own[got.shape[0] :]]).astype(BF)
        lines = jnp.broadcast_to(lines[None], (parts,) + lines.shape)
        last = scattered(jnp.concatenate([d_wqkv.reshape(parts, 3 * share, local), lines], axis=1))
        down_rows = hidden // parts
        d_wdown, d_wout = d_both[:down_rows], d_both[down_rows:]
        d_wqkv = last[: 3 * share].reshape(3, share, local).transpose(1, 0, 2)
        lines = last[3 * share :]
        d_vec = lax.dynamic_slice(lines, (0, dp_at * (local // parts)), (8, local // parts))
        d_vec, d_bqkv = d_vec[:5], d_vec[5:]
        up_lines = lines[8 : 8 + hidden // local].reshape(1, hidden)
        d_bup = lax.dynamic_slice_in_dim(up_lines, dp_at * down_rows, down_rows, 1)
        part = call_o(mixed, active, pack, ws)
        section_out, input_grad = call_tail(part, swap(part), up, grad, swap(grad), sources, ())
    return (
        section_out.reshape(1, micro, seqs, length, width),
        input_grad.reshape(1, micro, seqs, length, width),
        d_vec[0:1],
        d_vec[1:2],
        d_vec[2:3],
        d_vec[3:4],
        d_wqkv[None],
        d_bqkv[None],
        d_wout[None],
        d_vec[4:5],
        d_wup[None],
        d_bup,
        d_wdown[None],
        d_vec[4:5],
    )


def solution(mesh):
    return jax.shard_map(
        per_device,
        mesh=mesh,
        in_specs=(
            P(None, "dp", None, None),
            P(None, "dp", None, None),
            P("section", None),
            P("section", None),
            P("section", None),
            P("section", None),
            P("section", None, None, "tensor"),
            P("section", None, "tensor"),
            P("section", "tensor", None),
            P("section", None),
            P("section", None, "tensor"),
            P("section", "tensor"),
            P("section", "tensor", None),
            P("section", None),
        ),
        out_specs=(
            P("section", None, "dp", None, None),
            P("section", None, "dp", None, None),
            P("section", ("tensor", "dp")),
            P("section", ("tensor", "dp")),
            P("section", ("tensor", "dp")),
            P("section", ("tensor", "dp")),
            P("section", "dp", None, "tensor"),
            P("section", None, ("tensor", "dp")),
            P("section", ("tensor", "dp"), None),
            P("section", ("tensor", "dp")),
            P("section", "dp", "tensor"),
            P("section", ("tensor", "dp")),
            P("section", ("tensor", "dp"), None),
            P("section", ("tensor", "dp")),
        ),
        check_vma=False,
    )
```

```python
import functools
import math

import jax
import jax.numpy as jnp
import numpy as np
from jax import lax
from jax.experimental import pallas as pl
from jax.experimental.pallas import tpu as pltpu
from jax.sharding import PartitionSpec as P

HEAD = 64
ROT = 16
LANES = 128
PIECE = 512
AHEAD = 40
EPSILON = 1e-05
BF = jnp.bfloat16
F32 = jnp.float32


def rope_tables(length):
    half = ROT // 2
    inverse = np.exp(-math.log(10000.0) * np.arange(half, dtype=np.float32) * np.float32(2.0) / ROT)
    angle = np.arange(length, dtype=np.float32)[:, None] * inverse[None, :].astype(np.float32)
    cosine, sine = np.cos(angle), np.sin(angle)
    table = np.zeros((3, length, LANES), np.float32)
    table[0] = 1.0
    for head in range(LANES // HEAD):
        at = head * HEAD
        table[0, :, at : at + half] = cosine
        table[0, :, at + half : at + ROT] = cosine
        table[1, :, at : at + half] = -sine
        table[2, :, at + half : at + ROT] = sine
    return table


def dot(a, b):
    return jnp.dot(a, b, preferred_element_type=F32)


def dot_nt(a, b):
    return lax.dot_general(a, b, (((1,), (1,)), ((), ())), preferred_element_type=F32)


def dot_tn(a, b):
    return lax.dot_general(a, b, (((0,), (0,)), ((), ())), preferred_element_type=F32)


def roped(value, table, sign):
    half = ROT // 2
    ahead = pltpu.roll(value, LANES - half, 1) * table[1]
    behind = pltpu.roll(value, half, 1) * table[2]
    return value * table[0] + sign * (ahead + behind)


def head_pair(value):
    low = lax.broadcasted_iota(jnp.int32, value.shape, 1) < HEAD
    zero = jnp.zeros_like(value)
    return jnp.concatenate([jnp.where(low, value, zero), jnp.where(low, zero, value)], axis=0)


def pair_merge(value):
    rows = value.shape[0] // 2
    low = lax.broadcasted_iota(jnp.int32, (rows, LANES), 1) < HEAD
    return jnp.where(low, value[:rows], value[rows:])


def normal(block):
    width = block.shape[1]
    center = block - jnp.sum(block, axis=1, keepdims=True) * (1.0 / width)
    spread = jnp.sum(center * center, axis=1, keepdims=True) * (1.0 / width)
    scale = lax.rsqrt(spread + EPSILON)
    return center * scale, scale


def forward_part(x, vec, table, w, wait, put):
    rows, width = x.shape
    unit, unused = normal(x.astype(F32))
    first = (unit * vec["g1"] + vec["b1"]).astype(BF)
    second = (unit * vec["g2"] + vec["b2"]).astype(BF)
    put("a1", first)
    put("a2", second)
    bqkv = vec["bqkv"]
    raw = []
    for j in range(3):
        wait("wqkv", j)
        raw.append(dot(first, w["wqkv"][j]) + bqkv[j : j + 1])
    local = raw[0].shape[1]
    wait("table")
    length = table.shape[1]
    row = lax.broadcasted_iota(jnp.int32, (length, length), 0)
    keep = row >= lax.broadcasted_iota(jnp.int32, (length, length), 1)
    for start in range(0, rows, length):
        rs = slice(start, start + length)
        for p in range(local // LANES):
            sl = slice(p * LANES, (p + 1) * LANES)
            q = roped(raw[0][rs, sl], table, 1.0).astype(BF)
            k = roped(raw[1][rs, sl], table, 1.0).astype(BF)
            v = raw[2][rs, sl].astype(BF)
            put("q", q, sl)
            put("k", k, sl)
            put("v", v, sl)
            scores = dot_nt(q, head_pair(k)) * HEAD**-0.5
            prob = []
            for h in range(2):
                part = jnp.where(keep, scores[:, h * length : (h + 1) * length], -1e30)
                expo = jnp.exp(part - jnp.max(part, axis=1, keepdims=True))
                prob.append(expo * (1.0 / jnp.sum(expo, axis=1, keepdims=True)))
            prob = jnp.concatenate(prob, axis=1).astype(BF)
            put("prob", prob, slice(p * 2 * length, (p + 1) * 2 * length))
            put("mixed", dot(prob, head_pair(v)).astype(BF), sl, rs)
    hidden = w["wup"].shape[1]
    step = 256
    for c in range(0, hidden, step):
        sl = slice(c, c + step)
        wait("wup", c // PIECE)
        u = dot(second, w["wup"][:, sl]) + vec["bup"][:, sl]
        phi = 0.5 + 0.5 * lax.erf(u * (2.0**-0.5))
        put("g", (u * phi).astype(BF), sl)
        put("gp", lambda: phi + u * (jnp.exp(-0.5 * u * u) * (2.0 * math.pi) ** -0.5), sl)


def output_part(mixed, active, vec, w, wait):
    wait("wout")
    total = dot(mixed[...], w["wout"][...])
    wait("wdown")
    total = total + dot(active[...], w["wdown"][...])
    return (total + vec["extra"]).astype(BF)


def backward_part(dy, saved, table, w, wait, put):
    rows = dy.shape[0]
    hidden = w["wdown"].shape[0]
    step = 256
    wait("gp")
    for c in range(0, hidden, step):
        sl = slice(c, c + step)
        wait("wdown", c // PIECE)
        du = (dot_nt(dy, w["wdown"][sl, :]) * saved["gp"][:, sl].astype(F32)).astype(BF)
        put("du", du, sl)
    wait("wout")
    for name in ("table", "q", "k", "v", "prob"):
        wait(name)
    d_mixed = dot_nt(dy, w["wout"][...]).astype(BF)
    local = d_mixed.shape[1]
    length = table.shape[1]
    scale = HEAD**-0.5
    for start in range(0, rows, length):
        rs = slice(start, start + length)
        for p in range(local // LANES):
            sl = slice(p * LANES, (p + 1) * LANES)
            q, k, v = saved["q"][rs, sl], saved["k"][rs, sl], saved["v"][rs, sl]
            low = saved["prob"][rs, p * 2 * length : (p + 1) * 2 * length]
            prob = low.astype(F32)
            d_tile = d_mixed[rs, sl]
            d_prob = dot_nt(d_tile, head_pair(v))
            d_value = pair_merge(dot_tn(low, d_tile))
            d_scores = []
            for h in range(2):
                part = prob[:, h * length : (h + 1) * length]
                d_part = d_prob[:, h * length : (h + 1) * length]
                both = part * d_part
                d_scores.append(both - part * jnp.sum(both, axis=1, keepdims=True))
            d_scores = jnp.concatenate(d_scores, axis=1).astype(BF)
            d_query = dot(d_scores, head_pair(k)) * scale
            d_keys = pair_merge(dot_tn(d_scores, q)) * scale
            at = p * LANES
            put("dqkv", roped(d_query, table, -1.0).astype(BF), slice(at, at + LANES), rs)
            at += local
            put("dqkv", roped(d_keys, table, -1.0).astype(BF), slice(at, at + LANES), rs)
            at += local
            put("dqkv", d_value.astype(BF), slice(at, at + LANES), rs)


def norm_back(x, du, dqkv, local, vec, w, wait):
    wait("wup")
    d_second = dot_nt(du[...], w["wup"][...])
    for j in range(3):
        wait("wqkv", j)
    d_first = dot_nt(dqkv[:, :local], w["wqkv"][0])
    for j in range(1, 3):
        d_first = d_first + dot_nt(dqkv[:, j * local : (j + 1) * local], w["wqkv"][j])
    unit, scale = normal(x.astype(F32))
    e = d_first * vec["g1"] + d_second * vec["g2"]
    width = x.shape[1]
    mean = jnp.sum(e, axis=1, keepdims=True) * (1.0 / width)
    along = jnp.sum(e * unit, axis=1, keepdims=True) * (1.0 / width)
    dx = (e - mean - unit * along) * scale
    return dx.astype(BF), d_first, d_second, unit


WEIGHTS = ("wqkv", "wout", "wup", "wdown")
VECTORS = ("g1", "b1", "g2", "b2", "bqkv", "bout", "bup", "bdown")
NEEDED = ("q", "k", "v", "prob", "gp")
SAVED = ("a1", "a2", "q", "k", "v", "prob", "mixed", "g", "gp")


class Loads:
    def __init__(self, sems, ahead=64):
        self.sems, self.copies, self.queue, self.ahead = sems, {}, [], ahead
        self.started = self.waited = 0

    def start(self, name, source, target):
        copy = pltpu.make_async_copy(source, target, self.sems.at[len(self.queue)])
        self.copies.setdefault(name, {})[len(self.copies.get(name, {}))] = (len(self.queue), copy)
        self.queue.append(copy)
        self.pump(self.waited + self.ahead)

    def pump(self, until):
        while self.started < min(until, len(self.queue)):
            self.queue[self.started].start()
            self.started += 1

    def weight(self, name, hbm, w):
        source, target = hbm[name], w[name]
        if name == "wqkv":
            for j in range(3):
                self.start(name, source.at[j], target.at[j])
        elif name == "wout":
            self.start(name, source, target)
        else:
            for c in range(0, source.shape[0 if name == "wdown" else 1], PIECE):
                at = (pl.ds(c, PIECE), slice(None)) if name == "wdown" else (slice(None), pl.ds(c, PIECE))
                self.start(name, source.at[at], target.at[at])

    def wait(self, name, index=None):
        left = self.copies.get(name, {})
        for piece in [index] if index is not None else list(left):
            if piece in left:
                at, copy = left.pop(piece)
                self.pump(at + 1)
                copy.wait()
                self.waited += 1
                self.pump(self.waited + self.ahead)


def unpacked(pack, width, local, hidden):
    return {
        "g1": pack[0:1, :width],
        "b1": pack[1:2, :width],
        "g2": pack[2:3, :width],
        "b2": pack[3:4, :width],
        "extra": pack[4:5, :width],
        "bup": pack[5:6, :hidden],
        "bqkv": pack[6:9, :local],
    }


def f_kernel(micro, *refs):
    flag_ref, x_hbm, table_hbm = refs[:3]
    hbm = dict(zip(WEIGHTS, refs[3:7]))
    vec_hbm = dict(zip(VECTORS, refs[7:15]))
    out_refs, pack_ref = refs[15 : 15 + micro], refs[15 + micro]
    refs = refs[16 + micro :]
    w = dict(zip(WEIGHTS, refs[:4]))
    mixed, active, x_ref, table_ref, sems = refs[4:9]
    loads = Loads(sems)
    vec_ref = dict(zip(VECTORS, refs[9:]))
    rows, width = out_refs[0].shape
    for m in range(micro):
        loads.start("x", x_hbm.at[m], x_ref.at[pl.ds(m * rows, rows)])
    for name in VECTORS:
        loads.start(name, vec_hbm[name], vec_ref[name])
    loads.weight("wqkv", hbm, w)
    loads.start("table", table_hbm, table_ref)
    for name in ("wup", "wout", "wdown"):
        loads.weight(name, hbm, w)
    local, hidden = mixed.shape[1], active.shape[1]
    for name in VECTORS:
        loads.wait(name)
    for i, name in enumerate(("g1", "b1", "g2", "b2")):
        pack_ref[i : i + 1, :width] = vec_ref[name][...].astype(F32)
    extra = vec_ref["bout"][...].astype(F32) + vec_ref["bdown"][...].astype(F32)
    pack_ref[4:5, :width] = jnp.where(flag_ref[1] == 0, extra, jnp.zeros_like(extra))
    pack_ref[5:6, :hidden] = vec_ref["bup"][...].astype(F32)
    pack_ref[6:9, :local] = vec_ref["bqkv"][...].astype(F32)
    vec = unpacked(pack_ref, width, local, hidden)

    def put(name, value, sl=slice(None), rs=slice(None)):
        if name == "mixed":
            mixed[rs, sl] = value
        if name == "g":
            active[rs, sl] = value

    loads.wait("x")
    forward_part(x_ref[...], vec, table_ref, w, loads.wait, put)
    out = output_part(mixed, active, vec, w, loads.wait)
    for m in range(micro):
        out_refs[m][...] = out[m * rows : (m + 1) * rows]


def received(base, one, two):
    return (base.astype(F32) + (one.astype(F32) + two.astype(F32))).astype(BF)


def fb_kernel(at, *refs):
    flag_ref, x_hbm, dy_hbm, arrived_hbm, beside_hbm, table_hbm, pack_hbm = refs[:7]
    refs = refs[1:]
    hbm = dict(zip(WEIGHTS, refs[6:10]))
    names = ("dx", "source") + SAVED
    outs = dict(zip(names, refs[10 : 10 + len(names)]))
    refs = refs[10 + len(names) :]
    held = dict(zip(names, refs[: len(names)]))
    refs = refs[len(names) :]
    w = dict(zip(WEIGHTS, refs[:4]))
    du, dqkv, x_ref, dy_ref, arrived_ref, beside_ref, table_ref, pack_ref, sems, out_sems = refs[4:]
    loads, stores = Loads(sems), Loads(out_sems)
    loads.start("x", x_hbm.at[at], x_ref)
    loads.start("arrived", arrived_hbm, arrived_ref)
    loads.start("arrived", beside_hbm, beside_ref)
    loads.start("pack", pack_hbm, pack_ref)
    loads.weight("wqkv", hbm, w)
    loads.start("table", table_hbm, table_ref)
    loads.weight("wup", hbm, w)
    loads.start("dy", dy_hbm.at[at], dy_ref)
    loads.weight("wdown", hbm, w)
    loads.weight("wout", hbm, w)
    held_too = dict(held, du=du, dqkv=dqkv)

    def put(name, value, sl=slice(None), rs=slice(None)):
        ref = held_too[name]
        value = value() if callable(value) else value
        ref[rs, sl] = value.astype(ref.dtype)

    width, (local, hidden) = x_ref.shape[1], (dqkv.shape[1] // 3, du.shape[1])
    loads.wait("x")
    loads.wait("arrived")
    x = x_ref[...]
    x = jnp.where(flag_ref[0] == 0, x, received(x, arrived_ref[...], beside_ref[...]))
    loads.wait("pack")
    vec = unpacked(pack_ref, width, local, hidden)
    held["source"][...] = x
    forward_part(x, vec, table_ref, w, loads.wait, put)
    for name in ("source",) + SAVED:
        stores.start(name, held[name], outs[name])
    loads.wait("dy")
    backward_part(dy_ref[...], held, table_ref, w, loads.wait, put)
    held["dx"][...] = norm_back(x, du, dqkv, local, vec, w, loads.wait)[0]
    stores.start("dx", held["dx"], outs["dx"])
    for name in names:
        stores.wait(name)


def b_kernel(micro, *refs):
    flag_ref, dy_hbm, table_hbm, pack_hbm = refs[:4]
    hbm = dict(zip(WEIGHTS, refs[4:8]))
    names = ("arrived", "beside", "x") + NEEDED
    pieces = {n: refs[8 + i * micro : 8 + (i + 1) * micro] for i, n in enumerate(names)}
    refs = refs[-(6 + 4 + 3 + len(names) + 1) :]
    dx_ref, du, dqkv, own, other, dy_out = refs[:6]
    w = dict(zip(WEIGHTS, refs[6:10]))
    dy_ref, table_ref, pack_ref = refs[10:13]
    saved = dict(zip(names, refs[13:-1]))
    loads = Loads(refs[-1])
    rows = pieces["x"][0].shape[0]

    def both(name):
        for m in range(micro):
            loads.start(name, pieces[name][m], saved[name].at[pl.ds(m * rows, rows)])

    for m in range(micro):
        loads.start("dy", dy_hbm.at[m], dy_ref.at[pl.ds(m * rows, rows)])
    both("arrived")
    both("beside")
    both("gp")
    loads.weight("wdown", hbm, w)
    loads.weight("wout", hbm, w)
    loads.start("table", table_hbm, table_ref)
    for name in NEEDED[:4]:
        both(name)
    loads.weight("wup", hbm, w)
    loads.weight("wqkv", hbm, w)
    both("x")
    loads.start("pack", pack_hbm, pack_ref)
    kept = {"du": du, "dqkv": dqkv}

    def put(name, value, sl=slice(None), rs=slice(None)):
        kept[name][rs, sl] = value

    loads.wait("dy")
    loads.wait("arrived")
    loads.wait("beside")
    dy = dy_ref[...]
    dy = jnp.where(flag_ref[0] == 0, received(dy, saved["arrived"][...], saved["beside"][...]), dy)
    dy_out[...] = dy
    width, (local, hidden) = dy.shape[1], (dqkv.shape[1] // 3, du.shape[1])
    backward_part(dy, saved, table_ref, w, loads.wait, put)
    loads.wait("x")
    loads.wait("pack")
    vec = unpacked(pack_ref, width, local, hidden)
    dx, d_first, d_second, unit = norm_back(saved["x"][...], du, dqkv, local, vec, w, loads.wait)
    dx_ref[...] = dx
    own[...] = jnp.zeros_like(own)
    other[...] = jnp.zeros_like(other)
    low = flag_ref[1] == 0
    terms = (d_first * unit, d_first, d_second * unit, d_second, dy.astype(F32))
    for i, term in enumerate(terms):
        total = jnp.sum(term, axis=0, keepdims=True)
        front, back = total[:, :local], total[:, local:]
        own[i : i + 1] = jnp.where(low, front, back)
        if i < 4:
            other[i : i + 1] = jnp.where(low, back, front)
    line = 5
    for ref in (dqkv, du):
        for c in range(0, ref.shape[1], local):
            own[line : line + 1] = jnp.sum(ref[:, c : c + local].astype(F32), axis=0, keepdims=True)
            line += 1


def deal(theirs, mine, place, at, core, value, share):
    for z in range(value.shape[0] // (2 * share)):
        front = value[2 * z * share : (2 * z + 1) * share]
        back = value[(2 * z + 1) * share : (2 * z + 2) * share]
        theirs[place + z, at : at + share] = jnp.where(core == 0, back, front)
        mine[place + z, at : at + share] = jnp.where(core == 0, front, back)


def outer(pieces, sl, right):
    return dot_tn(jnp.concatenate([piece[:, sl] for piece in pieces], axis=0), right).astype(BF)


def down_kernel(chips, micro, *refs):
    flag_ref, dy_hbm = refs[:2]
    arrived, beside, active, mixed = (refs[2 + i * micro : 2 + (i + 1) * micro] for i in range(4))
    theirs, mine, dy_ref, sem = refs[2 + 4 * micro :]
    copy = pltpu.make_async_copy(dy_hbm, dy_ref, sem)
    copy.start()
    copy.wait()
    core = flag_ref[2]
    dy = [dy_ref[m] for m in range(micro)]
    for m in range(micro):
        dy[m] = jnp.where(flag_ref[0] == 0, received(dy[m], arrived[m][...], beside[m][...]), dy[m])
    dy = jnp.concatenate(dy, axis=0)
    hidden, local = active[0].shape[1], mixed[0].shape[1]
    share, step = hidden // (2 * chips), hidden // chips
    for z in range(chips):
        deal(theirs, mine, z, 0, core, outer(active, slice(z * step, (z + 1) * step), dy), share)
    deal(theirs, mine, 0, share, core, outer(mixed, slice(0, local), dy), local // (2 * chips))


def rest_kernel(chips, micro, *refs):
    flag_ref, du, dqkv, own, got = refs[:5]
    a1, a2, (theirs, mine) = refs[5 : 5 + micro], refs[5 + micro : 5 + 2 * micro], refs[-2:]
    width, local = a1[0].shape[1], own.shape[1]
    share = width // (2 * chips)
    step = width // 2
    at = 0
    for left, right in ((a2, du), (a1, dqkv)):
        for c in range(0, right.shape[1], local):
            columns = right[:, c : c + local]
            for j in range(2):
                value = outer(left, slice(j * step, (j + 1) * step), columns)
                deal(theirs, mine, j * chips // 2, at, flag_ref[2], value, share)
            at += share
    half = got.shape[0]
    lines = jnp.concatenate([own[:half] + got[...], own[half:]], axis=0).astype(BF)
    for z in range(chips):
        theirs[z, at:] = lines
        mine[z, at:] = lines


def split_kernel(which, *refs):
    flag_ref, mine, got = refs[:3]
    count = len(which)
    outs, (one, two, extra, sems) = refs[-4 - count : -4], refs[-4:]
    place = flag_ref[3]
    loads = Loads(sems)
    index = (
        jnp.where(place % 2 == 0, 3, 0),
        jnp.where(place == 1, 2, 1),
        jnp.where(place == 0, 2, 1),
        jnp.where(place == 0, 1, 2),
        jnp.where(place == 1, 3, 0),
    )
    for i, pick in enumerate(which):
        loads.start(2 * i, mine.at[index[pick]], one.at[i])
        loads.start(2 * i + 1, got.at[index[pick]], two.at[i])
        if pick == 4:
            loads.start("extra", refs[3], extra)
    for i, pick in enumerate(which):
        loads.wait(2 * i)
        loads.wait(2 * i + 1)
        value = one[i].astype(F32) + two[i].astype(F32)
        if pick == 4:
            loads.wait("extra")
            value = value + extra[...].astype(F32)
        outs[i][...] = value.astype(BF)


def arrived_sum(flag_ref, refs, scratch, sems):
    place = flag_ref[3]
    loads = Loads(sems)
    for i in range(2):
        loads.start(i, refs[i].at[place], scratch.at[i])
    edge = jnp.logical_or(place == 0, place == 3)
    for i in range(2):
        loads.wait(i)

    def total(at, rows):
        sl = slice(at, at + rows)
        value = refs[2][sl, :].astype(F32)
        value = jnp.where(edge, value, jnp.zeros_like(value))
        value = value + (scratch[0, sl, :].astype(F32) + scratch[1, sl, :].astype(F32))
        for ref in refs[3:7]:
            value = value + ref[sl, :].astype(F32)
        return value

    return total


def final_down_kernel(flag_ref, *refs):
    down_ref, out_ref, scratch, sems = refs[-4:]
    total = arrived_sum(flag_ref, refs[:7], scratch, sems)
    rows = down_ref.shape[0]
    down_ref[...] = total(0, rows)
    out_ref[...] = total(rows, out_ref.shape[0])


def final_rest_kernel(flag_ref, *refs):
    up_ref, qkv_ref, vec_ref, bqkv_ref, bup_ref, lines, scratch, sems = refs[-8:]
    total = arrived_sum(flag_ref, refs[:7], scratch, sems)
    share, local = qkv_ref.shape[1:]
    at = 0
    for c in range(0, up_ref.shape[1], local):
        up_ref[:, c : c + local] = total(at, share)
        at += share
    for t in range(3):
        qkv_ref[t] = total(at, share)
        at += share
    lines[...] = total(at, lines.shape[0])
    dp_at = 2 * flag_ref[3] + flag_ref[2]
    width = bqkv_ref.shape[1]
    front = pltpu.roll(lines[0:8], local - dp_at * width, 1)
    vec_ref[...] = front[0:5, :width]
    bqkv_ref[...] = front[5:8, :width]
    width = bup_ref.shape[1]
    per_line = local // width
    line = pltpu.roll(lines[8:16], local - (dp_at % per_line) * width, 1)
    row = dp_at // per_line
    picked = jnp.zeros((1, width), F32)
    for i in range(per_line and 8 // per_line):
        picked = jnp.where(row == i, line[i : i + 1, :width], picked)
    bup_ref[...] = picked


def tail_kernel(micro, *refs):
    part, other, up, grad, other_grad = refs[:5]
    sources = refs[5 : 5 + micro]
    out_ref, grad_ref = refs[-2:]
    rows = sources[0].shape[0]
    for m in range(micro):
        sl = slice(m * rows, (m + 1) * rows)
        both = part[sl].astype(F32) + other[sl].astype(F32)
        out_ref[sl] = (sources[m][...].astype(F32) + both).astype(BF)
    grad_ref[...] = up[...].astype(F32) + (grad[...].astype(F32) + other_grad[...].astype(F32))


def o_kernel(micro, *refs):
    mixed_refs, active_refs = refs[:micro], refs[micro : 2 * micro]
    pack_ref, wout_hbm, wdown_hbm = refs[2 * micro : 2 * micro + 3]
    out_ref, wout, wdown, mixed, active, sems = refs[-6:]
    loads = Loads(sems)
    hbm, w = {"wout": wout_hbm, "wdown": wdown_hbm}, {"wout": wout, "wdown": wdown}
    loads.weight("wout", hbm, w)
    loads.weight("wdown", hbm, w)
    rows = mixed_refs[0].shape[0]
    for m in range(micro):
        mixed[m * rows : (m + 1) * rows] = mixed_refs[m][...]
        active[m * rows : (m + 1) * rows] = active_refs[m][...]
    vec = unpacked(pack_ref, wout.shape[1], wout.shape[0], wdown.shape[0])
    out_ref[...] = output_part(mixed, active, vec, w, loads.wait)


VM = pl.BlockSpec(memory_space=pltpu.VMEM)
SM = pl.BlockSpec(memory_space=pltpu.SMEM)
HB = pl.BlockSpec(memory_space=pltpu.HBM)


def scratch_like(arrays):
    return [pltpu.VMEM(a.shape, a.dtype) for a in arrays]


def cost(ws, rows, passes):
    size = sum(math.prod(a.shape) for a in ws)
    return pl.CostEstimate(flops=2 * size * rows * passes, bytes_accessed=2 * size, transcendentals=0)


def params(mib):
    return pltpu.CompilerParams(vmem_limit_bytes=mib * 2**20)


def call_f(flags, xs, table, ws, vecs):
    micro, rows, width = xs.shape
    local, hidden = ws[1].shape[0], ws[3].shape[0]
    total = micro * rows
    scratch = scratch_like(ws) + [
        pltpu.VMEM((total, local), BF),
        pltpu.VMEM((total, hidden), BF),
        pltpu.VMEM((total, width), BF),
        pltpu.VMEM(table.shape, F32),
        pltpu.SemaphoreType.DMA((24,)),
    ]
    out = [jax.ShapeDtypeStruct((rows, width), BF)] * micro + [jax.ShapeDtypeStruct((16, hidden), F32)]
    return pl.pallas_call(
        functools.partial(f_kernel, micro),
        out_shape=out,
        in_specs=[SM] + [HB] * 14,
        out_specs=[VM] * len(out),
        scratch_shapes=scratch + scratch_like(vecs),
        compiler_params=params(54),
        cost_estimate=cost(ws, total, 1),
    )(flags, xs, table, *ws, *vecs)


def call_fb(at, flags, xs, cots, arrived, table, pack, ws):
    rows, width = xs.shape[1:]
    local, hidden = ws[1].shape[0], ws[3].shape[0]
    shape = jax.ShapeDtypeStruct
    outs = [shape((rows, width), BF)] * 4
    outs += [shape((rows, local), BF)] * 3
    outs += [
        shape((rows, 2 * rows * local // LANES), BF),
        shape((rows, local), BF),
        shape((rows, hidden), BF),
        shape((rows, hidden), BF),
    ]
    return pl.pallas_call(
        functools.partial(fb_kernel, at),
        out_shape=outs,
        in_specs=[SM] + [HB] * 10,
        out_specs=[HB] * len(outs),
        scratch_shapes=scratch_like(outs)
        + scratch_like(ws)
        + [
            pltpu.VMEM((rows, hidden), BF),
            pltpu.VMEM((rows, 3 * local), BF),
            pltpu.VMEM((rows, width), BF),
            pltpu.VMEM((rows, width), BF),
            pltpu.VMEM((rows, width), BF),
            pltpu.VMEM((rows, width), BF),
            pltpu.VMEM(table.shape, F32),
            pltpu.VMEM(pack.shape, F32),
            pltpu.SemaphoreType.DMA((24,)),
            pltpu.SemaphoreType.DMA((len(outs),)),
        ],
        compiler_params=params(54),
        cost_estimate=cost(ws, rows, 2),
    )(flags, xs, cots, *arrived, table, pack, *ws)


def call_b(flags, cots, table, pack, ws, pieces, after):
    micro, rows, width = cots.shape
    local, hidden = ws[1].shape[0], ws[3].shape[0]
    shape = jax.ShapeDtypeStruct
    total = micro * rows
    outs = [
        shape((total, width), BF),
        shape((total, hidden), BF),
        shape((total, 3 * local), BF),
        shape((16, local), F32),
        shape((8, local), F32),
        shape((total, width), BF),
    ]
    flat = [array for group in pieces for array in group]
    return pl.pallas_call(
        functools.partial(b_kernel, micro),
        out_shape=outs,
        in_specs=[SM] + [HB] * (7 + len(flat) + len(after)),
        out_specs=[VM] * len(outs),
        scratch_shapes=scratch_like(ws)
        + [pltpu.VMEM((total, width), BF)]
        + scratch_like([table, pack])
        + [pltpu.VMEM((total, group[0].shape[1]), group[0].dtype) for group in pieces]
        + [pltpu.SemaphoreType.DMA((32,))],
        compiler_params=params(54),
        cost_estimate=cost(ws, total, 1),
    )(flags, cots, table, pack, *ws, *flat, *after)


def call_blocks(kernel, flags, operands, specs, block, flops, scratch=()):
    outs = [jax.ShapeDtypeStruct(block, BF)] * 2
    return pl.pallas_call(
        kernel,
        out_shape=outs,
        in_specs=[SM] + specs,
        out_specs=[VM] * 2,
        scratch_shapes=list(scratch),
        compiler_params=params(54),
        cost_estimate=pl.CostEstimate(flops=flops, bytes_accessed=4 * math.prod(block), transcendentals=0),
    )(flags, *operands)


def call_split(flags, mine, got, which, after):
    block, count = mine.shape[1:], len(which)
    return pl.pallas_call(
        functools.partial(split_kernel, which),
        out_shape=[jax.ShapeDtypeStruct(block, BF)] * count,
        in_specs=[SM] + [HB] * (2 + len(after)),
        out_specs=[VM] * count,
        scratch_shapes=[pltpu.VMEM((count,) + block, BF)] * 2
        + [pltpu.VMEM(block, BF), pltpu.SemaphoreType.DMA((8,))],
        compiler_params=params(16),
    )(flags, mine, got, *after)


def call_final(kernel, flags, parts, outs, after, scratch=()):
    return pl.pallas_call(
        kernel,
        out_shape=[jax.ShapeDtypeStruct(shape, F32) for shape in outs],
        in_specs=[SM, HB, HB] + [VM] * 5 + [HB] * len(after),
        out_specs=[VM] * len(outs),
        scratch_shapes=list(scratch)
        + [pltpu.VMEM((2,) + parts[2].shape, BF), pltpu.SemaphoreType.DMA((2,))],
        compiler_params=params(16),
    )(flags, *parts, *after)


def call_tail(part, other, up, grad, other_grad, sources, after):
    micro = len(sources)
    return pl.pallas_call(
        functools.partial(tail_kernel, micro),
        out_shape=[jax.ShapeDtypeStruct(part.shape, BF), jax.ShapeDtypeStruct(part.shape, F32)],
        in_specs=[VM] * (5 + micro) + [HB] * len(after),
        out_specs=[VM] * 2,
        compiler_params=params(16),
    )(part, other, up, grad, other_grad, *sources, *after)


def call_o(mixed, active, pack, ws, after=()):
    micro, (rows, local) = len(mixed), mixed[0].shape
    hidden, width = ws[3].shape
    total = micro * rows
    return pl.pallas_call(
        functools.partial(o_kernel, micro),
        out_shape=jax.ShapeDtypeStruct((total, width), BF),
        in_specs=[VM] * (2 * micro + 1) + [HB] * (2 + len(after)),
        out_specs=VM,
        scratch_shapes=[
            pltpu.VMEM((local, width), BF),
            pltpu.VMEM((hidden, width), BF),
            pltpu.VMEM((total, local), BF),
            pltpu.VMEM((total, hidden), BF),
            pltpu.SemaphoreType.DMA((8,)),
        ],
        compiler_params=params(54),
        cost_estimate=cost((ws[1], ws[3]), total, 1),
    )(*mixed, *active, pack, ws[1], ws[3], *after)


def handed(value, source, target):
    straight = lax.ppermute(value, "section", [(source, target)])
    across = [(2 * source, 2 * target + 1), (2 * source + 1, 2 * target)]
    return straight, lax.ppermute(value, ("section", "tensor"), across)


def swap(value):
    return lax.ppermute(value, "tensor", [(0, 1), (1, 0)])


ONE = [(0, 1), (1, 0), (2, 3), (3, 2)]
TWO = [(0, 1), (3, 2)]
THREE = [(1, 2), (2, 1)]
FOUR = [(0, 2), (3, 1)]
FIVE = [(1, 3), (2, 0)]


class Line:
    def __init__(self, theirs, mine, at):
        self.place = at // 2
        self.mine = mine
        self.got = lax.ppermute(theirs, "dp", [(i, i ^ 1) for i in range(8)])

    def block(self, index):
        one = lax.dynamic_index_in_dim(self.mine, index, 0, keepdims=False)
        two = lax.dynamic_index_in_dim(self.got, index, 0, keepdims=False)
        return one.astype(F32) + two.astype(F32)

    def send(self, value, pairs):
        return lax.ppermute(value, "dp", [(2 * a + c, 2 * b + c) for a, b in pairs for c in range(2)])

    def start(self):
        place = self.place
        values = [
            self.block(index).astype(BF)
            for index in (
                jnp.where(place % 2 == 0, 3, 0),
                jnp.where(place == 1, 2, 1),
                jnp.where(place == 0, 2, 1),
                jnp.where(place == 0, 1, 2),
            )
        ]
        self.one = self.send(values[0], ONE)
        self.three = self.send(values[1], THREE)
        self.four = self.send(values[2], FOUR)
        self.two = self.send(values[3], TWO)
        return tuple(values)

    def relay(self):
        value = (self.block(jnp.where(self.place == 1, 3, 0)) + self.one.astype(F32)).astype(BF)
        self.five = self.send(value, FIVE)
        return value

    def staged(self, flags):
        first = call_split(flags, self.mine, self.got, (0, 1), ())
        self.one = self.send(first[0], ONE)
        self.three = self.send(first[1], THREE)
        rest = call_split(flags, self.mine, self.got, (4, 2, 3), (self.one, self.three))
        self.five = self.send(rest[0], FIVE)
        self.four = self.send(rest[1], FOUR)
        self.two = self.send(rest[2], TWO)

    def parts(self):
        return self.mine, self.got, self.one, self.two, self.three, self.four, self.five


def wide(pieces, others):
    left, right = jnp.concatenate(pieces, axis=0), jnp.concatenate(others, axis=0)
    return jnp.einsum("ta,tb->ab", left, right, preferred_element_type=F32).astype(BF)


def scattered(blocks):
    parts, rows, columns = blocks.shape
    return lax.psum_scatter(blocks.reshape(parts * rows, columns), "dp", scatter_dimension=0, tiled=True).astype(F32)


def per_device(inputs, cotangent, g1, b1, g2, b2, w_qkv, b_qkv, w_out, b_out, w_up, b_up, w_down, b_down):
    section = lax.axis_index("section")
    owner = lax.axis_index("tensor")
    dp_at = lax.axis_index("dp")
    parts = lax.axis_size("dp")
    micro, seqs, length, width = inputs.shape
    rows = seqs * length
    local, hidden = w_out.shape[1], w_up.shape[2]
    flags = jnp.stack([section, owner, dp_at % 2, dp_at // 2]).astype(jnp.int32)
    table = jnp.asarray(rope_tables(length))
    vecs = (g1, b1, g2, b2, b_qkv[0], b_out, b_up, b_down)
    ws = (w_qkv[0].transpose(1, 0, 2), w_out[0], w_up[0], w_down[0])
    xs = inputs.reshape(micro, rows, width)
    cots = cotangent.reshape(micro, rows, width)
    lined = parts == 8
    chips = parts // 2

    *outs, pack = call_f(flags, xs, table, ws, vecs)
    arrivals = []
    for m in range(micro):
        arrivals.append(handed(outs[m], 0, 1))
    kept, sources, backs = [], [], []
    for m in range(micro):
        dx, source, *saved = call_fb(m, flags, xs, cots, arrivals[m], table, pack, ws)
        backs.append(handed(dx, 1, 0))
        kept.append(dict(zip(SAVED, saved)))
        sources.append(source)
    a1, a2, mixed, active = ([kept[m][n] for m in range(micro)] for n in ("a1", "a2", "mixed", "g"))

    after = ()
    arrived, beside = ([back[i] for back in backs] for i in range(2))
    if lined:
        theirs, mine = call_blocks(
            functools.partial(down_kernel, chips, micro),
            flags,
            (cots, *arrived, *beside, *active, *mixed),
            [HB] + [VM] * (4 * micro),
            (chips, hidden // parts + local // parts, width),
            2 * micro * rows * width * (hidden + local),
            [pltpu.VMEM(cots.shape, BF), pltpu.SemaphoreType.DMA],
        )
        line_down = Line(theirs, mine, dp_at)
        after = line_down.start()
    pieces = [arrived, beside, sources] + [[kept[m][n] for m in range(micro)] for n in NEEDED]
    grad, du, dqkv, own, other, up = call_b(flags, cots, table, pack, ws, pieces, after)
    got = swap(other)
    share = width // parts
    if lined:
        after = (line_down.relay(), line_down.two, line_down.three, line_down.four)
        slabs = hidden // local
        lines = own.shape[0]
        theirs, mine = call_blocks(
            functools.partial(rest_kernel, chips, micro),
            flags,
            (du, dqkv, own, got, *a1, *a2, *after),
            [VM] * (4 + 2 * micro) + [HB] * len(after),
            (chips, (slabs + 3) * share + lines, local),
            2 * micro * rows * width * (hidden + 3 * local),
        )
        line_rest = Line(theirs, mine, dp_at)
        part = call_o(mixed, active, pack, ws, (mine,))
        line_rest.staged(flags)
        after = (line_rest.one,)
        down_rows = hidden // parts
        outs = [(down_rows, width), (local // parts, width)]
        d_wdown, d_wout = call_final(final_down_kernel, flags, line_down.parts(), outs, after)
        section_out, input_grad = call_tail(part, swap(part), up, grad, swap(grad), sources, after)
        outs = [(share, hidden), (3, share, local), (5, local // parts), (3, local // parts), (1, down_rows)]
        d_wup, d_wqkv, d_vec, d_bqkv, d_bup = call_final(
            final_rest_kernel, flags, line_rest.parts(), outs, (), [pltpu.VMEM((lines, local), F32)]
        )
        d_wqkv = d_wqkv.transpose(1, 0, 2)
    else:
        d_wdown = wide(active, [up]).reshape(parts, -1, width)
        d_wout = wide(mixed, [up]).reshape(parts, -1, width)
        d_both = scattered(jnp.concatenate([d_wdown, d_wout], axis=1))
        d_wup = scattered(wide(a2, [du]).reshape(parts, -1, hidden))
        d_wqkv = wide(a1, [dqkv]).reshape(parts, share, 3, local).transpose(0, 2, 1, 3)
        lines = jnp.concatenate([own[: got.shape[0]] + got, own[got.shape[0] :]]).astype(BF)
        lines = jnp.broadcast_to(lines[None], (parts,) + lines.shape)
        last = scattered(jnp.concatenate([d_wqkv.reshape(parts, 3 * share, local), lines], axis=1))
        down_rows = hidden // parts
        d_wdown, d_wout = d_both[:down_rows], d_both[down_rows:]
        d_wqkv = last[: 3 * share].reshape(3, share, local).transpose(1, 0, 2)
        lines = last[3 * share :]
        d_vec = lax.dynamic_slice(lines, (0, dp_at * (local // parts)), (8, local // parts))
        d_vec, d_bqkv = d_vec[:5], d_vec[5:]
        up_lines = lines[8 : 8 + hidden // local].reshape(1, hidden)
        d_bup = lax.dynamic_slice_in_dim(up_lines, dp_at * down_rows, down_rows, 1)
        part = call_o(mixed, active, pack, ws)
        section_out, input_grad = call_tail(part, swap(part), up, grad, swap(grad), sources, ())
    return (
        section_out.reshape(1, micro, seqs, length, width),
        input_grad.reshape(1, micro, seqs, length, width),
        d_vec[0:1],
        d_vec[1:2],
        d_vec[2:3],
        d_vec[3:4],
        d_wqkv[None],
        d_bqkv[None],
        d_wout[None],
        d_vec[4:5],
        d_wup[None],
        d_bup,
        d_wdown[None],
        d_vec[4:5],
    )


def solution(mesh):
    return jax.shard_map(
        per_device,
        mesh=mesh,
        in_specs=(
            P(None, "dp", None, None),
            P(None, "dp", None, None),
            P("section", None),
            P("section", None),
            P("section", None),
            P("section", None),
            P("section", None, None, "tensor"),
            P("section", None, "tensor"),
            P("section", "tensor", None),
            P("section", None),
            P("section", None, "tensor"),
            P("section", "tensor"),
            P("section", "tensor", None),
            P("section", None),
        ),
        out_specs=(
            P("section", None, "dp", None, None),
            P("section", None, "dp", None, None),
            P("section", ("tensor", "dp")),
            P("section", ("tensor", "dp")),
            P("section", ("tensor", "dp")),
            P("section", ("tensor", "dp")),
            P("section", "dp", None, "tensor"),
            P("section", None, ("tensor", "dp")),
            P("section", ("tensor", "dp"), None),
            P("section", ("tensor", "dp")),
            P("section", "dp", "tensor"),
            P("section", ("tensor", "dp")),
            P("section", ("tensor", "dp"), None),
            P("section", ("tensor", "dp")),
        ),
        check_vma=False,
    )
```

```python
import functools
import math

import jax
import jax.numpy as jnp
import numpy as np
from jax import lax
from jax.experimental import pallas as pl
from jax.experimental.pallas import tpu as pltpu
from jax.sharding import PartitionSpec as P

HEAD = 64
ROT = 16
LANES = 128
PIECE = 512
AHEAD = 40
EPSILON = 1e-05
BF = jnp.bfloat16
F32 = jnp.float32


def rope_tables(length):
    half = ROT // 2
    inverse = np.exp(-math.log(10000.0) * np.arange(half, dtype=np.float32) * np.float32(2.0) / ROT)
    angle = np.arange(length, dtype=np.float32)[:, None] * inverse[None, :].astype(np.float32)
    cosine, sine = np.cos(angle), np.sin(angle)
    table = np.zeros((3, length, LANES), np.float32)
    table[0] = 1.0
    for head in range(LANES // HEAD):
        at = head * HEAD
        table[0, :, at : at + half] = cosine
        table[0, :, at + half : at + ROT] = cosine
        table[1, :, at : at + half] = -sine
        table[2, :, at + half : at + ROT] = sine
    return table


def dot(a, b):
    return jnp.dot(a, b, preferred_element_type=F32)


def dot_nt(a, b):
    return lax.dot_general(a, b, (((1,), (1,)), ((), ())), preferred_element_type=F32)


def dot_tn(a, b):
    return lax.dot_general(a, b, (((0,), (0,)), ((), ())), preferred_element_type=F32)


def roped(value, table, sign):
    half = ROT // 2
    ahead = pltpu.roll(value, LANES - half, 1) * table[1]
    behind = pltpu.roll(value, half, 1) * table[2]
    return value * table[0] + sign * (ahead + behind)


def head_pair(value):
    low = lax.broadcasted_iota(jnp.int32, value.shape, 1) < HEAD
    zero = jnp.zeros_like(value)
    return jnp.concatenate([jnp.where(low, value, zero), jnp.where(low, zero, value)], axis=0)


def pair_merge(value):
    rows = value.shape[0] // 2
    low = lax.broadcasted_iota(jnp.int32, (rows, LANES), 1) < HEAD
    return jnp.where(low, value[:rows], value[rows:])


def normal(block):
    width = block.shape[1]
    center = block - jnp.sum(block, axis=1, keepdims=True) * (1.0 / width)
    spread = jnp.sum(center * center, axis=1, keepdims=True) * (1.0 / width)
    scale = lax.rsqrt(spread + EPSILON)
    return center * scale, scale


def forward_part(x, vec, table, w, wait, put):
    rows, width = x.shape
    unit, unused = normal(x.astype(F32))
    first = (unit * vec["g1"] + vec["b1"]).astype(BF)
    second = (unit * vec["g2"] + vec["b2"]).astype(BF)
    put("a1", first)
    put("a2", second)
    bqkv = vec["bqkv"]
    raw = []
    for j in range(3):
        wait("wqkv", j)
        raw.append(dot(first, w["wqkv"][j]) + bqkv[j : j + 1])
    local = raw[0].shape[1]
    wait("table")
    length = table.shape[1]
    row = lax.broadcasted_iota(jnp.int32, (length, length), 0)
    keep = row >= lax.broadcasted_iota(jnp.int32, (length, length), 1)
    for start in range(0, rows, length):
        rs = slice(start, start + length)
        for p in range(local // LANES):
            sl = slice(p * LANES, (p + 1) * LANES)
            q = roped(raw[0][rs, sl], table, 1.0).astype(BF)
            k = roped(raw[1][rs, sl], table, 1.0).astype(BF)
            v = raw[2][rs, sl].astype(BF)
            put("q", q, sl)
            put("k", k, sl)
            put("v", v, sl)
            scores = dot_nt(q, head_pair(k)) * HEAD**-0.5
            prob = []
            for h in range(2):
                part = jnp.where(keep, scores[:, h * length : (h + 1) * length], -1e30)
                expo = jnp.exp(part - jnp.max(part, axis=1, keepdims=True))
                prob.append(expo * (1.0 / jnp.sum(expo, axis=1, keepdims=True)))
            prob = jnp.concatenate(prob, axis=1).astype(BF)
            put("prob", prob, slice(p * 2 * length, (p + 1) * 2 * length))
            put("mixed", dot(prob, head_pair(v)).astype(BF), sl, rs)
    hidden = w["wup"].shape[1]
    step = 256
    for c in range(0, hidden, step):
        sl = slice(c, c + step)
        wait("wup", c // PIECE)
        u = dot(second, w["wup"][:, sl]) + vec["bup"][:, sl]
        phi = 0.5 + 0.5 * lax.erf(u * (2.0**-0.5))
        put("g", (u * phi).astype(BF), sl)
        put("gp", lambda: phi + u * (jnp.exp(-0.5 * u * u) * (2.0 * math.pi) ** -0.5), sl)


def output_part(mixed, active, vec, w, wait):
    wait("wout")
    total = dot(mixed[...], w["wout"][...])
    wait("wdown")
    total = total + dot(active[...], w["wdown"][...])
    return (total + vec["extra"]).astype(BF)


def backward_part(dy, saved, table, w, wait, put):
    rows = dy.shape[0]
    hidden = w["wdown"].shape[0]
    step = 256
    wait("gp")
    for c in range(0, hidden, step):
        sl = slice(c, c + step)
        wait("wdown", c // PIECE)
        du = (dot_nt(dy, w["wdown"][sl, :]) * saved["gp"][:, sl].astype(F32)).astype(BF)
        put("du", du, sl)
    wait("wout")
    for name in ("table", "q", "k", "v", "prob"):
        wait(name)
    d_mixed = dot_nt(dy, w["wout"][...]).astype(BF)
    local = d_mixed.shape[1]
    length = table.shape[1]
    scale = HEAD**-0.5
    for start in range(0, rows, length):
        rs = slice(start, start + length)
        for p in range(local // LANES):
            sl = slice(p * LANES, (p + 1) * LANES)
            q, k, v = saved["q"][rs, sl], saved["k"][rs, sl], saved["v"][rs, sl]
            low = saved["prob"][rs, p * 2 * length : (p + 1) * 2 * length]
            prob = low.astype(F32)
            d_tile = d_mixed[rs, sl]
            d_prob = dot_nt(d_tile, head_pair(v))
            d_value = pair_merge(dot_tn(low, d_tile))
            d_scores = []
            for h in range(2):
                part = prob[:, h * length : (h + 1) * length]
                d_part = d_prob[:, h * length : (h + 1) * length]
                both = part * d_part
                d_scores.append(both - part * jnp.sum(both, axis=1, keepdims=True))
            d_scores = jnp.concatenate(d_scores, axis=1).astype(BF)
            d_query = dot(d_scores, head_pair(k)) * scale
            d_keys = pair_merge(dot_tn(d_scores, q)) * scale
            at = p * LANES
            put("dqkv", roped(d_query, table, -1.0).astype(BF), slice(at, at + LANES), rs)
            at += local
            put("dqkv", roped(d_keys, table, -1.0).astype(BF), slice(at, at + LANES), rs)
            at += local
            put("dqkv", d_value.astype(BF), slice(at, at + LANES), rs)


def norm_back(x, du, dqkv, local, vec, w, wait):
    wait("wup")
    d_second = dot_nt(du[...], w["wup"][...])
    for j in range(3):
        wait("wqkv", j)
    d_first = dot_nt(dqkv[:, :local], w["wqkv"][0])
    for j in range(1, 3):
        d_first = d_first + dot_nt(dqkv[:, j * local : (j + 1) * local], w["wqkv"][j])
    unit, scale = normal(x.astype(F32))
    e = d_first * vec["g1"] + d_second * vec["g2"]
    width = x.shape[1]
    mean = jnp.sum(e, axis=1, keepdims=True) * (1.0 / width)
    along = jnp.sum(e * unit, axis=1, keepdims=True) * (1.0 / width)
    dx = (e - mean - unit * along) * scale
    return dx.astype(BF), d_first, d_second, unit


WEIGHTS = ("wqkv", "wout", "wup", "wdown")
VECTORS = ("g1", "b1", "g2", "b2", "bqkv", "bout", "bup", "bdown")
NEEDED = ("q", "k", "v", "prob", "gp")
SAVED = ("a1", "a2", "q", "k", "v", "prob", "mixed", "g", "gp")


class Loads:
    def __init__(self, sems, ahead=64):
        self.sems, self.copies, self.queue, self.ahead = sems, {}, [], ahead
        self.started = self.waited = 0

    def start(self, name, source, target):
        copy = pltpu.make_async_copy(source, target, self.sems.at[len(self.queue)])
        self.copies.setdefault(name, {})[len(self.copies.get(name, {}))] = (len(self.queue), copy)
        self.queue.append(copy)
        self.pump(self.waited + self.ahead)

    def pump(self, until):
        while self.started < min(until, len(self.queue)):
            self.queue[self.started].start()
            self.started += 1

    def weight(self, name, hbm, w):
        source, target = hbm[name], w[name]
        if name == "wqkv":
            for j in range(3):
                self.start(name, source.at[j], target.at[j])
        elif name == "wout":
            self.start(name, source, target)
        else:
            for c in range(0, source.shape[0 if name == "wdown" else 1], PIECE):
                at = (pl.ds(c, PIECE), slice(None)) if name == "wdown" else (slice(None), pl.ds(c, PIECE))
                self.start(name, source.at[at], target.at[at])

    def wait(self, name, index=None):
        left = self.copies.get(name, {})
        for piece in [index] if index is not None else list(left):
            if piece in left:
                at, copy = left.pop(piece)
                self.pump(at + 1)
                copy.wait()
                self.waited += 1
                self.pump(self.waited + self.ahead)


def unpacked(pack, width, local, hidden):
    return {
        "g1": pack[0:1, :width],
        "b1": pack[1:2, :width],
        "g2": pack[2:3, :width],
        "b2": pack[3:4, :width],
        "extra": pack[4:5, :width],
        "bup": pack[5:6, :hidden],
        "bqkv": pack[6:9, :local],
    }


def f_kernel(micro, *refs):
    flag_ref, x_hbm, table_hbm = refs[:3]
    hbm = dict(zip(WEIGHTS, refs[3:7]))
    vec_hbm = dict(zip(VECTORS, refs[7:15]))
    out_refs, pack_ref = refs[15 : 15 + micro], refs[15 + micro]
    refs = refs[16 + micro :]
    w = dict(zip(WEIGHTS, refs[:4]))
    mixed, active, x_ref, table_ref, sems = refs[4:9]
    loads = Loads(sems)
    vec_ref = dict(zip(VECTORS, refs[9:]))
    rows, width = out_refs[0].shape
    for m in range(micro):
        loads.start("x", x_hbm.at[m], x_ref.at[pl.ds(m * rows, rows)])
    for name in VECTORS:
        loads.start(name, vec_hbm[name], vec_ref[name])
    loads.weight("wqkv", hbm, w)
    loads.start("table", table_hbm, table_ref)
    for name in ("wup", "wout", "wdown"):
        loads.weight(name, hbm, w)
    local, hidden = mixed.shape[1], active.shape[1]
    for name in VECTORS:
        loads.wait(name)
    for i, name in enumerate(("g1", "b1", "g2", "b2")):
        pack_ref[i : i + 1, :width] = vec_ref[name][...].astype(F32)
    extra = vec_ref["bout"][...].astype(F32) + vec_ref["bdown"][...].astype(F32)
    pack_ref[4:5, :width] = jnp.where(flag_ref[1] == 0, extra, jnp.zeros_like(extra))
    pack_ref[5:6, :hidden] = vec_ref["bup"][...].astype(F32)
    pack_ref[6:9, :local] = vec_ref["bqkv"][...].astype(F32)
    vec = unpacked(pack_ref, width, local, hidden)

    def put(name, value, sl=slice(None), rs=slice(None)):
        if name == "mixed":
            mixed[rs, sl] = value
        if name == "g":
            active[rs, sl] = value

    loads.wait("x")
    forward_part(x_ref[...], vec, table_ref, w, loads.wait, put)
    out = output_part(mixed, active, vec, w, loads.wait)
    for m in range(micro):
        out_refs[m][...] = out[m * rows : (m + 1) * rows]


def received(base, one, two):
    return (base.astype(F32) + (one.astype(F32) + two.astype(F32))).astype(BF)


def fb_kernel(at, *refs):
    flag_ref, x_hbm, dy_hbm, arrived_hbm, beside_hbm, table_hbm, pack_hbm = refs[:7]
    refs = refs[1:]
    hbm = dict(zip(WEIGHTS, refs[6:10]))
    names = ("dx", "source") + SAVED
    outs = dict(zip(names, refs[10 : 10 + len(names)]))
    refs = refs[10 + len(names) :]
    held = dict(zip(names, refs[: len(names)]))
    refs = refs[len(names) :]
    w = dict(zip(WEIGHTS, refs[:4]))
    du, dqkv, x_ref, dy_ref, arrived_ref, beside_ref, table_ref, pack_ref, sems, out_sems = refs[4:]
    loads, stores = Loads(sems), Loads(out_sems)
    loads.start("x", x_hbm.at[at], x_ref)
    loads.start("arrived", arrived_hbm, arrived_ref)
    loads.start("arrived", beside_hbm, beside_ref)
    loads.start("pack", pack_hbm, pack_ref)
    loads.weight("wqkv", hbm, w)
    loads.start("table", table_hbm, table_ref)
    loads.weight("wup", hbm, w)
    loads.start("dy", dy_hbm.at[at], dy_ref)
    loads.weight("wdown", hbm, w)
    loads.weight("wout", hbm, w)
    held_too = dict(held, du=du, dqkv=dqkv)

    def put(name, value, sl=slice(None), rs=slice(None)):
        ref = held_too[name]
        value = value() if callable(value) else value
        ref[rs, sl] = value.astype(ref.dtype)

    width, (local, hidden) = x_ref.shape[1], (dqkv.shape[1] // 3, du.shape[1])
    loads.wait("x")
    loads.wait("arrived")
    x = x_ref[...]
    x = jnp.where(flag_ref[0] == 0, x, received(x, arrived_ref[...], beside_ref[...]))
    loads.wait("pack")
    vec = unpacked(pack_ref, width, local, hidden)
    held["source"][...] = x
    forward_part(x, vec, table_ref, w, loads.wait, put)
    for name in ("source",) + SAVED:
        stores.start(name, held[name], outs[name])
    loads.wait("dy")
    backward_part(dy_ref[...], held, table_ref, w, loads.wait, put)
    held["dx"][...] = norm_back(x, du, dqkv, local, vec, w, loads.wait)[0]
    stores.start("dx", held["dx"], outs["dx"])
    for name in names:
        stores.wait(name)


def b_kernel(micro, *refs):
    flag_ref, dy_hbm, table_hbm, pack_hbm = refs[:4]
    hbm = dict(zip(WEIGHTS, refs[4:8]))
    names = ("arrived", "beside", "x") + NEEDED
    pieces = {n: refs[8 + i * micro : 8 + (i + 1) * micro] for i, n in enumerate(names)}
    refs = refs[-(6 + 4 + 3 + len(names) + 1) :]
    dx_ref, du, dqkv, own, other, dy_out = refs[:6]
    w = dict(zip(WEIGHTS, refs[6:10]))
    dy_ref, table_ref, pack_ref = refs[10:13]
    saved = dict(zip(names, refs[13:-1]))
    loads = Loads(refs[-1])
    rows = pieces["x"][0].shape[0]

    def both(name):
        for m in range(micro):
            loads.start(name, pieces[name][m], saved[name].at[pl.ds(m * rows, rows)])

    for m in range(micro):
        loads.start("dy", dy_hbm.at[m], dy_ref.at[pl.ds(m * rows, rows)])
    both("arrived")
    both("beside")
    both("gp")
    loads.weight("wdown", hbm, w)
    loads.weight("wout", hbm, w)
    loads.start("table", table_hbm, table_ref)
    for name in NEEDED[:4]:
        both(name)
    loads.weight("wup", hbm, w)
    loads.weight("wqkv", hbm, w)
    both("x")
    loads.start("pack", pack_hbm, pack_ref)
    kept = {"du": du, "dqkv": dqkv}

    def put(name, value, sl=slice(None), rs=slice(None)):
        kept[name][rs, sl] = value

    loads.wait("dy")
    loads.wait("arrived")
    loads.wait("beside")
    dy = dy_ref[...]
    dy = jnp.where(flag_ref[0] == 0, received(dy, saved["arrived"][...], saved["beside"][...]), dy)
    dy_out[...] = dy
    width, (local, hidden) = dy.shape[1], (dqkv.shape[1] // 3, du.shape[1])
    backward_part(dy, saved, table_ref, w, loads.wait, put)
    loads.wait("x")
    loads.wait("pack")
    vec = unpacked(pack_ref, width, local, hidden)
    dx, d_first, d_second, unit = norm_back(saved["x"][...], du, dqkv, local, vec, w, loads.wait)
    dx_ref[...] = dx
    own[...] = jnp.zeros_like(own)
    other[...] = jnp.zeros_like(other)
    low = flag_ref[1] == 0
    terms = (d_first * unit, d_first, d_second * unit, d_second, dy.astype(F32))
    for i, term in enumerate(terms):
        total = jnp.sum(term, axis=0, keepdims=True)
        front, back = total[:, :local], total[:, local:]
        own[i : i + 1] = jnp.where(low, front, back)
        if i < 4:
            other[i : i + 1] = jnp.where(low, back, front)
    line = 5
    for ref in (dqkv, du):
        for c in range(0, ref.shape[1], local):
            own[line : line + 1] = jnp.sum(ref[:, c : c + local].astype(F32), axis=0, keepdims=True)
            line += 1


def deal(theirs, mine, place, at, core, value, share):
    for z in range(value.shape[0] // (2 * share)):
        front = value[2 * z * share : (2 * z + 1) * share]
        back = value[(2 * z + 1) * share : (2 * z + 2) * share]
        theirs[place + z, at : at + share] = jnp.where(core == 0, back, front)
        mine[place + z, at : at + share] = jnp.where(core == 0, front, back)


def outer(pieces, sl, right):
    return dot_tn(jnp.concatenate([piece[:, sl] for piece in pieces], axis=0), right).astype(BF)


def down_kernel(chips, micro, *refs):
    flag_ref, dy_hbm = refs[:2]
    arrived, beside, active, mixed = (refs[2 + i * micro : 2 + (i + 1) * micro] for i in range(4))
    theirs, mine, dy_ref, sem = refs[2 + 4 * micro :]
    copy = pltpu.make_async_copy(dy_hbm, dy_ref, sem)
    copy.start()
    copy.wait()
    core = flag_ref[2]
    dy = [dy_ref[m] for m in range(micro)]
    for m in range(micro):
        dy[m] = jnp.where(flag_ref[0] == 0, received(dy[m], arrived[m][...], beside[m][...]), dy[m])
    dy = jnp.concatenate(dy, axis=0)
    hidden, local = active[0].shape[1], mixed[0].shape[1]
    share, step = hidden // (2 * chips), hidden // chips
    for z in range(chips):
        deal(theirs, mine, z, 0, core, outer(active, slice(z * step, (z + 1) * step), dy), share)
    deal(theirs, mine, 0, share, core, outer(mixed, slice(0, local), dy), local // (2 * chips))


def rest_kernel(chips, micro, *refs):
    flag_ref, du, dqkv, own, got = refs[:5]
    a1, a2, (theirs, mine) = refs[5 : 5 + micro], refs[5 + micro : 5 + 2 * micro], refs[-2:]
    width, local = a1[0].shape[1], own.shape[1]
    share = width // (2 * chips)
    step = width // 2
    at = 0
    for left, right in ((a2, du), (a1, dqkv)):
        for c in range(0, right.shape[1], local):
            columns = right[:, c : c + local]
            for j in range(2):
                value = outer(left, slice(j * step, (j + 1) * step), columns)
                deal(theirs, mine, j * chips // 2, at, flag_ref[2], value, share)
            at += share
    half = got.shape[0]
    lines = jnp.concatenate([own[:half] + got[...], own[half:]], axis=0).astype(BF)
    for z in range(chips):
        theirs[z, at:] = lines
        mine[z, at:] = lines


def split_kernel(which, *refs):
    flag_ref, mine, got = refs[:3]
    count = len(which)
    outs, (one, two, extra, sems) = refs[-4 - count : -4], refs[-4:]
    place = flag_ref[3]
    loads = Loads(sems)
    index = (
        jnp.where(place % 2 == 0, 3, 0),
        jnp.where(place == 1, 2, 1),
        jnp.where(place == 0, 2, 1),
        jnp.where(place == 0, 1, 2),
        jnp.where(place == 1, 3, 0),
    )
    for i, pick in enumerate(which):
        loads.start(2 * i, mine.at[index[pick]], one.at[i])
        loads.start(2 * i + 1, got.at[index[pick]], two.at[i])
        if pick == 4:
            loads.start("extra", refs[3], extra)
    for i, pick in enumerate(which):
        loads.wait(2 * i)
        loads.wait(2 * i + 1)
        value = one[i].astype(F32) + two[i].astype(F32)
        if pick == 4:
            loads.wait("extra")
            value = value + extra[...].astype(F32)
        outs[i][...] = value.astype(BF)


def arrived_sum(flag_ref, refs, scratch, sems):
    place = flag_ref[3]
    loads = Loads(sems)
    for i in range(2):
        loads.start(i, refs[i].at[place], scratch.at[i])
    edge = jnp.logical_or(place == 0, place == 3)
    for i in range(2):
        loads.wait(i)

    def total(at, rows):
        sl = slice(at, at + rows)
        value = refs[2][sl, :].astype(F32)
        value = jnp.where(edge, value, jnp.zeros_like(value))
        value = value + (scratch[0, sl, :].astype(F32) + scratch[1, sl, :].astype(F32))
        for ref in refs[3:7]:
            value = value + ref[sl, :].astype(F32)
        return value

    return total


def final_down_kernel(flag_ref, *refs):
    down_ref, out_ref, scratch, sems = refs[-4:]
    total = arrived_sum(flag_ref, refs[:7], scratch, sems)
    rows = down_ref.shape[0]
    down_ref[...] = total(0, rows)
    out_ref[...] = total(rows, out_ref.shape[0])


def final_rest_kernel(flag_ref, *refs):
    up_ref, qkv_ref, vec_ref, bqkv_ref, bup_ref, lines, scratch, sems = refs[-8:]
    total = arrived_sum(flag_ref, refs[:7], scratch, sems)
    share, local = qkv_ref.shape[1:]
    at = 0
    for c in range(0, up_ref.shape[1], local):
        up_ref[:, c : c + local] = total(at, share)
        at += share
    for t in range(3):
        qkv_ref[t] = total(at, share)
        at += share
    lines[...] = total(at, lines.shape[0])
    dp_at = 2 * flag_ref[3] + flag_ref[2]
    width = bqkv_ref.shape[1]
    front = pltpu.roll(lines[0:8], local - dp_at * width, 1)
    vec_ref[...] = front[0:5, :width]
    bqkv_ref[...] = front[5:8, :width]
    width = bup_ref.shape[1]
    per_line = local // width
    line = pltpu.roll(lines[8:16], local - (dp_at % per_line) * width, 1)
    row = dp_at // per_line
    picked = jnp.zeros((1, width), F32)
    for i in range(per_line and 8 // per_line):
        picked = jnp.where(row == i, line[i : i + 1, :width], picked)
    bup_ref[...] = picked


def tail_kernel(micro, *refs):
    part, other, up, grad, other_grad = refs[:5]
    sources = refs[5 : 5 + micro]
    out_ref, grad_ref = refs[-2:]
    rows = sources[0].shape[0]
    for m in range(micro):
        sl = slice(m * rows, (m + 1) * rows)
        both = part[sl].astype(F32) + other[sl].astype(F32)
        out_ref[sl] = (sources[m][...].astype(F32) + both).astype(BF)
    grad_ref[...] = up[...].astype(F32) + (grad[...].astype(F32) + other_grad[...].astype(F32))


def o_kernel(micro, *refs):
    mixed_refs, active_refs = refs[:micro], refs[micro : 2 * micro]
    pack_ref, wout_hbm, wdown_hbm = refs[2 * micro : 2 * micro + 3]
    out_ref, wout, wdown, mixed, active, sems = refs[-6:]
    loads = Loads(sems)
    hbm, w = {"wout": wout_hbm, "wdown": wdown_hbm}, {"wout": wout, "wdown": wdown}
    loads.weight("wout", hbm, w)
    loads.weight("wdown", hbm, w)
    rows = mixed_refs[0].shape[0]
    for m in range(micro):
        mixed[m * rows : (m + 1) * rows] = mixed_refs[m][...]
        active[m * rows : (m + 1) * rows] = active_refs[m][...]
    vec = unpacked(pack_ref, wout.shape[1], wout.shape[0], wdown.shape[0])
    out_ref[...] = output_part(mixed, active, vec, w, loads.wait)


VM = pl.BlockSpec(memory_space=pltpu.VMEM)
SM = pl.BlockSpec(memory_space=pltpu.SMEM)
HB = pl.BlockSpec(memory_space=pltpu.HBM)


def scratch_like(arrays):
    return [pltpu.VMEM(a.shape, a.dtype) for a in arrays]


def cost(ws, rows, passes):
    size = sum(math.prod(a.shape) for a in ws)
    return pl.CostEstimate(flops=2 * size * rows * passes, bytes_accessed=2 * size, transcendentals=0)


def params(mib):
    return pltpu.CompilerParams(vmem_limit_bytes=mib * 2**20)


def call_f(flags, xs, table, ws, vecs):
    micro, rows, width = xs.shape
    local, hidden = ws[1].shape[0], ws[3].shape[0]
    total = micro * rows
    scratch = scratch_like(ws) + [
        pltpu.VMEM((total, local), BF),
        pltpu.VMEM((total, hidden), BF),
        pltpu.VMEM((total, width), BF),
        pltpu.VMEM(table.shape, F32),
        pltpu.SemaphoreType.DMA((24,)),
    ]
    out = [jax.ShapeDtypeStruct((rows, width), BF)] * micro + [jax.ShapeDtypeStruct((16, hidden), F32)]
    return pl.pallas_call(
        functools.partial(f_kernel, micro),
        out_shape=out,
        in_specs=[SM] + [HB] * 14,
        out_specs=[VM] * len(out),
        scratch_shapes=scratch + scratch_like(vecs),
        compiler_params=params(54),
        cost_estimate=cost(ws, total, 1),
    )(flags, xs, table, *ws, *vecs)


def call_fb(at, flags, xs, cots, arrived, table, pack, ws):
    rows, width = xs.shape[1:]
    local, hidden = ws[1].shape[0], ws[3].shape[0]
    shape = jax.ShapeDtypeStruct
    outs = [shape((rows, width), BF)] * 4
    outs += [shape((rows, local), BF)] * 3
    outs += [
        shape((rows, 2 * rows * local // LANES), BF),
        shape((rows, local), BF),
        shape((rows, hidden), BF),
        shape((rows, hidden), BF),
    ]
    return pl.pallas_call(
        functools.partial(fb_kernel, at),
        out_shape=outs,
        in_specs=[SM] + [HB] * 10,
        out_specs=[HB] * len(outs),
        scratch_shapes=scratch_like(outs)
        + scratch_like(ws)
        + [
            pltpu.VMEM((rows, hidden), BF),
            pltpu.VMEM((rows, 3 * local), BF),
            pltpu.VMEM((rows, width), BF),
            pltpu.VMEM((rows, width), BF),
            pltpu.VMEM((rows, width), BF),
            pltpu.VMEM((rows, width), BF),
            pltpu.VMEM(table.shape, F32),
            pltpu.VMEM(pack.shape, F32),
            pltpu.SemaphoreType.DMA((24,)),
            pltpu.SemaphoreType.DMA((len(outs),)),
        ],
        compiler_params=params(54),
        cost_estimate=cost(ws, rows, 2),
    )(flags, xs, cots, *arrived, table, pack, *ws)


def call_b(flags, cots, table, pack, ws, pieces, after):
    micro, rows, width = cots.shape
    local, hidden = ws[1].shape[0], ws[3].shape[0]
    shape = jax.ShapeDtypeStruct
    total = micro * rows
    outs = [
        shape((total, width), BF),
        shape((total, hidden), BF),
        shape((total, 3 * local), BF),
        shape((16, local), F32),
        shape((8, local), F32),
        shape((total, width), BF),
    ]
    flat = [array for group in pieces for array in group]
    return pl.pallas_call(
        functools.partial(b_kernel, micro),
        out_shape=outs,
        in_specs=[SM] + [HB] * (7 + len(flat) + len(after)),
        out_specs=[VM] * len(outs),
        scratch_shapes=scratch_like(ws)
        + [pltpu.VMEM((total, width), BF)]
        + scratch_like([table, pack])
        + [pltpu.VMEM((total, group[0].shape[1]), group[0].dtype) for group in pieces]
        + [pltpu.SemaphoreType.DMA((32,))],
        compiler_params=params(54),
        cost_estimate=cost(ws, total, 1),
    )(flags, cots, table, pack, *ws, *flat, *after)


def call_blocks(kernel, flags, operands, specs, block, flops, scratch=()):
    outs = [jax.ShapeDtypeStruct(block, BF)] * 2
    return pl.pallas_call(
        kernel,
        out_shape=outs,
        in_specs=[SM] + specs,
        out_specs=[VM] * 2,
        scratch_shapes=list(scratch),
        compiler_params=params(24),
        cost_estimate=pl.CostEstimate(flops=flops, bytes_accessed=4 * math.prod(block), transcendentals=0),
    )(flags, *operands)


def call_split(flags, mine, got, which, after):
    block, count = mine.shape[1:], len(which)
    return pl.pallas_call(
        functools.partial(split_kernel, which),
        out_shape=[jax.ShapeDtypeStruct(block, BF)] * count,
        in_specs=[SM] + [HB] * (2 + len(after)),
        out_specs=[VM] * count,
        scratch_shapes=[pltpu.VMEM((count,) + block, BF)] * 2
        + [pltpu.VMEM(block, BF), pltpu.SemaphoreType.DMA((8,))],
        compiler_params=params(16),
    )(flags, mine, got, *after)


def call_final(kernel, flags, parts, outs, after, scratch=()):
    return pl.pallas_call(
        kernel,
        out_shape=[jax.ShapeDtypeStruct(shape, F32) for shape in outs],
        in_specs=[SM, HB, HB] + [VM] * 5 + [HB] * len(after),
        out_specs=[VM] * len(outs),
        scratch_shapes=list(scratch)
        + [pltpu.VMEM((2,) + parts[2].shape, BF), pltpu.SemaphoreType.DMA((2,))],
        compiler_params=params(16),
    )(flags, *parts, *after)


def call_tail(part, other, up, grad, other_grad, sources, after):
    micro = len(sources)
    return pl.pallas_call(
        functools.partial(tail_kernel, micro),
        out_shape=[jax.ShapeDtypeStruct(part.shape, BF), jax.ShapeDtypeStruct(part.shape, F32)],
        in_specs=[VM] * (5 + micro) + [HB] * len(after),
        out_specs=[VM] * 2,
        compiler_params=params(16),
    )(part, other, up, grad, other_grad, *sources, *after)


def call_o(mixed, active, pack, ws, after=()):
    micro, (rows, local) = len(mixed), mixed[0].shape
    hidden, width = ws[3].shape
    total = micro * rows
    return pl.pallas_call(
        functools.partial(o_kernel, micro),
        out_shape=jax.ShapeDtypeStruct((total, width), BF),
        in_specs=[VM] * (2 * micro + 1) + [HB] * (2 + len(after)),
        out_specs=VM,
        scratch_shapes=[
            pltpu.VMEM((local, width), BF),
            pltpu.VMEM((hidden, width), BF),
            pltpu.VMEM((total, local), BF),
            pltpu.VMEM((total, hidden), BF),
            pltpu.SemaphoreType.DMA((8,)),
        ],
        compiler_params=params(54),
        cost_estimate=cost((ws[1], ws[3]), total, 1),
    )(*mixed, *active, pack, ws[1], ws[3], *after)


def handed(value, source, target):
    straight = lax.ppermute(value, "section", [(source, target)])
    across = [(2 * source, 2 * target + 1), (2 * source + 1, 2 * target)]
    return straight, lax.ppermute(value, ("section", "tensor"), across)


def swap(value):
    return lax.ppermute(value, "tensor", [(0, 1), (1, 0)])


ONE = [(0, 1), (1, 0), (2, 3), (3, 2)]
TWO = [(0, 1), (3, 2)]
THREE = [(1, 2), (2, 1)]
FOUR = [(0, 2), (3, 1)]
FIVE = [(1, 3), (2, 0)]


class Line:
    def __init__(self, theirs, mine, at):
        self.place = at // 2
        self.mine = mine
        self.got = lax.ppermute(theirs, "dp", [(i, i ^ 1) for i in range(8)])

    def block(self, index):
        one = lax.dynamic_index_in_dim(self.mine, index, 0, keepdims=False)
        two = lax.dynamic_index_in_dim(self.got, index, 0, keepdims=False)
        return one.astype(F32) + two.astype(F32)

    def send(self, value, pairs):
        return lax.ppermute(value, "dp", [(2 * a + c, 2 * b + c) for a, b in pairs for c in range(2)])

    def start(self):
        place = self.place
        values = [
            self.block(index).astype(BF)
            for index in (
                jnp.where(place % 2 == 0, 3, 0),
                jnp.where(place == 1, 2, 1),
                jnp.where(place == 0, 2, 1),
                jnp.where(place == 0, 1, 2),
            )
        ]
        self.one = self.send(values[0], ONE)
        self.three = self.send(values[1], THREE)
        self.four = self.send(values[2], FOUR)
        self.two = self.send(values[3], TWO)
        return tuple(values)

    def relay(self):
        value = (self.block(jnp.where(self.place == 1, 3, 0)) + self.one.astype(F32)).astype(BF)
        self.five = self.send(value, FIVE)
        return value

    def staged(self, flags):
        first = call_split(flags, self.mine, self.got, (0, 1), ())
        self.one = self.send(first[0], ONE)
        self.three = self.send(first[1], THREE)
        rest = call_split(flags, self.mine, self.got, (4, 2, 3), (self.one, self.three))
        self.five = self.send(rest[0], FIVE)
        self.four = self.send(rest[1], FOUR)
        self.two = self.send(rest[2], TWO)

    def parts(self):
        return self.mine, self.got, self.one, self.two, self.three, self.four, self.five


def wide(pieces, others):
    left, right = jnp.concatenate(pieces, axis=0), jnp.concatenate(others, axis=0)
    return jnp.einsum("ta,tb->ab", left, right, preferred_element_type=F32).astype(BF)


def scattered(blocks):
    parts, rows, columns = blocks.shape
    return lax.psum_scatter(blocks.reshape(parts * rows, columns), "dp", scatter_dimension=0, tiled=True).astype(F32)


def per_device(inputs, cotangent, g1, b1, g2, b2, w_qkv, b_qkv, w_out, b_out, w_up, b_up, w_down, b_down):
    section = lax.axis_index("section")
    owner = lax.axis_index("tensor")
    dp_at = lax.axis_index("dp")
    parts = lax.axis_size("dp")
    micro, seqs, length, width = inputs.shape
    rows = seqs * length
    local, hidden = w_out.shape[1], w_up.shape[2]
    flags = jnp.stack([section, owner, dp_at % 2, dp_at // 2]).astype(jnp.int32)
    table = jnp.asarray(rope_tables(length))
    vecs = (g1, b1, g2, b2, b_qkv[0], b_out, b_up, b_down)
    ws = (w_qkv[0].transpose(1, 0, 2), w_out[0], w_up[0], w_down[0])
    xs = inputs.reshape(micro, rows, width)
    cots = cotangent.reshape(micro, rows, width)
    lined = parts == 8
    chips = parts // 2

    *outs, pack = call_f(flags, xs, table, ws, vecs)
    arrivals = []
    for m in range(micro):
        arrivals.append(handed(outs[m], 0, 1))
    kept, sources, backs = [], [], []
    for m in range(micro):
        dx, source, *saved = call_fb(m, flags, xs, cots, arrivals[m], table, pack, ws)
        backs.append(handed(dx, 1, 0))
        kept.append(dict(zip(SAVED, saved)))
        sources.append(source)
    a1, a2, mixed, active = ([kept[m][n] for m in range(micro)] for n in ("a1", "a2", "mixed", "g"))

    after = ()
    arrived, beside = ([back[i] for back in backs] for i in range(2))
    if lined:
        theirs, mine = call_blocks(
            functools.partial(down_kernel, chips, micro),
            flags,
            (cots, *arrived, *beside, *active, *mixed),
            [HB] + [VM] * (4 * micro),
            (chips, hidden // parts + local // parts, width),
            2 * micro * rows * width * (hidden + local),
            [pltpu.VMEM(cots.shape, BF), pltpu.SemaphoreType.DMA],
        )
        line_down = Line(theirs, mine, dp_at)
        after = line_down.start()
    pieces = [arrived, beside, sources] + [[kept[m][n] for m in range(micro)] for n in NEEDED]
    grad, du, dqkv, own, other, up = call_b(flags, cots, table, pack, ws, pieces, after)
    got = swap(other)
    share = width // parts
    if lined:
        after = (line_down.relay(), line_down.two, line_down.three, line_down.four)
        slabs = hidden // local
        lines = own.shape[0]
        theirs, mine = call_blocks(
            functools.partial(rest_kernel, chips, micro),
            flags,
            (du, dqkv, own, got, *a1, *a2, *after),
            [VM] * (4 + 2 * micro) + [HB] * len(after),
            (chips, (slabs + 3) * share + lines, local),
            2 * micro * rows * width * (hidden + 3 * local),
        )
        line_rest = Line(theirs, mine, dp_at)
        part = call_o(mixed, active, pack, ws, (mine,))
        line_rest.staged(flags)
        after = (line_rest.one,)
        down_rows = hidden // parts
        outs = [(down_rows, width), (local // parts, width)]
        d_wdown, d_wout = call_final(final_down_kernel, flags, line_down.parts(), outs, after)
        section_out, input_grad = call_tail(part, swap(part), up, grad, swap(grad), sources, after)
        outs = [(share, hidden), (3, share, local), (5, local // parts), (3, local // parts), (1, down_rows)]
        d_wup, d_wqkv, d_vec, d_bqkv, d_bup = call_final(
            final_rest_kernel, flags, line_rest.parts(), outs, (), [pltpu.VMEM((lines, local), F32)]
        )
        d_wqkv = d_wqkv.transpose(1, 0, 2)
    else:
        d_wdown = wide(active, [up]).reshape(parts, -1, width)
        d_wout = wide(mixed, [up]).reshape(parts, -1, width)
        d_both = scattered(jnp.concatenate([d_wdown, d_wout], axis=1))
        d_wup = scattered(wide(a2, [du]).reshape(parts, -1, hidden))
        d_wqkv = wide(a1, [dqkv]).reshape(parts, share, 3, local).transpose(0, 2, 1, 3)
        lines = jnp.concatenate([own[: got.shape[0]] + got, own[got.shape[0] :]]).astype(BF)
        lines = jnp.broadcast_to(lines[None], (parts,) + lines.shape)
        last = scattered(jnp.concatenate([d_wqkv.reshape(parts, 3 * share, local), lines], axis=1))
        down_rows = hidden // parts
        d_wdown, d_wout = d_both[:down_rows], d_both[down_rows:]
        d_wqkv = last[: 3 * share].reshape(3, share, local).transpose(1, 0, 2)
        lines = last[3 * share :]
        d_vec = lax.dynamic_slice(lines, (0, dp_at * (local // parts)), (8, local // parts))
        d_vec, d_bqkv = d_vec[:5], d_vec[5:]
        up_lines = lines[8 : 8 + hidden // local].reshape(1, hidden)
        d_bup = lax.dynamic_slice_in_dim(up_lines, dp_at * down_rows, down_rows, 1)
        part = call_o(mixed, active, pack, ws)
        section_out, input_grad = call_tail(part, swap(part), up, grad, swap(grad), sources, ())
    return (
        section_out.reshape(1, micro, seqs, length, width),
        input_grad.reshape(1, micro, seqs, length, width),
        d_vec[0:1],
        d_vec[1:2],
        d_vec[2:3],
        d_vec[3:4],
        d_wqkv[None],
        d_bqkv[None],
        d_wout[None],
        d_vec[4:5],
        d_wup[None],
        d_bup,
        d_wdown[None],
        d_vec[4:5],
    )


def solution(mesh):
    return jax.shard_map(
        per_device,
        mesh=mesh,
        in_specs=(
            P(None, "dp", None, None),
            P(None, "dp", None, None),
            P("section", None),
            P("section", None),
            P("section", None),
            P("section", None),
            P("section", None, None, "tensor"),
            P("section", None, "tensor"),
            P("section", "tensor", None),
            P("section", None),
            P("section", None, "tensor"),
            P("section", "tensor"),
            P("section", "tensor", None),
            P("section", None),
        ),
        out_specs=(
            P("section", None, "dp", None, None),
            P("section", None, "dp", None, None),
            P("section", ("tensor", "dp")),
            P("section", ("tensor", "dp")),
            P("section", ("tensor", "dp")),
            P("section", ("tensor", "dp")),
            P("section", "dp", None, "tensor"),
            P("section", None, ("tensor", "dp")),
            P("section", ("tensor", "dp"), None),
            P("section", ("tensor", "dp")),
            P("section", "dp", "tensor"),
            P("section", ("tensor", "dp")),
            P("section", ("tensor", "dp"), None),
            P("section", ("tensor", "dp")),
        ),
        check_vma=False,
    )
```

```python
import functools
import math

import jax
import jax.numpy as jnp
import numpy as np
from jax import lax
from jax.experimental import pallas as pl
from jax.experimental.pallas import tpu as pltpu
from jax.sharding import PartitionSpec as P

HEAD = 64
ROT = 16
LANES = 128
PIECE = 512
AHEAD = 40
EPSILON = 1e-05
BF = jnp.bfloat16
F32 = jnp.float32


def rope_tables(length):
    half = ROT // 2
    inverse = np.exp(-math.log(10000.0) * np.arange(half, dtype=np.float32) * np.float32(2.0) / ROT)
    angle = np.arange(length, dtype=np.float32)[:, None] * inverse[None, :].astype(np.float32)
    cosine, sine = np.cos(angle), np.sin(angle)
    table = np.zeros((3, length, LANES), np.float32)
    table[0] = 1.0
    for head in range(LANES // HEAD):
        at = head * HEAD
        table[0, :, at : at + half] = cosine
        table[0, :, at + half : at + ROT] = cosine
        table[1, :, at : at + half] = -sine
        table[2, :, at + half : at + ROT] = sine
    return table


def dot(a, b):
    return jnp.dot(a, b, preferred_element_type=F32)


def dot_nt(a, b):
    return lax.dot_general(a, b, (((1,), (1,)), ((), ())), preferred_element_type=F32)


def dot_tn(a, b):
    return lax.dot_general(a, b, (((0,), (0,)), ((), ())), preferred_element_type=F32)


def roped(value, table, sign):
    half = ROT // 2
    ahead = pltpu.roll(value, LANES - half, 1) * table[1]
    behind = pltpu.roll(value, half, 1) * table[2]
    return value * table[0] + sign * (ahead + behind)


def head_pair(value):
    low = lax.broadcasted_iota(jnp.int32, value.shape, 1) < HEAD
    zero = jnp.zeros_like(value)
    return jnp.concatenate([jnp.where(low, value, zero), jnp.where(low, zero, value)], axis=0)


def pair_merge(value):
    rows = value.shape[0] // 2
    low = lax.broadcasted_iota(jnp.int32, (rows, LANES), 1) < HEAD
    return jnp.where(low, value[:rows], value[rows:])


def normal(block):
    width = block.shape[1]
    center = block - jnp.sum(block, axis=1, keepdims=True) * (1.0 / width)
    spread = jnp.sum(center * center, axis=1, keepdims=True) * (1.0 / width)
    scale = lax.rsqrt(spread + EPSILON)
    return center * scale, scale


def forward_part(x, vec, table, w, wait, put):
    rows, width = x.shape
    unit, unused = normal(x.astype(F32))
    first = (unit * vec["g1"] + vec["b1"]).astype(BF)
    second = (unit * vec["g2"] + vec["b2"]).astype(BF)
    put("a1", first)
    put("a2", second)
    bqkv = vec["bqkv"]
    raw = []
    for j in range(3):
        wait("wqkv", j)
        raw.append(dot(first, w["wqkv"][j]) + bqkv[j : j + 1])
    local = raw[0].shape[1]
    wait("table")
    length = table.shape[1]
    row = lax.broadcasted_iota(jnp.int32, (length, length), 0)
    keep = row >= lax.broadcasted_iota(jnp.int32, (length, length), 1)
    for start in range(0, rows, length):
        rs = slice(start, start + length)
        for p in range(local // LANES):
            sl = slice(p * LANES, (p + 1) * LANES)
            q = roped(raw[0][rs, sl], table, 1.0).astype(BF)
            k = roped(raw[1][rs, sl], table, 1.0).astype(BF)
            v = raw[2][rs, sl].astype(BF)
            put("q", q, sl)
            put("k", k, sl)
            put("v", v, sl)
            scores = dot_nt(q, head_pair(k)) * HEAD**-0.5
            prob = []
            for h in range(2):
                part = jnp.where(keep, scores[:, h * length : (h + 1) * length], -1e30)
                expo = jnp.exp(part - jnp.max(part, axis=1, keepdims=True))
                prob.append(expo * (1.0 / jnp.sum(expo, axis=1, keepdims=True)))
            prob = jnp.concatenate(prob, axis=1).astype(BF)
            put("prob", prob, slice(p * 2 * length, (p + 1) * 2 * length))
            put("mixed", dot(prob, head_pair(v)).astype(BF), sl, rs)
    hidden = w["wup"].shape[1]
    step = 256
    for c in range(0, hidden, step):
        sl = slice(c, c + step)
        wait("wup", c // PIECE)
        u = dot(second, w["wup"][:, sl]) + vec["bup"][:, sl]
        phi = 0.5 + 0.5 * lax.erf(u * (2.0**-0.5))
        put("g", (u * phi).astype(BF), sl)
        put("gp", lambda: phi + u * (jnp.exp(-0.5 * u * u) * (2.0 * math.pi) ** -0.5), sl)


def output_part(mixed, active, vec, w, wait):
    wait("wout")
    total = dot(mixed[...], w["wout"][...])
    wait("wdown")
    total = total + dot(active[...], w["wdown"][...])
    return (total + vec["extra"]).astype(BF)


def backward_part(dy, saved, table, w, wait, put):
    rows = dy.shape[0]
    hidden = w["wdown"].shape[0]
    step = 256
    wait("gp")
    for c in range(0, hidden, step):
        sl = slice(c, c + step)
        wait("wdown", c // PIECE)
        du = (dot_nt(dy, w["wdown"][sl, :]) * saved["gp"][:, sl].astype(F32)).astype(BF)
        put("du", du, sl)
    wait("wout")
    for name in ("table", "q", "k", "v", "prob"):
        wait(name)
    d_mixed = dot_nt(dy, w["wout"][...]).astype(BF)
    local = d_mixed.shape[1]
    length = table.shape[1]
    scale = HEAD**-0.5
    for start in range(0, rows, length):
        rs = slice(start, start + length)
        for p in range(local // LANES):
            sl = slice(p * LANES, (p + 1) * LANES)
            q, k, v = saved["q"][rs, sl], saved["k"][rs, sl], saved["v"][rs, sl]
            low = saved["prob"][rs, p * 2 * length : (p + 1) * 2 * length]
            prob = low.astype(F32)
            d_tile = d_mixed[rs, sl]
            d_prob = dot_nt(d_tile, head_pair(v))
            d_value = pair_merge(dot_tn(low, d_tile))
            d_scores = []
            for h in range(2):
                part = prob[:, h * length : (h + 1) * length]
                d_part = d_prob[:, h * length : (h + 1) * length]
                both = part * d_part
                d_scores.append(both - part * jnp.sum(both, axis=1, keepdims=True))
            d_scores = jnp.concatenate(d_scores, axis=1).astype(BF)
            d_query = dot(d_scores, head_pair(k)) * scale
            d_keys = pair_merge(dot_tn(d_scores, q)) * scale
            at = p * LANES
            put("dqkv", roped(d_query, table, -1.0).astype(BF), slice(at, at + LANES), rs)
            at += local
            put("dqkv", roped(d_keys, table, -1.0).astype(BF), slice(at, at + LANES), rs)
            at += local
            put("dqkv", d_value.astype(BF), slice(at, at + LANES), rs)


def norm_back(x, du, dqkv, local, vec, w, wait):
    wait("wup")
    d_second = dot_nt(du[...], w["wup"][...])
    for j in range(3):
        wait("wqkv", j)
    d_first = dot_nt(dqkv[:, :local], w["wqkv"][0])
    for j in range(1, 3):
        d_first = d_first + dot_nt(dqkv[:, j * local : (j + 1) * local], w["wqkv"][j])
    unit, scale = normal(x.astype(F32))
    e = d_first * vec["g1"] + d_second * vec["g2"]
    width = x.shape[1]
    mean = jnp.sum(e, axis=1, keepdims=True) * (1.0 / width)
    along = jnp.sum(e * unit, axis=1, keepdims=True) * (1.0 / width)
    dx = (e - mean - unit * along) * scale
    return dx.astype(BF), d_first, d_second, unit


WEIGHTS = ("wqkv", "wout", "wup", "wdown")
VECTORS = ("g1", "b1", "g2", "b2", "bqkv", "bout", "bup", "bdown")
NEEDED = ("q", "k", "v", "prob", "gp")
SAVED = ("a1", "a2", "q", "k", "v", "prob", "mixed", "g", "gp")


class Loads:
    def __init__(self, sems, ahead=64):
        self.sems, self.copies, self.queue, self.ahead = sems, {}, [], ahead
        self.started = self.waited = 0

    def start(self, name, source, target):
        copy = pltpu.make_async_copy(source, target, self.sems.at[len(self.queue)])
        self.copies.setdefault(name, {})[len(self.copies.get(name, {}))] = (len(self.queue), copy)
        self.queue.append(copy)
        self.pump(self.waited + self.ahead)

    def pump(self, until):
        while self.started < min(until, len(self.queue)):
            self.queue[self.started].start()
            self.started += 1

    def weight(self, name, hbm, w):
        source, target = hbm[name], w[name]
        if name == "wqkv":
            for j in range(3):
                self.start(name, source.at[j], target.at[j])
        elif name == "wout":
            self.start(name, source, target)
        else:
            for c in range(0, source.shape[0 if name == "wdown" else 1], PIECE):
                at = (pl.ds(c, PIECE), slice(None)) if name == "wdown" else (slice(None), pl.ds(c, PIECE))
                self.start(name, source.at[at], target.at[at])

    def wait(self, name, index=None):
        left = self.copies.get(name, {})
        for piece in [index] if index is not None else list(left):
            if piece in left:
                at, copy = left.pop(piece)
                self.pump(at + 1)
                copy.wait()
                self.waited += 1
                self.pump(self.waited + self.ahead)


def unpacked(pack, width, local, hidden):
    return {
        "g1": pack[0:1, :width],
        "b1": pack[1:2, :width],
        "g2": pack[2:3, :width],
        "b2": pack[3:4, :width],
        "extra": pack[4:5, :width],
        "bup": pack[5:6, :hidden],
        "bqkv": pack[6:9, :local],
    }


def f_kernel(micro, *refs):
    flag_ref, x_hbm, table_hbm = refs[:3]
    hbm = dict(zip(WEIGHTS, refs[3:7]))
    vec_hbm = dict(zip(VECTORS, refs[7:15]))
    out_refs, pack_ref = refs[15 : 15 + micro], refs[15 + micro]
    refs = refs[16 + micro :]
    w = dict(zip(WEIGHTS, refs[:4]))
    mixed, active, x_ref, table_ref, sems = refs[4:9]
    loads = Loads(sems)
    vec_ref = dict(zip(VECTORS, refs[9:]))
    rows, width = out_refs[0].shape
    for m in range(micro):
        loads.start("x", x_hbm.at[m], x_ref.at[pl.ds(m * rows, rows)])
    for name in VECTORS:
        loads.start(name, vec_hbm[name], vec_ref[name])
    loads.weight("wqkv", hbm, w)
    loads.start("table", table_hbm, table_ref)
    for name in ("wup", "wout", "wdown"):
        loads.weight(name, hbm, w)
    local, hidden = mixed.shape[1], active.shape[1]
    for name in VECTORS:
        loads.wait(name)
    for i, name in enumerate(("g1", "b1", "g2", "b2")):
        pack_ref[i : i + 1, :width] = vec_ref[name][...].astype(F32)
    extra = vec_ref["bout"][...].astype(F32) + vec_ref["bdown"][...].astype(F32)
    pack_ref[4:5, :width] = jnp.where(flag_ref[1] == 0, extra, jnp.zeros_like(extra))
    pack_ref[5:6, :hidden] = vec_ref["bup"][...].astype(F32)
    pack_ref[6:9, :local] = vec_ref["bqkv"][...].astype(F32)
    vec = unpacked(pack_ref, width, local, hidden)

    def put(name, value, sl=slice(None), rs=slice(None)):
        if name == "mixed":
            mixed[rs, sl] = value
        if name == "g":
            active[rs, sl] = value

    loads.wait("x")
    forward_part(x_ref[...], vec, table_ref, w, loads.wait, put)
    out = output_part(mixed, active, vec, w, loads.wait)
    for m in range(micro):
        out_refs[m][...] = out[m * rows : (m + 1) * rows]


def received(base, one, two):
    return (base.astype(F32) + (one.astype(F32) + two.astype(F32))).astype(BF)


def fb_kernel(at, *refs):
    flag_ref, x_hbm, dy_hbm, arrived_hbm, beside_hbm, table_hbm, pack_hbm = refs[:7]
    refs = refs[1:]
    hbm = dict(zip(WEIGHTS, refs[6:10]))
    names = ("dx", "source") + SAVED
    outs = dict(zip(names, refs[10 : 10 + len(names)]))
    refs = refs[10 + len(names) :]
    held = dict(zip(names, refs[: len(names)]))
    refs = refs[len(names) :]
    w = dict(zip(WEIGHTS, refs[:4]))
    du, dqkv, x_ref, dy_ref, arrived_ref, beside_ref, table_ref, pack_ref, sems, out_sems = refs[4:]
    loads, stores = Loads(sems), Loads(out_sems)
    loads.start("x", x_hbm.at[at], x_ref)
    loads.start("arrived", arrived_hbm, arrived_ref)
    loads.start("arrived", beside_hbm, beside_ref)
    loads.start("pack", pack_hbm, pack_ref)
    loads.weight("wqkv", hbm, w)
    loads.start("table", table_hbm, table_ref)
    loads.weight("wup", hbm, w)
    loads.start("dy", dy_hbm.at[at], dy_ref)
    loads.weight("wdown", hbm, w)
    loads.weight("wout", hbm, w)
    held_too = dict(held, du=du, dqkv=dqkv)

    def put(name, value, sl=slice(None), rs=slice(None)):
        ref = held_too[name]
        value = value() if callable(value) else value
        ref[rs, sl] = value.astype(ref.dtype)

    width, (local, hidden) = x_ref.shape[1], (dqkv.shape[1] // 3, du.shape[1])
    loads.wait("x")
    loads.wait("arrived")
    x = x_ref[...]
    x = jnp.where(flag_ref[0] == 0, x, received(x, arrived_ref[...], beside_ref[...]))
    loads.wait("pack")
    vec = unpacked(pack_ref, width, local, hidden)
    held["source"][...] = x
    forward_part(x, vec, table_ref, w, loads.wait, put)
    for name in ("source",) + SAVED:
        stores.start(name, held[name], outs[name])
    loads.wait("dy")
    backward_part(dy_ref[...], held, table_ref, w, loads.wait, put)
    held["dx"][...] = norm_back(x, du, dqkv, local, vec, w, loads.wait)[0]
    stores.start("dx", held["dx"], outs["dx"])
    for name in names:
        stores.wait(name)


def b_kernel(micro, *refs):
    flag_ref, dy_hbm, table_hbm, pack_hbm = refs[:4]
    hbm = dict(zip(WEIGHTS, refs[4:8]))
    names = ("arrived", "beside", "x") + NEEDED
    pieces = {n: refs[8 + i * micro : 8 + (i + 1) * micro] for i, n in enumerate(names)}
    refs = refs[-(6 + 4 + 3 + len(names) + 1) :]
    dx_ref, du, dqkv, own, other, dy_out = refs[:6]
    w = dict(zip(WEIGHTS, refs[6:10]))
    dy_ref, table_ref, pack_ref = refs[10:13]
    saved = dict(zip(names, refs[13:-1]))
    loads = Loads(refs[-1])
    rows = pieces["x"][0].shape[0]

    def both(name):
        for m in range(micro):
            loads.start(name, pieces[name][m], saved[name].at[pl.ds(m * rows, rows)])

    for m in range(micro):
        loads.start("dy", dy_hbm.at[m], dy_ref.at[pl.ds(m * rows, rows)])
    both("arrived")
    both("beside")
    both("gp")
    loads.weight("wdown", hbm, w)
    loads.weight("wout", hbm, w)
    loads.start("table", table_hbm, table_ref)
    for name in NEEDED[:4]:
        both(name)
    loads.weight("wup", hbm, w)
    loads.weight("wqkv", hbm, w)
    both("x")
    loads.start("pack", pack_hbm, pack_ref)
    kept = {"du": du, "dqkv": dqkv}

    def put(name, value, sl=slice(None), rs=slice(None)):
        kept[name][rs, sl] = value

    loads.wait("dy")
    loads.wait("arrived")
    loads.wait("beside")
    dy = dy_ref[...]
    dy = jnp.where(flag_ref[0] == 0, received(dy, saved["arrived"][...], saved["beside"][...]), dy)
    dy_out[...] = dy
    width, (local, hidden) = dy.shape[1], (dqkv.shape[1] // 3, du.shape[1])
    backward_part(dy, saved, table_ref, w, loads.wait, put)
    loads.wait("x")
    loads.wait("pack")
    vec = unpacked(pack_ref, width, local, hidden)
    dx, d_first, d_second, unit = norm_back(saved["x"][...], du, dqkv, local, vec, w, loads.wait)
    dx_ref[...] = dx
    own[...] = jnp.zeros_like(own)
    other[...] = jnp.zeros_like(other)
    low = flag_ref[1] == 0
    terms = (d_first * unit, d_first, d_second * unit, d_second, dy.astype(F32))
    for i, term in enumerate(terms):
        total = jnp.sum(term, axis=0, keepdims=True)
        front, back = total[:, :local], total[:, local:]
        own[i : i + 1] = jnp.where(low, front, back)
        if i < 4:
            other[i : i + 1] = jnp.where(low, back, front)
    line = 5
    for ref in (dqkv, du):
        for c in range(0, ref.shape[1], local):
            own[line : line + 1] = jnp.sum(ref[:, c : c + local].astype(F32), axis=0, keepdims=True)
            line += 1


def deal(theirs, mine, place, at, core, value, share):
    for z in range(value.shape[0] // (2 * share)):
        front = value[2 * z * share : (2 * z + 1) * share]
        back = value[(2 * z + 1) * share : (2 * z + 2) * share]
        theirs[place + z, at : at + share] = jnp.where(core == 0, back, front)
        mine[place + z, at : at + share] = jnp.where(core == 0, front, back)


def outer(pieces, sl, right):
    return dot_tn(jnp.concatenate([piece[:, sl] for piece in pieces], axis=0), right).astype(BF)


def down_kernel(chips, micro, *refs):
    flag_ref, dy_hbm = refs[:2]
    arrived, beside, active, mixed = (refs[2 + i * micro : 2 + (i + 1) * micro] for i in range(4))
    theirs, mine, dy_ref, sem = refs[2 + 4 * micro :]
    copy = pltpu.make_async_copy(dy_hbm, dy_ref, sem)
    copy.start()
    copy.wait()
    core = flag_ref[2]
    dy = [dy_ref[m] for m in range(micro)]
    for m in range(micro):
        dy[m] = jnp.where(flag_ref[0] == 0, received(dy[m], arrived[m][...], beside[m][...]), dy[m])
    dy = jnp.concatenate(dy, axis=0)
    hidden, local = active[0].shape[1], mixed[0].shape[1]
    share, step = hidden // (2 * chips), hidden // chips
    for z in range(chips):
        deal(theirs, mine, z, 0, core, outer(active, slice(z * step, (z + 1) * step), dy), share)
    deal(theirs, mine, 0, share, core, outer(mixed, slice(0, local), dy), local // (2 * chips))


def rest_kernel(chips, micro, *refs):
    flag_ref, du, dqkv, own, got = refs[:5]
    a1, a2, (theirs, mine) = refs[5 : 5 + micro], refs[5 + micro : 5 + 2 * micro], refs[-2:]
    width, local = a1[0].shape[1], own.shape[1]
    share = width // (2 * chips)
    step = width // 2
    at = 0
    for left, right in ((a2, du), (a1, dqkv)):
        for c in range(0, right.shape[1], local):
            columns = right[:, c : c + local]
            for j in range(2):
                value = outer(left, slice(j * step, (j + 1) * step), columns)
                deal(theirs, mine, j * chips // 2, at, flag_ref[2], value, share)
            at += share
    half = got.shape[0]
    lines = jnp.concatenate([own[:half] + got[...], own[half:]], axis=0).astype(BF)
    for z in range(chips):
        theirs[z, at:] = lines
        mine[z, at:] = lines


def split_kernel(which, *refs):
    flag_ref, mine, got = refs[:3]
    count = len(which)
    outs, (one, two, extra, sems) = refs[-4 - count : -4], refs[-4:]
    place = flag_ref[3]
    loads = Loads(sems)
    index = (
        jnp.where(place % 2 == 0, 3, 0),
        jnp.where(place == 1, 2, 1),
        jnp.where(place == 0, 2, 1),
        jnp.where(place == 0, 1, 2),
        jnp.where(place == 1, 3, 0),
    )
    for i, pick in enumerate(which):
        loads.start(2 * i, mine.at[index[pick]], one.at[i])
        loads.start(2 * i + 1, got.at[index[pick]], two.at[i])
        if pick == 4:
            loads.start("extra", refs[3], extra)
    for i, pick in enumerate(which):
        loads.wait(2 * i)
        loads.wait(2 * i + 1)
        value = one[i].astype(F32) + two[i].astype(F32)
        if pick == 4:
            loads.wait("extra")
            value = value + extra[...].astype(F32)
        outs[i][...] = value.astype(BF)


def arrived_sum(flag_ref, refs, scratch, sems):
    place = flag_ref[3]
    loads = Loads(sems)
    for i in range(2):
        loads.start(i, refs[i].at[place], scratch.at[i])
    edge = jnp.logical_or(place == 0, place == 3)
    for i in range(2):
        loads.wait(i)

    def total(at, rows):
        sl = slice(at, at + rows)
        value = refs[2][sl, :].astype(F32)
        value = jnp.where(edge, value, jnp.zeros_like(value))
        value = value + (scratch[0, sl, :].astype(F32) + scratch[1, sl, :].astype(F32))
        for ref in refs[3:7]:
            value = value + ref[sl, :].astype(F32)
        return value

    return total


def final_down_kernel(flag_ref, *refs):
    down_ref, out_ref, scratch, sems = refs[-4:]
    total = arrived_sum(flag_ref, refs[:7], scratch, sems)
    rows = down_ref.shape[0]
    down_ref[...] = total(0, rows)
    out_ref[...] = total(rows, out_ref.shape[0])


def final_rest_kernel(flag_ref, *refs):
    up_ref, qkv_ref, vec_ref, bqkv_ref, bup_ref, lines, scratch, sems = refs[-8:]
    total = arrived_sum(flag_ref, refs[:7], scratch, sems)
    share, local = qkv_ref.shape[1:]
    at = 0
    for c in range(0, up_ref.shape[1], local):
        up_ref[:, c : c + local] = total(at, share)
        at += share
    for t in range(3):
        qkv_ref[t] = total(at, share)
        at += share
    lines[...] = total(at, lines.shape[0])
    dp_at = 2 * flag_ref[3] + flag_ref[2]
    width = bqkv_ref.shape[1]
    front = pltpu.roll(lines[0:8], local - dp_at * width, 1)
    vec_ref[...] = front[0:5, :width]
    bqkv_ref[...] = front[5:8, :width]
    width = bup_ref.shape[1]
    per_line = local // width
    line = pltpu.roll(lines[8:16], local - (dp_at % per_line) * width, 1)
    row = dp_at // per_line
    picked = jnp.zeros((1, width), F32)
    for i in range(per_line and 8 // per_line):
        picked = jnp.where(row == i, line[i : i + 1, :width], picked)
    bup_ref[...] = picked


def tail_kernel(micro, *refs):
    part, other, up, grad, other_grad = refs[:5]
    sources = refs[5 : 5 + micro]
    out_ref, grad_ref = refs[-2:]
    rows = sources[0].shape[0]
    for m in range(micro):
        sl = slice(m * rows, (m + 1) * rows)
        both = part[sl].astype(F32) + other[sl].astype(F32)
        out_ref[sl] = (sources[m][...].astype(F32) + both).astype(BF)
    grad_ref[...] = up[...].astype(F32) + (grad[...].astype(F32) + other_grad[...].astype(F32))


def o_kernel(micro, *refs):
    mixed_refs, active_refs = refs[:micro], refs[micro : 2 * micro]
    pack_ref, wout_hbm, wdown_hbm = refs[2 * micro : 2 * micro + 3]
    out_ref, wout, wdown, mixed, active, sems = refs[-6:]
    loads = Loads(sems)
    hbm, w = {"wout": wout_hbm, "wdown": wdown_hbm}, {"wout": wout, "wdown": wdown}
    loads.weight("wout", hbm, w)
    loads.weight("wdown", hbm, w)
    rows = mixed_refs[0].shape[0]
    for m in range(micro):
        mixed[m * rows : (m + 1) * rows] = mixed_refs[m][...]
        active[m * rows : (m + 1) * rows] = active_refs[m][...]
    vec = unpacked(pack_ref, wout.shape[1], wout.shape[0], wdown.shape[0])
    out_ref[...] = output_part(mixed, active, vec, w, loads.wait)


VM = pl.BlockSpec(memory_space=pltpu.VMEM)
SM = pl.BlockSpec(memory_space=pltpu.SMEM)
HB = pl.BlockSpec(memory_space=pltpu.HBM)


def scratch_like(arrays):
    return [pltpu.VMEM(a.shape, a.dtype) for a in arrays]


def cost(ws, rows, passes):
    size = sum(math.prod(a.shape) for a in ws)
    return pl.CostEstimate(flops=2 * size * rows * passes, bytes_accessed=2 * size, transcendentals=0)


def params(mib):
    return pltpu.CompilerParams(vmem_limit_bytes=mib * 2**20)


def call_f(flags, xs, table, ws, vecs):
    micro, rows, width = xs.shape
    local, hidden = ws[1].shape[0], ws[3].shape[0]
    total = micro * rows
    scratch = scratch_like(ws) + [
        pltpu.VMEM((total, local), BF),
        pltpu.VMEM((total, hidden), BF),
        pltpu.VMEM((total, width), BF),
        pltpu.VMEM(table.shape, F32),
        pltpu.SemaphoreType.DMA((24,)),
    ]
    out = [jax.ShapeDtypeStruct((rows, width), BF)] * micro + [jax.ShapeDtypeStruct((16, hidden), F32)]
    return pl.pallas_call(
        functools.partial(f_kernel, micro),
        out_shape=out,
        in_specs=[SM] + [HB] * 14,
        out_specs=[VM] * len(out),
        scratch_shapes=scratch + scratch_like(vecs),
        compiler_params=params(54),
        cost_estimate=cost(ws, total, 1),
    )(flags, xs, table, *ws, *vecs)


def call_fb(at, flags, xs, cots, arrived, table, pack, ws):
    rows, width = xs.shape[1:]
    local, hidden = ws[1].shape[0], ws[3].shape[0]
    shape = jax.ShapeDtypeStruct
    outs = [shape((rows, width), BF)] * 4
    outs += [shape((rows, local), BF)] * 3
    outs += [
        shape((rows, 2 * rows * local // LANES), BF),
        shape((rows, local), BF),
        shape((rows, hidden), BF),
        shape((rows, hidden), BF),
    ]
    return pl.pallas_call(
        functools.partial(fb_kernel, at),
        out_shape=outs,
        in_specs=[SM] + [HB] * 10,
        out_specs=[HB] * len(outs),
        scratch_shapes=scratch_like(outs)
        + scratch_like(ws)
        + [
            pltpu.VMEM((rows, hidden), BF),
            pltpu.VMEM((rows, 3 * local), BF),
            pltpu.VMEM((rows, width), BF),
            pltpu.VMEM((rows, width), BF),
            pltpu.VMEM((rows, width), BF),
            pltpu.VMEM((rows, width), BF),
            pltpu.VMEM(table.shape, F32),
            pltpu.VMEM(pack.shape, F32),
            pltpu.SemaphoreType.DMA((24,)),
            pltpu.SemaphoreType.DMA((len(outs),)),
        ],
        compiler_params=params(54),
        cost_estimate=cost(ws, rows, 2),
    )(flags, xs, cots, *arrived, table, pack, *ws)


def call_b(flags, cots, table, pack, ws, pieces, after):
    micro, rows, width = cots.shape
    local, hidden = ws[1].shape[0], ws[3].shape[0]
    shape = jax.ShapeDtypeStruct
    total = micro * rows
    outs = [
        shape((total, width), BF),
        shape((total, hidden), BF),
        shape((total, 3 * local), BF),
        shape((16, local), F32),
        shape((8, local), F32),
        shape((total, width), BF),
    ]
    flat = [array for group in pieces for array in group]
    return pl.pallas_call(
        functools.partial(b_kernel, micro),
        out_shape=outs,
        in_specs=[SM] + [HB] * (7 + len(flat) + len(after)),
        out_specs=[VM] * len(outs),
        scratch_shapes=scratch_like(ws)
        + [pltpu.VMEM((total, width), BF)]
        + scratch_like([table, pack])
        + [pltpu.VMEM((total, group[0].shape[1]), group[0].dtype) for group in pieces]
        + [pltpu.SemaphoreType.DMA((32,))],
        compiler_params=params(54),
        cost_estimate=cost(ws, total, 1),
    )(flags, cots, table, pack, *ws, *flat, *after)


def call_blocks(kernel, flags, operands, specs, block, flops, scratch=()):
    outs = [jax.ShapeDtypeStruct(block, BF)] * 2
    return pl.pallas_call(
        kernel,
        out_shape=outs,
        in_specs=[SM] + specs,
        out_specs=[VM] * 2,
        scratch_shapes=list(scratch),
        compiler_params=params(24),
        cost_estimate=pl.CostEstimate(flops=flops, bytes_accessed=4 * math.prod(block), transcendentals=0),
    )(flags, *operands)


def call_split(flags, mine, got, which, after):
    block, count = mine.shape[1:], len(which)
    return pl.pallas_call(
        functools.partial(split_kernel, which),
        out_shape=[jax.ShapeDtypeStruct(block, BF)] * count,
        in_specs=[SM] + [HB] * (2 + len(after)),
        out_specs=[VM] * count,
        scratch_shapes=[pltpu.VMEM((count,) + block, BF)] * 2
        + [pltpu.VMEM(block, BF), pltpu.SemaphoreType.DMA((8,))],
        compiler_params=params(16),
    )(flags, mine, got, *after)


def call_final(kernel, flags, parts, outs, after, scratch=()):
    return pl.pallas_call(
        kernel,
        out_shape=[jax.ShapeDtypeStruct(shape, F32) for shape in outs],
        in_specs=[SM, HB, HB] + [VM] * 5 + [HB] * len(after),
        out_specs=[VM] * len(outs),
        scratch_shapes=list(scratch)
        + [pltpu.VMEM((2,) + parts[2].shape, BF), pltpu.SemaphoreType.DMA((2,))],
        compiler_params=params(16),
    )(flags, *parts, *after)


def call_tail(part, other, up, grad, other_grad, sources, after):
    micro = len(sources)
    return pl.pallas_call(
        functools.partial(tail_kernel, micro),
        out_shape=[jax.ShapeDtypeStruct(part.shape, BF), jax.ShapeDtypeStruct(part.shape, F32)],
        in_specs=[VM] * (5 + micro) + [HB] * len(after),
        out_specs=[VM] * 2,
        compiler_params=params(16),
    )(part, other, up, grad, other_grad, *sources, *after)


def call_o(mixed, active, pack, ws, after=()):
    micro, (rows, local) = len(mixed), mixed[0].shape
    hidden, width = ws[3].shape
    total = micro * rows
    return pl.pallas_call(
        functools.partial(o_kernel, micro),
        out_shape=jax.ShapeDtypeStruct((total, width), BF),
        in_specs=[VM] * (2 * micro + 1) + [HB] * (2 + len(after)),
        out_specs=VM,
        scratch_shapes=[
            pltpu.VMEM((local, width), BF),
            pltpu.VMEM((hidden, width), BF),
            pltpu.VMEM((total, local), BF),
            pltpu.VMEM((total, hidden), BF),
            pltpu.SemaphoreType.DMA((8,)),
        ],
        compiler_params=params(24),
        cost_estimate=cost((ws[1], ws[3]), total, 1),
    )(*mixed, *active, pack, ws[1], ws[3], *after)


def handed(value, source, target):
    straight = lax.ppermute(value, "section", [(source, target)])
    across = [(2 * source, 2 * target + 1), (2 * source + 1, 2 * target)]
    return straight, lax.ppermute(value, ("section", "tensor"), across)


def swap(value):
    return lax.ppermute(value, "tensor", [(0, 1), (1, 0)])


ONE = [(0, 1), (1, 0), (2, 3), (3, 2)]
TWO = [(0, 1), (3, 2)]
THREE = [(1, 2), (2, 1)]
FOUR = [(0, 2), (3, 1)]
FIVE = [(1, 3), (2, 0)]


class Line:
    def __init__(self, theirs, mine, at):
        self.place = at // 2
        self.mine = mine
        self.got = lax.ppermute(theirs, "dp", [(i, i ^ 1) for i in range(8)])

    def block(self, index):
        one = lax.dynamic_index_in_dim(self.mine, index, 0, keepdims=False)
        two = lax.dynamic_index_in_dim(self.got, index, 0, keepdims=False)
        return one.astype(F32) + two.astype(F32)

    def send(self, value, pairs):
        return lax.ppermute(value, "dp", [(2 * a + c, 2 * b + c) for a, b in pairs for c in range(2)])

    def start(self):
        place = self.place
        values = [
            self.block(index).astype(BF)
            for index in (
                jnp.where(place % 2 == 0, 3, 0),
                jnp.where(place == 1, 2, 1),
                jnp.where(place == 0, 2, 1),
                jnp.where(place == 0, 1, 2),
            )
        ]
        self.one = self.send(values[0], ONE)
        self.three = self.send(values[1], THREE)
        self.four = self.send(values[2], FOUR)
        self.two = self.send(values[3], TWO)
        return tuple(values)

    def relay(self):
        value = (self.block(jnp.where(self.place == 1, 3, 0)) + self.one.astype(F32)).astype(BF)
        self.five = self.send(value, FIVE)
        return value

    def staged(self, flags):
        first = call_split(flags, self.mine, self.got, (0, 1), ())
        self.one = self.send(first[0], ONE)
        self.three = self.send(first[1], THREE)
        rest = call_split(flags, self.mine, self.got, (4, 2, 3), (self.one, self.three))
        self.five = self.send(rest[0], FIVE)
        self.four = self.send(rest[1], FOUR)
        self.two = self.send(rest[2], TWO)

    def parts(self):
        return self.mine, self.got, self.one, self.two, self.three, self.four, self.five


def wide(pieces, others):
    left, right = jnp.concatenate(pieces, axis=0), jnp.concatenate(others, axis=0)
    return jnp.einsum("ta,tb->ab", left, right, preferred_element_type=F32).astype(BF)


def scattered(blocks):
    parts, rows, columns = blocks.shape
    return lax.psum_scatter(blocks.reshape(parts * rows, columns), "dp", scatter_dimension=0, tiled=True).astype(F32)


def per_device(inputs, cotangent, g1, b1, g2, b2, w_qkv, b_qkv, w_out, b_out, w_up, b_up, w_down, b_down):
    section = lax.axis_index("section")
    owner = lax.axis_index("tensor")
    dp_at = lax.axis_index("dp")
    parts = lax.axis_size("dp")
    micro, seqs, length, width = inputs.shape
    rows = seqs * length
    local, hidden = w_out.shape[1], w_up.shape[2]
    flags = jnp.stack([section, owner, dp_at % 2, dp_at // 2]).astype(jnp.int32)
    table = jnp.asarray(rope_tables(length))
    vecs = (g1, b1, g2, b2, b_qkv[0], b_out, b_up, b_down)
    ws = (w_qkv[0].transpose(1, 0, 2), w_out[0], w_up[0], w_down[0])
    xs = inputs.reshape(micro, rows, width)
    cots = cotangent.reshape(micro, rows, width)
    lined = parts == 8
    chips = parts // 2

    *outs, pack = call_f(flags, xs, table, ws, vecs)
    arrivals = []
    for m in range(micro):
        arrivals.append(handed(outs[m], 0, 1))
    kept, sources, backs = [], [], []
    for m in range(micro):
        dx, source, *saved = call_fb(m, flags, xs, cots, arrivals[m], table, pack, ws)
        backs.append(handed(dx, 1, 0))
        kept.append(dict(zip(SAVED, saved)))
        sources.append(source)
    a1, a2, mixed, active = ([kept[m][n] for m in range(micro)] for n in ("a1", "a2", "mixed", "g"))

    after = ()
    arrived, beside = ([back[i] for back in backs] for i in range(2))
    if lined:
        theirs, mine = call_blocks(
            functools.partial(down_kernel, chips, micro),
            flags,
            (cots, *arrived, *beside, *active, *mixed),
            [HB] + [VM] * (4 * micro),
            (chips, hidden // parts + local // parts, width),
            2 * micro * rows * width * (hidden + local),
            [pltpu.VMEM(cots.shape, BF), pltpu.SemaphoreType.DMA],
        )
        line_down = Line(theirs, mine, dp_at)
        after = line_down.start()
    pieces = [arrived, beside, sources] + [[kept[m][n] for m in range(micro)] for n in NEEDED]
    grad, du, dqkv, own, other, up = call_b(flags, cots, table, pack, ws, pieces, after)
    got = swap(other)
    share = width // parts
    if lined:
        after = (line_down.relay(), line_down.two, line_down.three, line_down.four)
        slabs = hidden // local
        lines = own.shape[0]
        theirs, mine = call_blocks(
            functools.partial(rest_kernel, chips, micro),
            flags,
            (du, dqkv, own, got, *a1, *a2, *after),
            [VM] * (4 + 2 * micro) + [HB] * len(after),
            (chips, (slabs + 3) * share + lines, local),
            2 * micro * rows * width * (hidden + 3 * local),
        )
        line_rest = Line(theirs, mine, dp_at)
        part = call_o(mixed, active, pack, ws, (mine,))
        line_rest.staged(flags)
        after = (line_rest.one,)
        down_rows = hidden // parts
        outs = [(down_rows, width), (local // parts, width)]
        d_wdown, d_wout = call_final(final_down_kernel, flags, line_down.parts(), outs, after)
        section_out, input_grad = call_tail(part, swap(part), up, grad, swap(grad), sources, after)
        outs = [(share, hidden), (3, share, local), (5, local // parts), (3, local // parts), (1, down_rows)]
        d_wup, d_wqkv, d_vec, d_bqkv, d_bup = call_final(
            final_rest_kernel, flags, line_rest.parts(), outs, (), [pltpu.VMEM((lines, local), F32)]
        )
        d_wqkv = d_wqkv.transpose(1, 0, 2)
    else:
        d_wdown = wide(active, [up]).reshape(parts, -1, width)
        d_wout = wide(mixed, [up]).reshape(parts, -1, width)
        d_both = scattered(jnp.concatenate([d_wdown, d_wout], axis=1))
        d_wup = scattered(wide(a2, [du]).reshape(parts, -1, hidden))
        d_wqkv = wide(a1, [dqkv]).reshape(parts, share, 3, local).transpose(0, 2, 1, 3)
        lines = jnp.concatenate([own[: got.shape[0]] + got, own[got.shape[0] :]]).astype(BF)
        lines = jnp.broadcast_to(lines[None], (parts,) + lines.shape)
        last = scattered(jnp.concatenate([d_wqkv.reshape(parts, 3 * share, local), lines], axis=1))
        down_rows = hidden // parts
        d_wdown, d_wout = d_both[:down_rows], d_both[down_rows:]
        d_wqkv = last[: 3 * share].reshape(3, share, local).transpose(1, 0, 2)
        lines = last[3 * share :]
        d_vec = lax.dynamic_slice(lines, (0, dp_at * (local // parts)), (8, local // parts))
        d_vec, d_bqkv = d_vec[:5], d_vec[5:]
        up_lines = lines[8 : 8 + hidden // local].reshape(1, hidden)
        d_bup = lax.dynamic_slice_in_dim(up_lines, dp_at * down_rows, down_rows, 1)
        part = call_o(mixed, active, pack, ws)
        section_out, input_grad = call_tail(part, swap(part), up, grad, swap(grad), sources, ())
    return (
        section_out.reshape(1, micro, seqs, length, width),
        input_grad.reshape(1, micro, seqs, length, width),
        d_vec[0:1],
        d_vec[1:2],
        d_vec[2:3],
        d_vec[3:4],
        d_wqkv[None],
        d_bqkv[None],
        d_wout[None],
        d_vec[4:5],
        d_wup[None],
        d_bup,
        d_wdown[None],
        d_vec[4:5],
    )


def solution(mesh):
    return jax.shard_map(
        per_device,
        mesh=mesh,
        in_specs=(
            P(None, "dp", None, None),
            P(None, "dp", None, None),
            P("section", None),
            P("section", None),
            P("section", None),
            P("section", None),
            P("section", None, None, "tensor"),
            P("section", None, "tensor"),
            P("section", "tensor", None),
            P("section", None),
            P("section", None, "tensor"),
            P("section", "tensor"),
            P("section", "tensor", None),
            P("section", None),
        ),
        out_specs=(
            P("section", None, "dp", None, None),
            P("section", None, "dp", None, None),
            P("section", ("tensor", "dp")),
            P("section", ("tensor", "dp")),
            P("section", ("tensor", "dp")),
            P("section", ("tensor", "dp")),
            P("section", "dp", None, "tensor"),
            P("section", None, ("tensor", "dp")),
            P("section", ("tensor", "dp"), None),
            P("section", ("tensor", "dp")),
            P("section", "dp", "tensor"),
            P("section", ("tensor", "dp")),
            P("section", ("tensor", "dp"), None),
            P("section", ("tensor", "dp")),
        ),
        check_vma=False,
    )
```
